32 devices in a mesh: dp: 4 (over x, core), head: 8 (over z, y).
Axes of the slice: x: 2, y: 2, z: 4, core: 2. Of those that a mesh axis runs over, the one named last changes fastest.
Arguments:
- block_input: bfloat16 [4, 4096, 1024], P('dp', 'head'), may hold values from -6 to 6
- lengths: int32 [4, 3], P('dp'), may hold values from 680 to 2240, as said below
- scale_ids: int32 [4, 4096], P('dp'), may hold values from 0 to 9, as said below
- class_ids: int32 [4], P('dp'), may hold values from 0 to 1000
- code_ids: int32 [4, 4096], P('dp', 'head'), may hold values from 0 to 4095
- cotangent: bfloat16 [4, 4096, 1024], P('dp', 'head'), may hold values from -6 to 6
- class_table: bfloat16 [1001, 1024], replicated, may hold values from -6 to 6
- ada_weight: bfloat16 [1024, 6144], P(None, 'head'), may hold values from -0.1875 to 0.1875
- ada_bias: bfloat16 [6144], P('head'), may hold values from -3 to 3
- qkv_weight: bfloat16 [1024, 3072], P(None, 'head'), may hold values from -0.1875 to 0.1875
- qv_bias: bfloat16 [2048], P('head'), may hold values from -3 to 3
- qk_scale: float32 [16], P('head'), may hold values from 2 to 3.2
- proj_weight: bfloat16 [1024, 1024], P('head'), may hold values from -1 to 1
- proj_bias: bfloat16 [1024], replicated, may hold values from -4 to 4
- fc1_weight: bfloat16 [1024, 4096], P(None, 'head'), may hold values from -0.1875 to 0.1875
- fc1_bias: bfloat16 [4096], P('head'), may hold values from -3 to 3
- fc2_weight: bfloat16 [4096, 1024], P('head'), may hold values from -0.375 to 0.375
- fc2_bias: bfloat16 [1024], replicated, may hold values from -4 to 4
Outputs:
- block_output: bfloat16 [4, 4096, 1024], P('dp', 'head')
- input_grad: bfloat16 [4, 4096, 1024], P('dp', 'head')
- class_table_grad: float32 [1001, 1024], replicated
- ada_weight_grad: float32 [1024, 6144], P(None, 'head')
- ada_bias_grad: float32 [6144], P('head')
- qkv_weight_grad: float32 [1024, 3072], P(None, 'head')
- qv_bias_grad: float32 [2048], P('head')
- qk_scale_grad: float32 [16], P('head')
- proj_weight_grad: float32 [1024, 1024], P('head')
- proj_bias_grad: float32 [1024], replicated
- fc1_weight_grad: float32 [1024, 4096], P(None, 'head')
- fc1_bias_grad: float32 [4096], P('head')
- fc2_weight_grad: float32 [4096, 1024], P('head')
- fc2_bias_grad: float32 [1024], replicated
- code_hist: int32 [4096], replicated
The draws below stay inside these ranges and needn't reach their ends.
Inputs may be any that keep to these rules, and one draw needn't show every extreme that they name: `lengths`: each row holds one item of 2240 tokens and two of 680, in an order that varies from row to row; the slots after them are padding. `scale_ids`: within an item, the slot at offset o has scale k where k counts the entries of c that are at most o, with c = 1, 5, 14, 30, 66, 147, 316, 640, 1216, 2240 for an item of 2240 tokens and c = 1, 5, 14, 30, 55, 91, 155, 255, 424, 680 for one of 680; padding slots have scale 0.
All inputs are finite; a program needn't handle non-finite values.
Results may differ from the reference program's by a relative error of at most 0.03.
Values may be sent and summed in bfloat16 or wider, within the bound.
No kernel may reach another device: no remote copies, remote signals or barrier semaphores. Data moves between devices by JAX's collectives and lax.ppermute only.
A program may use at most 256 MiB of HBM per device.

```python
import jax
import jax.numpy as jnp
from jax import lax

D = 1024
HEADS = 16
HD = 64
FF = 4096
CLASSES = 1001
CODES = 4096
SLOTS = 4096
BIG_LEN = 2240
SMALL_LEN = 680
QBLOCK = 512
ROWS = 4


BIG_CUMS = (1, 5, 14, 30, 66, 147, 316, 640, 1216, 2240)


SMALL_CUMS = (1, 5, 14, 30, 55, 91, 155, 255, 424, 680)


def layout_place(key):
    return jax.random.randint(jax.random.fold_in(key, 17), (ROWS,), 0, 3)


def draw_lengths(key, part):
    place = layout_place(key)
    column = jnp.arange(3, dtype=jnp.int32)[None, :]
    return jnp.where(column == place[:, None], BIG_LEN, SMALL_LEN).astype(jnp.int32)


def draw_scale_ids(key, part):
    lengths = draw_lengths(key, part)
    ends = jnp.cumsum(lengths, 1)
    starts = ends - lengths
    places = jnp.arange(SLOTS, dtype=jnp.int32)[None, :]
    big_table = jnp.array(BIG_CUMS, dtype=jnp.int32)
    small_table = jnp.array(SMALL_CUMS, dtype=jnp.int32)
    levels_all = jnp.zeros((ROWS, SLOTS), jnp.int32)
    for column in range(3):
        begin = starts[:, column:column + 1]
        finish = ends[:, column:column + 1]
        inside = (places >= begin) & (places < finish)
        offset = places - begin
        table = jnp.where(lengths[:, column:column + 1, None] == BIG_LEN, big_table[None, None, :], small_table[None, None, :])
        level = jnp.sum((offset[:, :, None] >= table).astype(jnp.int32), -1)
        levels_all = jnp.where(inside, level, levels_all)
    return levels_all


def draw_code_ids(key, part):
    places = jnp.arange(SLOTS, dtype=jnp.int32)[None, :]
    base = places * CODES // SLOTS
    offset = jax.random.randint(jax.random.fold_in(key, 29), (ROWS, SLOTS), 0, CODES // 4).astype(jnp.int32)
    return ((base + offset) % CODES).astype(jnp.int32)


def with_ends(values, rng, smallest, largest):
    spot = [jax.random.randint(jax.random.fold_in(rng, axis), (), 0, length) for axis, length in enumerate(values.shape)]
    main_axis = values.shape.index(max(values.shape))
    beside = spot[:main_axis] + [(spot[main_axis] + 1) % values.shape[main_axis]] + spot[main_axis + 1:]
    return values.at[tuple(spot)].set(smallest).at[tuple(beside)].set(largest)


def shard_levels(stream_key, dims, cuts, least, top_value):
    loudness, own = 1.0, jax.random.fold_in(stream_key, 6)
    for axis_at, parts in cuts:
        steps = jnp.exp(jax.random.uniform(jax.random.fold_in(own, axis_at), (parts,), jnp.float32, least / len(cuts), top_value / len(cuts)))
        loudness = loudness * jnp.repeat(steps, dims[axis_at] // parts).reshape([-1 if axis == axis_at else 1 for axis in range(len(dims))])
    return loudness


def centred(key, shape, scale, limit, cuts=(), held_as=jnp.bfloat16):
    entries = scale * jax.random.normal(key, shape, jnp.float32)
    if cuts:
        entries = entries * shard_levels(key, shape, cuts, -0.22, 0.18)
    return jnp.clip(entries, -limit, limit).astype(held_as)


def setup_inputs(seed: int = 0) -> dict:
    key_list = jax.random.split(jax.random.key(seed), 19)
    block_input = centred(key_list[0], (ROWS, SLOTS, D), 1.0, 6.0, ((0, 4), (1, 8)))
    lengths = draw_lengths(jax.random.fold_in(key_list[18], 71), 0)
    scale_ids = draw_scale_ids(jax.random.fold_in(key_list[18], 71), 0)
    class_ids = with_ends(jax.random.randint(key_list[3], (ROWS,), 0, CLASSES), jax.random.fold_in(key_list[3], 1), 0, CLASSES - 1).astype(jnp.int32)
    code_ids = draw_code_ids(jax.random.fold_in(key_list[18], 71), 0)
    cotangent = centred(key_list[5], (ROWS, SLOTS, D), 1.0, 6.0, ((0, 4), (1, 8)))
    class_table = centred(key_list[6], (CLASSES, D), 1.0, 6.0)
    ada_weight = centred(key_list[7], (D, 6 * D), D ** -0.5, 0.1875, ((1, 8),))
    ada_bias = centred(key_list[8], (6 * D,), 0.5, 3.0, ((0, 8),))
    qkv_weight = centred(key_list[9], (D, 3 * D), D ** -0.5, 0.1875, ((1, 8),))
    qv_bias = centred(key_list[10], (2 * D,), 0.5, 3.0, ((0, 8),))
    qk_scale = jnp.clip(2.0 + 1.2 * jax.random.uniform(key_list[11], (HEADS,), jnp.float32) ** shard_levels(key_list[11], (HEADS,), ((0, 8),), -0.2, 0.2), 2.0, 3.2)
    proj_weight = centred(key_list[12], (D, D), (D // 32) ** -0.5, 1.0, ((0, 8),))
    proj_bias = centred(key_list[13], (D,), 1.0, 4.0)
    fc1_weight = centred(key_list[14], (D, FF), D ** -0.5, 0.1875, ((1, 8),))
    fc1_bias = centred(key_list[15], (FF,), 0.5, 3.0, ((0, 8),))
    fc2_weight = centred(key_list[16], (FF, D), (FF // 16) ** -0.5, 0.375, ((0, 8),))
    fc2_bias = centred(key_list[17], (D,), 1.0, 4.0)
    return {"block_input": block_input, "lengths": lengths, "scale_ids": scale_ids, "class_ids": class_ids, "code_ids": code_ids, "cotangent": cotangent, "class_table": class_table, "ada_weight": ada_weight, "ada_bias": ada_bias, "qkv_weight": qkv_weight, "qv_bias": qv_bias, "qk_scale": qk_scale, "proj_weight": proj_weight, "proj_bias": proj_bias, "fc1_weight": fc1_weight, "fc1_bias": fc1_bias, "fc2_weight": fc2_weight, "fc2_bias": fc2_bias}


@jax.custom_vjp
def low(v):
    return lax.optimization_barrier(v.astype(jnp.bfloat16)).astype(jnp.float32)

@jax.custom_vjp
def low_back(v):
    return v

def low_keep(v):
    return (low(v), None)

def low_pass(kept, grad):
    return (grad,)

def back_keep(v):
    return (v, None)

def back_low(kept, grad):
    return (low(grad),)
low.defvjp(low_keep, low_pass)
low_back.defvjp(back_keep, back_low)
EPS_NORM = 1e-06
HIGH = lax.Precision.HIGHEST

def mix_norm(values, shift, scale):
    mean_val = lax.optimization_barrier(jnp.mean(values, -1, keepdims=True))
    centered = values - mean_val
    variance = lax.optimization_barrier(jnp.mean(centered * centered, -1, keepdims=True))
    return centered * lax.rsqrt(variance + EPS_NORM) * (1.0 + scale) + shift

def row_grouped(left, weight):
    return jnp.dot(left, weight, precision=HIGH)

def col_grouped(left, weight):
    return jnp.dot(left, weight, precision=HIGH)

def item_index(lengths_row):
    first = lengths_row[0]
    second = first + lengths_row[1]
    third = second + lengths_row[2]
    places = jnp.arange(SLOTS, dtype=jnp.int32)
    return (places >= first).astype(jnp.int32) + (places >= second).astype(jnp.int32) + (places >= third).astype(jnp.int32)

def attend(query_low, key_low, value_low, items, scales):
    blocks = SLOTS // QBLOCK
    query_blocks = query_low.reshape(blocks, QBLOCK, HEADS, HD)
    item_blocks = items.reshape(blocks, QBLOCK)
    scale_blocks = scales.reshape(blocks, QBLOCK)

    @jax.checkpoint
    def one_block(pieces):
        query_part, item_part, scale_part = pieces
        scores = low_back(jnp.einsum('qhd,khd->hqk', query_part, key_low, precision=HIGH))
        allowed = (item_part[:, None] == items[None, :]) & (scales[None, :] <= scale_part[:, None])
        scores = jnp.where(allowed[None], scores, jnp.full_like(scores, -1e+30))
        top_score = lax.optimization_barrier(jnp.max(scores, -1, keepdims=True))
        exp_scores = jnp.exp(scores - top_score)
        probs = low(exp_scores / lax.optimization_barrier(jnp.sum(exp_scores, -1, keepdims=True)))
        return jnp.einsum('hqk,khd->qhd', probs, value_low, precision=HIGH)
    result = lax.map(one_block, (query_blocks, item_blocks, scale_blocks))
    return result.reshape(SLOTS, HEADS, HD)

def row_forward(row_input, params, class_id, items, scales):
    table, ada_w, ada_b, qkv_w, qv_b, scale_log, proj_w, proj_b, up_w, up_b, down_w, down_b = params
    cond = lax.dynamic_index_in_dim(table, class_id, 0, keepdims=False)
    act = low(jax.nn.silu(cond))
    modulation = jnp.dot(act, ada_w, precision=HIGH) + ada_b
    shift_one, scale_one, gate_one, shift_two, scale_two, gate_two = jnp.split(modulation, 6)
    normed_one = low(mix_norm(row_input, shift_one, scale_one))
    bias_pair = qv_b.reshape(HEADS, 2, HD)
    bias_full = jnp.stack([bias_pair[:, 0], jnp.zeros_like(bias_pair[:, 0]), bias_pair[:, 1]], 1).reshape(3 * D)
    projected = low_back(col_grouped(normed_one, qkv_w) + bias_full).reshape(SLOTS, HEADS, 3, HD)
    queries = projected[:, :, 0]
    key_raw = projected[:, :, 1]
    value_raw = projected[:, :, 2]
    query_unit = queries * lax.rsqrt(lax.optimization_barrier(jnp.sum(queries * queries, -1, keepdims=True)) + EPS_NORM)
    key_unit_vector = key_raw * lax.rsqrt(lax.optimization_barrier(jnp.sum(key_raw * key_raw, -1, keepdims=True)) + EPS_NORM)
    query_low = low(query_unit * jnp.exp(scale_log)[None, :, None])
    key_low = low(key_unit_vector)
    value_low = low(value_raw)
    attended = low_back(low(attend(query_low, key_low, value_low, items, scales))).reshape(SLOTS, D)
    attn_branch = low_back(row_grouped(attended, proj_w) + proj_b)
    resid = row_input + gate_one * attn_branch
    normed_two = low(mix_norm(resid, shift_two, scale_two))
    pre_act = low_back(col_grouped(normed_two, up_w) + up_b)
    hidden = low(jax.nn.gelu(pre_act, approximate=True))
    mlp_branch = low_back(row_grouped(hidden, down_w) + down_b)
    return resid + gate_two * mlp_branch

def reference(block_input, lengths, scale_ids, class_ids, code_ids, cotangent, class_table, ada_weight, ada_bias, qkv_weight, qv_bias, qk_scale, proj_weight, proj_bias, fc1_weight, fc1_bias, fc2_weight, fc2_bias):
    params = tuple((weight.astype(jnp.float32) for weight in (class_table, ada_weight, ada_bias, qkv_weight, qv_bias, qk_scale, proj_weight, proj_bias, fc1_weight, fc1_bias, fc2_weight, fc2_bias)))

    def one_row(totals, row):
        row_input, row_lengths, row_scales, class_id, row_cot = row
        items = item_index(row_lengths)

        def forward(inputs_full, weights):
            return row_forward(inputs_full, weights, class_id, items, row_scales)
        row_out, pull = jax.vjp(forward, row_input.astype(jnp.float32), params)
        row_grad, weight_grads = pull(row_cot.astype(jnp.float32))
        totals = jax.tree.map(lambda left, right: left + right, totals, weight_grads)
        return (totals, (row_out.astype(jnp.bfloat16), row_grad.astype(jnp.bfloat16)))
    zero_grads = jax.tree.map(jnp.zeros_like, params)
    grads, (block_output, input_grad) = lax.scan(one_row, zero_grads, (block_input, lengths, scale_ids, class_ids, cotangent))

    def count_row(row):
        row_codes, row_lengths = row
        valid = jnp.arange(SLOTS, dtype=jnp.int32) < jnp.sum(row_lengths).astype(jnp.int32)
        hits = (row_codes[:, None] == jnp.arange(CODES, dtype=jnp.int32)[None, :]) & valid[:, None]
        return lax.optimization_barrier(jnp.sum(hits.astype(jnp.int32), 0)).astype(jnp.int32)
    code_hist = lax.optimization_barrier(jnp.sum(lax.map(count_row, (code_ids, lengths)), 0)).astype(jnp.int32)
    return (block_output, input_grad, grads[0], grads[1], grads[2], grads[3], grads[4], grads[5], grads[6], grads[7], grads[8], grads[9], grads[10], grads[11], code_hist)
```

```python
import functools

import jax
import jax.numpy as jnp
import numpy as np
from jax import lax
from jax.experimental import pallas as pl
from jax.experimental.pallas import tpu as pltpu
from jax.sharding import PartitionSpec as P

HD = 64
CODES = 4096
BLK = 256
EPS_NORM = 1e-06
HIGH = lax.Precision.HIGHEST
F32 = jnp.float32
BF16 = jnp.bfloat16
BIG_LEN = 2240
BIG_CUMS = (1, 5, 14, 30, 66, 147, 316, 640, 1216, 2240)
SMALL_CUMS = (1, 5, 14, 30, 55, 91, 155, 255, 424, 680)
ORDER = (0, 2, 1, 3)


def normalize(values):
    mean_val = jnp.mean(values, -1, keepdims=True)
    centered = values - mean_val
    variance = jnp.mean(centered * centered, -1, keepdims=True)
    recip = lax.rsqrt(variance + EPS_NORM)
    return (centered * recip, recip)


def norm_back(unit, recip, upstream):
    mean_up = jnp.mean(upstream, -1, keepdims=True)
    mean_cross = jnp.mean(upstream * unit, -1, keepdims=True)
    return recip * (upstream - mean_up - unit * mean_cross)


def gelu_tanh(values):
    return jax.nn.gelu(values, approximate=True)


def dot(left, right, left_dim, right_dim):
    return lax.dot_general(
        left, right, (((left_dim,), (right_dim,)), ((), ())), preferred_element_type=F32
    )


def head_pad(part, head, heads):
    pieces = [part if other == head else jnp.zeros_like(part) for other in range(heads)]
    return pieces[0] if heads == 1 else jnp.concatenate(pieces, 0)


def unit_rows(raw):
    recip = lax.rsqrt(jnp.sum(raw * raw, 0, keepdims=True) + EPS_NORM)
    return raw * recip, recip


def key_loops(span_ref, step, body, carry):
    first, full_first = span_ref[4 * step], span_ref[4 * step + 1]
    full_last, last = span_ref[4 * step + 2], span_ref[4 * step + 3]
    carry = lax.fori_loop(first, full_first, functools.partial(body, True), carry)
    carry = lax.fori_loop(full_first, full_last, functools.partial(body, False), carry)
    return lax.fori_loop(full_last, last, functools.partial(body, True), carry)


def allowed_block(block, low_row, high_row):
    places = block * BLK + lax.broadcasted_iota(jnp.int32, (BLK, BLK), 0)
    return (places >= low_row) & (places < high_row)


def forward_kernel(
    heads, span_ref, scale_ref, low_ref, high_ref, raw_ref, out_ref, outlow_ref, lse_ref, key_s, value_s
):
    step = pl.program_id(0)
    width = heads * HD
    slots = raw_ref.shape[1]

    @pl.when(step == 0)
    def _():
        def prepare(block, carry):
            cols = pl.ds(pl.multiple_of(block * BLK, BLK), BLK)
            parts = []
            for head in range(heads):
                unit, _ = unit_rows(raw_ref[width + head * HD : width + (head + 1) * HD, cols])
                parts.append(unit)
            keys = parts[0] if heads == 1 else jnp.concatenate(parts, 0)
            key_s[cols, :] = jnp.transpose(keys).astype(BF16)
            value_s[:, cols] = raw_ref[2 * width :, cols].astype(BF16)
            return carry

        lax.fori_loop(0, slots // BLK, prepare, 0)

    cols = pl.ds(pl.multiple_of(step * BLK, BLK), BLK)
    queries = []
    for head in range(heads):
        unit, _ = unit_rows(raw_ref[head * HD : (head + 1) * HD, cols])
        queries.append(head_pad((unit * scale_ref[head]).astype(BF16), head, heads))
    low_row, high_row = low_ref[...], high_ref[...]

    def body(masked, block, carry):
        rows = pl.ds(pl.multiple_of(block * BLK, BLK), BLK)
        keys = key_s[rows, :]
        if masked:
            allowed = allowed_block(block, low_row, high_row)
        result = []
        for head in range(heads):
            total, acc = carry[head]
            probs = jnp.exp(dot(keys, queries[head], 1, 0))
            if masked:
                probs = jnp.where(allowed, probs, 0.0)
            total = total + jnp.sum(probs.reshape(BLK // 8, 8, BLK), 0)
            acc = acc + dot(value_s[head * HD : (head + 1) * HD, rows], probs.astype(BF16), 1, 0)
            result.append((total, acc))
        return tuple(result)

    start = tuple((jnp.zeros((8, BLK), F32), jnp.zeros((HD, BLK), F32)) for _ in range(heads))
    final = key_loops(span_ref, step, body, start)
    for head in range(heads):
        total, acc = final[head]
        denom = jnp.sum(total, 0, keepdims=True)
        result = acc / denom
        out_ref[head * HD : (head + 1) * HD, :] = result
        outlow_ref[head * HD : (head + 1) * HD, :] = result.astype(BF16)
        lse_ref[head : head + 1, :] = jnp.log(denom)


def backward_kernel(
    heads,
    span_ref,
    scale_ref,
    low_ref,
    high_ref,
    raw_ref,
    out_ref,
    lse_ref,
    up_ref,
    grad_ref,
    qsum_ref,
    key_s,
    keyt_s,
    value_s,
    gkey_s,
    gvalue_s,
):
    step = pl.program_id(0)
    width = heads * HD
    slots = raw_ref.shape[1]

    @pl.when(step == 0)
    def _():
        def prepare(block, carry):
            cols = pl.ds(pl.multiple_of(block * BLK, BLK), BLK)
            parts = []
            for head in range(heads):
                unit, _ = unit_rows(raw_ref[width + head * HD : width + (head + 1) * HD, cols])
                parts.append(unit)
            keys = parts[0] if heads == 1 else jnp.concatenate(parts, 0)
            keyt_s[:, cols] = keys.astype(BF16)
            key_s[cols, :] = jnp.transpose(keys).astype(BF16)
            value_s[cols, :] = jnp.transpose(raw_ref[2 * width :, cols]).astype(BF16)
            gkey_s[cols, :] = jnp.zeros((BLK, width), F32)
            gvalue_s[cols, :] = jnp.zeros((BLK, width), F32)
            return carry

        lax.fori_loop(0, slots // BLK, prepare, 0)

    cols = pl.ds(pl.multiple_of(step * BLK, BLK), BLK)
    units, recips, queries, query_rows, ups, up_rows, deltas, lses = [], [], [], [], [], [], [], []
    for head in range(heads):
        part = slice(head * HD, (head + 1) * HD)
        unit, recip = unit_rows(raw_ref[part, cols])
        units.append(unit)
        recips.append(recip)
        padded = head_pad(unit * scale_ref[head], head, heads)
        queries.append(padded.astype(BF16))
        query_rows.append(jnp.transpose(padded).astype(BF16))
        up = up_ref[part, :].astype(F32)
        padded = head_pad(up, head, heads)
        ups.append(padded.astype(BF16))
        up_rows.append(jnp.transpose(padded).astype(BF16))
        deltas.append(jnp.sum(up * out_ref[part, :], 0, keepdims=True))
        lses.append(lse_ref[head : head + 1, :])
    low_row, high_row = low_ref[...], high_ref[...]

    def body(masked, block, carry):
        rows = pl.ds(pl.multiple_of(block * BLK, BLK), BLK)
        keys, values = key_s[rows, :], value_s[rows, :]
        if masked:
            allowed = allowed_block(block, low_row, high_row)
        result = []
        gkey, gvalue = gkey_s[rows, :], gvalue_s[rows, :]
        for head in range(heads):
            probs = jnp.exp(dot(keys, queries[head], 1, 0) - lses[head])
            if masked:
                probs = jnp.where(allowed, probs, 0.0)
            grad_probs = dot(values, ups[head], 1, 0)
            grad_scores = (probs * (grad_probs - deltas[head])).astype(BF16)
            gvalue = gvalue + dot(probs.astype(BF16), up_rows[head], 1, 0)
            gkey = gkey + dot(grad_scores, query_rows[head], 1, 0)
            result.append(
                carry[head] + dot(keyt_s[head * HD : (head + 1) * HD, rows], grad_scores, 1, 0)
            )
        gkey_s[rows, :] = gkey
        gvalue_s[rows, :] = gvalue
        return tuple(result)

    start = tuple(jnp.zeros((HD, BLK), F32) for _ in range(heads))
    final = key_loops(span_ref, step, body, start)
    for head in range(heads):
        grad, unit = final[head], units[head]
        cross = grad * unit
        qsum_ref[head : head + 1, :] = jnp.sum(cross, 0, keepdims=True)
        scaled = scale_ref[head] * grad
        back = recips[head] * (scaled - unit * jnp.sum(scaled * unit, 0, keepdims=True))
        grad_ref[head * HD : (head + 1) * HD, cols] = back.astype(BF16)

    @pl.when(step == pl.num_programs(0) - 1)
    def _():
        def finish(block, carry):
            cols = pl.ds(pl.multiple_of(block * BLK, BLK), BLK)
            gkey = jnp.transpose(gkey_s[cols, :])
            for head in range(heads):
                unit, recip = unit_rows(raw_ref[width + head * HD : width + (head + 1) * HD, cols])
                grad = gkey[head * HD : (head + 1) * HD, :]
                back = recip * (grad - unit * jnp.sum(grad * unit, 0, keepdims=True))
                grad_ref[width + head * HD : width + (head + 1) * HD, cols] = back.astype(BF16)
            grad_ref[2 * width :, cols] = jnp.transpose(gvalue_s[cols, :]).astype(BF16)
            return carry

        lax.fori_loop(0, slots // BLK, finish, 0)


def whole_spec(shape):
    return pl.BlockSpec(shape, lambda step, *_: (0,) * len(shape))


def column_spec(rows):
    return pl.BlockSpec((rows, BLK), lambda step, *_: (0, step))


def attention_forward(raw, spans, scales, low, high, heads):
    width, slots = heads * HD, raw.shape[1]
    return pl.pallas_call(
        functools.partial(forward_kernel, heads),
        grid_spec=pltpu.PrefetchScalarGridSpec(
            num_scalar_prefetch=2,
            grid=(slots // BLK,),
            in_specs=[column_spec(1), column_spec(1), whole_spec(raw.shape)],
            out_specs=[column_spec(width), column_spec(width), column_spec(heads)],
            scratch_shapes=[pltpu.VMEM((slots, width), BF16), pltpu.VMEM((width, slots), BF16)],
        ),
        out_shape=[
            jax.ShapeDtypeStruct((width, slots), F32),
            jax.ShapeDtypeStruct((width, slots), BF16),
            jax.ShapeDtypeStruct((heads, slots), F32),
        ],
        compiler_params=pltpu.CompilerParams(
            dimension_semantics=("arbitrary",), vmem_limit_bytes=48 * 2**20
        ),
        cost_estimate=pl.CostEstimate(
            flops=heads * slots * slots * 64, bytes_accessed=12 * 2**20, transcendentals=heads * slots * slots // 3
        ),
        name="attend",
    )(spans, scales, low, high, raw)


def attention_backward(raw, out, lse, up, spans, scales, low, high, heads):
    width, slots = heads * HD, raw.shape[1]
    return pl.pallas_call(
        functools.partial(backward_kernel, heads),
        grid_spec=pltpu.PrefetchScalarGridSpec(
            num_scalar_prefetch=2,
            grid=(slots // BLK,),
            in_specs=[
                column_spec(1),
                column_spec(1),
                whole_spec(raw.shape),
                column_spec(width),
                column_spec(heads),
                column_spec(width),
            ],
            out_specs=[whole_spec(raw.shape), column_spec(heads)],
            scratch_shapes=[
                pltpu.VMEM((slots, width), BF16),
                pltpu.VMEM((width, slots), BF16),
                pltpu.VMEM((slots, width), BF16),
                pltpu.VMEM((slots, width), F32),
                pltpu.VMEM((slots, width), F32),
            ],
        ),
        out_shape=[
            jax.ShapeDtypeStruct(raw.shape, BF16),
            jax.ShapeDtypeStruct((heads, slots), F32),
        ],
        compiler_params=pltpu.CompilerParams(
            dimension_semantics=("arbitrary",), vmem_limit_bytes=56 * 2**20
        ),
        cost_estimate=pl.CostEstimate(
            flops=heads * slots * slots * 160, bytes_accessed=16 * 2**20, transcendentals=heads * slots * slots // 3
        ),
        name="attend_back",
    )(spans, scales, low, high, raw, out, lse, up)


def intervals(lengths_row, slots):
    places = jnp.arange(slots, dtype=jnp.int32)
    ends = jnp.cumsum(lengths_row)
    low = jnp.zeros((slots,), jnp.int32)
    high = jnp.zeros((slots,), jnp.int32)
    for item in range(3):
        begin, finish = ends[item] - lengths_row[item], ends[item]
        table = jnp.where(
            lengths_row[item] == BIG_LEN, jnp.array(BIG_CUMS, jnp.int32), jnp.array(SMALL_CUMS, jnp.int32)
        )
        inside = (places >= begin) & (places < finish)
        reach = jnp.full((slots,), table[0], jnp.int32)
        for level in range(1, len(BIG_CUMS)):
            reach = jnp.where(places - begin >= table[level - 1], table[level], reach)
        low = jnp.where(inside, begin, low)
        high = jnp.where(inside, begin + reach, high)
    padding = places >= ends[2]
    low = jnp.where(padding, ends[2], low)
    high = jnp.where(padding, slots, high)
    blocks_low, blocks_high = low.reshape(-1, BLK), high.reshape(-1, BLK)
    first = blocks_low[:, 0] // BLK
    last = (blocks_high[:, -1] + BLK - 1) // BLK
    full_first = jnp.minimum((blocks_low[:, -1] + BLK - 1) // BLK, last)
    full_last = jnp.maximum(blocks_high[:, 0] // BLK, full_first)
    spans = jnp.stack([first, full_first, full_last, last], 1).reshape(-1)
    return low[None, :], high[None, :], spans


def shards(
    block_input,
    lengths,
    scale_ids,
    class_ids,
    code_ids,
    cotangent,
    class_table,
    ada_weight,
    ada_bias,
    qkv_weight,
    qv_bias,
    qk_scale,
    proj_weight,
    proj_bias,
    fc1_weight,
    fc1_bias,
    fc2_weight,
    fc2_bias,
):
    count, data_count = lax.axis_size("head"), lax.axis_size("dp")
    me, data_me = lax.axis_index("head"), lax.axis_index("dp")
    _, local, width = block_input.shape
    slots = local * count
    heads = qk_scale.shape[0]
    feats = heads * HD
    hidden_here = fc1_weight.shape[1]
    quarter = jnp.bitwise_and(data_me, 3)
    order = jnp.array(ORDER, jnp.int32)
    rel_quarters = jnp.bitwise_xor(quarter, order)
    abs_to_rel = jnp.take(order, jnp.bitwise_xor(quarter, jnp.arange(4, dtype=jnp.int32)))

    ring = list(range(0, count, 2)) + list(range(count - 1, 0, -2))
    half_count = count // 2
    offsets = [0]
    for away in range(1, half_count):
        offsets += [away, -away]
    offsets.append(half_count)
    my_pos = jnp.where(me % 2 == 0, me // 2, count - 1 - me // 2)

    def at(away):
        pos = (my_pos + away + count) % count
        return jnp.where(pos < half_count, 2 * pos, 2 * (count - 1 - pos) + 1)

    def rot(value, away):
        pairs = [(ring[(i + away) % count], ring[i]) for i in range(count)]
        return lax.ppermute(value, "head", pairs)

    def swap(value, mask):
        return lax.ppermute(value, "dp", [(i, i ^ mask) for i in range(data_count)])

    def xor_head(value, mask):
        return lax.ppermute(value, "head", [(i, i ^ mask) for i in range(count)])

    def ring_gather(value):
        half = value.shape[0] // 2
        got = {0: value}
        for away in range(1, half_count):
            got[away] = rot(got[away - 1], 1)
            got[-away] = rot(got[1 - away], -1)
        got[half_count] = jnp.concatenate(
            [rot(got[half_count - 1][:half], 1), rot(got[1 - half_count][half:], -1)], 0
        )
        return got

    def ring_reduce(block):
        far = block(half_count)
        half = far.shape[0] // 2
        up, down = rot(far[:half], -1), rot(far[half:], 1)
        near = block(half_count - 1)
        ups = jnp.concatenate([near[:half].astype(F32) + up, near[half:].astype(F32)], 0)
        near = block(1 - half_count)
        downs = jnp.concatenate([near[:half].astype(F32), near[half:].astype(F32) + down], 0)
        for away in range(half_count - 1, 0, -1):
            up, down = rot(ups.astype(BF16), -1), rot(downs.astype(BF16), 1)
            if away > 1:
                ups = block(away - 1).astype(F32) + up
                downs = block(1 - away).astype(F32) + down
        return block(0).astype(F32) + up.astype(F32) + down.astype(F32)

    cond = jnp.take(class_table, class_ids, axis=0).astype(F32)
    act = jax.nn.silu(cond).astype(BF16)
    mod_local = jnp.dot(act, ada_weight, preferred_element_type=F32)[0] + ada_bias.astype(F32)
    small = jnp.concatenate([mod_local, fc1_bias.astype(F32)])[None, :]
    small_all = jnp.concatenate(
        [small] + [xor_head(small, mask) for mask in range(1, count)], 0
    )
    small_all = jnp.take(
        small_all, jnp.bitwise_xor(me, jnp.arange(count, dtype=jnp.int32)), axis=0
    )
    mod_here = mod_local.shape[0]
    modulation = small_all[:, :mod_here].reshape(6, width)
    shift_one, scale_one, gate_one, shift_two, scale_two, gate_two = [
        modulation[i : i + 1] for i in range(6)
    ]
    class_rows = jnp.concatenate(
        [class_ids] + [swap(class_ids, mask) for mask in range(1, data_count)], 0
    )

    def quarters(value):
        return value.reshape(4, value.shape[0] // 4, width)

    fc1_rows, fc2_rows, proj_rows = quarters(fc1_weight.T), quarters(fc2_weight), quarters(proj_weight)
    fc_part, proj_part = fc1_rows.shape[1], proj_rows.shape[1]

    def pick(rows):
        return lax.dynamic_index_in_dim(rows, quarter, 0, keepdims=False)

    def spread(own, own_all):
        got = ring_gather(own)
        result = [own_all[i : i + 1] for i in range(4)]
        pairs = [(away, -away) for away in range(1, half_count)] + [(half_count,)]
        for group in pairs:
            mine = jnp.stack([got[away] for away in group], 0)
            both = jnp.stack([mine, swap(mine, 2)], 0)
            other = swap(both, 1)
            for i in range(2):
                result[i] = jnp.concatenate([result[i], both[i]], 0)
                result[2 + i] = jnp.concatenate([result[2 + i], other[i]], 0)
        return jnp.stack(result, 0)

    first_own = jnp.concatenate([fc1_rows, proj_rows], 1)
    first_full = spread(pick(first_own), jnp.take(first_own, rel_quarters, axis=0))
    second_full = spread(pick(fc2_rows), jnp.take(fc2_rows, rel_quarters, axis=0))
    fc1_full = first_full[:, :, :fc_part].reshape(-1, width)
    proj_full = jnp.take(first_full[:, :, fc_part:], abs_to_rel, axis=0)
    proj_full = jnp.transpose(proj_full, (1, 0, 2, 3)).reshape(-1, width)
    fc2_full = second_full.reshape(-1, width)
    offset_heads = jnp.stack([at(away) for away in offsets])
    bias_full = jnp.take(small_all[:, mod_here:], offset_heads, axis=0).reshape(count, 4, fc_part)
    bias_full = jnp.transpose(jnp.take(bias_full, rel_quarters, axis=1), (1, 0, 2)).reshape(1, -1)

    inputs_full = block_input[0].astype(F32)
    unit_one, recip_one = normalize(inputs_full)
    unit_low = unit_one.astype(BF16)
    qkv_rows = jnp.transpose(qkv_weight.T.reshape(heads, 3, HD, width), (1, 0, 2, 3)).reshape(
        3 * feats, width
    )
    qkv_mod = (qkv_rows.astype(F32) * (1.0 + scale_one)).astype(BF16)
    bias_pair = qv_bias.astype(F32).reshape(heads, 2, HD)
    qkv_bias = jnp.stack([bias_pair[:, 0], jnp.zeros_like(bias_pair[:, 0]), bias_pair[:, 1]], 0)
    qkv_bias = qkv_bias.reshape(3 * feats, 1) + jnp.sum(
        qkv_rows.astype(F32) * shift_one, 1, keepdims=True
    )
    units = ring_gather(unit_low)
    unit_all = jnp.zeros((slots, width), BF16)
    raw = jnp.zeros((3 * feats, slots), F32)
    for away in offsets:
        piece = units[away]
        start = at(away) * local
        unit_all = lax.dynamic_update_slice(unit_all, piece, (start, 0))
        raw = lax.dynamic_update_slice(raw, dot(qkv_mod, piece, 1, 1) + qkv_bias, (0, start))
    low, high, spans = intervals(lengths[0], slots)
    scale_exp = jnp.exp(qk_scale)
    out, out_low, lse = attention_forward(raw, spans, scale_exp, low, high, heads)

    attended = []
    for away in offsets:
        piece = lax.dynamic_slice(out_low, (0, at(-away) * local), (feats, local))
        attended.append(piece if away == 0 else rot(piece, away))
    attended = jnp.concatenate(attended, 0)
    attn_branch = dot(attended, proj_full, 0, 0) + proj_bias.astype(F32)
    resid = inputs_full + gate_one * attn_branch
    unit_two, recip_two = normalize(resid)
    normed_two = (unit_two * (1.0 + scale_two) + shift_two).astype(BF16)
    pre_act = dot(normed_two, fc1_full, 1, 1) + bias_full
    hidden = gelu_tanh(pre_act).astype(BF16)
    mlp_branch = dot(hidden, fc2_full, 1, 0) + fc2_bias.astype(F32)
    block_output = (resid + gate_two * mlp_branch).astype(BF16)

    cot_full = cotangent[0].astype(F32)
    grad_mlp = (cot_full * gate_two).astype(BF16)
    grad_gate_two = jnp.sum(cot_full * mlp_branch, 0)
    fc2_bias_sum = jnp.sum(grad_mlp.astype(F32), 0)
    grad_hidden = dot(grad_mlp, fc2_full, 1, 1)
    _, gelu_pull = jax.vjp(gelu_tanh, pre_act)
    grad_pre = gelu_pull(grad_hidden)[0].astype(BF16)
    fc1_bias_sum = jnp.sum(grad_pre.astype(F32), 0)
    grad_normed_two = dot(grad_pre, fc1_full, 1, 0)
    grad_shift_two = jnp.sum(grad_normed_two, 0)
    grad_scale_two = jnp.sum(grad_normed_two * unit_two, 0)
    grad_resid = cot_full + norm_back(unit_two, recip_two, grad_normed_two * (1.0 + scale_two))
    grad_attn = (grad_resid * gate_one).astype(BF16)
    grad_gate_one = jnp.sum(grad_resid * attn_branch, 0)
    proj_bias_sum = jnp.sum(grad_attn.astype(F32), 0)
    grad_attended = dot(proj_full, grad_attn, 1, 1).astype(BF16)
    up = jnp.zeros((feats, slots), BF16)
    for index, away in enumerate(offsets):
        piece = grad_attended[index * feats : (index + 1) * feats]
        piece = piece if away == 0 else rot(piece, -away)
        up = lax.dynamic_update_slice(up, piece, (0, at(-away) * local))

    half_cols = 2 * count * fc_part

    def reduce_rows(send, keep, part):
        kept = keep.astype(F32) + swap(send.astype(BF16), 1)
        kept = kept.reshape(2, count, part, width)
        mine = (kept[0] + swap(kept[1].astype(BF16), 2)).astype(BF16)
        return mine

    fc2_mine = reduce_rows(
        dot(hidden[:, half_cols:], grad_mlp, 0, 0), dot(hidden[:, :half_cols], grad_mlp, 0, 0), fc_part
    )
    fc1_mine = reduce_rows(
        dot(grad_pre[:, half_cols:], normed_two, 0, 0),
        dot(grad_pre[:, :half_cols], normed_two, 0, 0),
        fc_part,
    )
    proj_grad = dot(attended, grad_attn, 1, 0).astype(BF16)
    proj_grad = jnp.transpose(proj_grad.reshape(count, 4, proj_part, width), (1, 0, 2, 3))
    proj_grad = jnp.take(proj_grad, rel_quarters, axis=0)
    proj_mine = reduce_rows(proj_grad[2:], proj_grad[:2], proj_part)

    def ring_rest(mine):
        total = ring_reduce(lambda away: mine[offsets.index(away)])
        mask = 4
        while mask < data_count:
            total = total + swap(total.astype(BF16), mask)
            mask *= 2
        total = total.astype(BF16)
        both = jnp.stack([total, swap(total, 2)], 0)
        return jnp.take(jnp.concatenate([both, swap(both, 1)], 0), abs_to_rel, axis=0)

    fc2_rows_grad = ring_rest(fc2_mine)
    first_grad = ring_rest(jnp.concatenate([fc1_mine, proj_mine], 1))
    fc2_weight_grad = fc2_rows_grad.reshape(-1, width).astype(F32)
    fc1_weight_grad = first_grad[:, :fc_part].reshape(-1, width).astype(F32).T
    proj_weight_grad = first_grad[:, fc_part:].reshape(-1, width).astype(F32)

    bounds = jnp.sum(lengths[0])
    slot_places = me * local + jnp.arange(local, dtype=jnp.int32)
    valid = slot_places < bounds
    code_range = jnp.arange(CODES, dtype=jnp.int32)
    code_hits = (code_ids[0][:, None] == code_range[None, :]) & valid[:, None]
    local_counts = jnp.sum(code_hits.astype(F32), 0)
    fc1_bias_blocks = jnp.take(fc1_bias_sum.reshape(4, count, fc_part), abs_to_rel, axis=0)
    fc1_bias_blocks = jnp.transpose(fc1_bias_blocks, (1, 0, 2)).reshape(count, hidden_here)
    common = jnp.concatenate([local_counts, fc2_bias_sum, proj_bias_sum])
    parts = []
    for index, away in enumerate(offsets):
        piece = jnp.concatenate([fc1_bias_blocks[index], common])[None, :]
        parts.append(piece if away == 0 else rot(piece, -away))
    sums = functools.reduce(lambda a, b: a + b, parts)
    mask = 1
    while mask < data_count:
        sums = sums + swap(sums, mask)
        mask *= 2
    sums = sums[0]
    fc1_bias_grad = sums[:hidden_here]
    code_hist = sums[hidden_here : hidden_here + CODES].astype(jnp.int32)
    fc2_bias_grad = sums[hidden_here + CODES : hidden_here + CODES + width]
    proj_bias_grad = sums[hidden_here + CODES + width :]

    grad_raw, query_sums = attention_backward(
        raw, out, lse, up, spans, scale_exp, low, high, heads
    )

    def one_terms(away):
        piece = lax.dynamic_slice(grad_raw, (0, at(away) * local), (3 * feats, local))
        return dot(piece, qkv_rows, 0, 0).astype(BF16)

    grad_normed_one = ring_reduce(one_terms)
    bias_sums = jnp.sum(grad_raw.astype(F32), 1)
    qkv_grad = dot(grad_raw, unit_all, 1, 0) * (1.0 + scale_one) + bias_sums[:, None] * shift_one
    qkv_grad = qkv_grad.astype(BF16)
    scale_sums = scale_exp * jnp.sum(query_sums, 1)
    tail = jnp.concatenate([bias_sums, scale_sums])[None, :]
    mask = 1
    while mask < data_count:
        qkv_grad = (qkv_grad.astype(F32) + swap(qkv_grad, mask)).astype(BF16)
        tail = tail + swap(tail, mask)
        mask *= 2
    qkv_weight_grad = (
        jnp.transpose(qkv_grad.reshape(3, heads, HD, width), (1, 0, 2, 3))
        .reshape(3 * feats, width)
        .astype(F32)
        .T
    )
    tail = tail[0]
    qk_scale_grad = tail[3 * feats :]
    bias_sums = tail[: 3 * feats].reshape(3, heads, HD)
    qv_bias_grad = jnp.stack([bias_sums[0], bias_sums[2]], 1).reshape(-1)

    grad_shift_one = jnp.sum(grad_normed_one, 0)
    grad_scale_one = jnp.sum(grad_normed_one * unit_one, 0)
    input_grad = (
        grad_resid + norm_back(unit_one, recip_one, grad_normed_one * (1.0 + scale_one))
    ).astype(BF16)

    grad_mod = jnp.concatenate(
        [
            grad_shift_one,
            grad_scale_one,
            grad_gate_one,
            grad_shift_two,
            grad_scale_two,
            grad_gate_two,
        ]
    ).reshape(count, mod_here)
    mod_sum = lax.dynamic_slice_in_dim(grad_mod, me, 1, 0)
    for mask in range(1, count):
        mine = lax.dynamic_slice_in_dim(grad_mod, jnp.bitwise_xor(me, mask), 1, 0)
        mod_sum = mod_sum + xor_head(mine, mask)
    mod_rows = jnp.concatenate(
        [mod_sum] + [swap(mod_sum, mask) for mask in range(1, data_count)], 0
    )
    cond_rows = jnp.take(class_table, class_rows, axis=0).astype(F32)
    act_rows = jax.nn.silu(cond_rows).astype(BF16).astype(F32)
    ada_weight_grad = lax.dot_general(
        act_rows, mod_rows, (((0,), (0,)), ((), ())), precision=HIGH
    )
    ada_bias_grad = jnp.sum(mod_rows, 0)
    cond_terms = lax.dot_general(
        mod_rows, ada_weight.astype(F32), (((1,), (1,)), ((), ())), precision=HIGH
    )
    cond_sums = cond_terms
    for mask in range(1, count):
        cond_sums = cond_sums + xor_head(cond_terms, mask)
    _, silu_pull = jax.vjp(jax.nn.silu, cond_rows)
    grad_rows = silu_pull(cond_sums)[0]
    class_range = jnp.arange(class_table.shape[0], dtype=jnp.int32)
    class_table_grad = jnp.zeros(class_table.shape, F32)
    for row in range(data_count):
        hit = class_range[:, None] == class_rows[row]
        class_table_grad = class_table_grad + jnp.where(hit, grad_rows[row][None, :], 0.0)
    return (
        block_output[None],
        input_grad[None],
        class_table_grad,
        ada_weight_grad,
        ada_bias_grad,
        qkv_weight_grad,
        qv_bias_grad,
        qk_scale_grad,
        proj_weight_grad,
        proj_bias_grad,
        fc1_weight_grad,
        fc1_bias_grad,
        fc2_weight_grad,
        fc2_bias_grad,
        code_hist,
    )


def solution(mesh):
    placed = (
        P("dp", "head", None),
        P("dp", None),
        P("dp", None),
        P("dp"),
        P("dp", "head"),
        P("dp", "head", None),
        P(),
        P(None, "head"),
        P("head"),
        P(None, "head"),
        P("head"),
        P("head"),
        P("head", None),
        P(),
        P(None, "head"),
        P("head"),
        P("head", None),
        P(),
    )
    return jax.shard_map(
        shards,
        mesh=mesh,
        in_specs=placed,
        out_specs=(
            P("dp", "head", None),
            P("dp", "head", None),
            P(),
            P(None, "head"),
            P("head"),
            P(None, "head"),
            P("head"),
            P("head"),
            P("head", None),
            P(),
            P(None, "head"),
            P("head"),
            P("head", None),
            P(),
            P(),
        ),
        check_vma=False,
    )
```

```python
import functools

import jax
import jax.numpy as jnp
from jax import lax
from jax.experimental import pallas as pl
from jax.experimental.pallas import tpu as pltpu
from jax.sharding import PartitionSpec as P

HD = 64
CODES = 4096
BLK = 256
FORWARD_BLOCK = (512, 512)
BACKWARD_BLOCK = (256, 512)
EPS_NORM = 1e-06
HIGH = lax.Precision.HIGHEST
F32 = jnp.float32
BF16 = jnp.bfloat16
BIG_LEN = 2240
BIG_CUMS = (1, 5, 14, 30, 66, 147, 316, 640, 1216, 2240)
SMALL_CUMS = (1, 5, 14, 30, 55, 91, 155, 255, 424, 680)


def normalize(values):
    mean_val = jnp.mean(values, -1, keepdims=True)
    centered = values - mean_val
    variance = jnp.mean(centered * centered, -1, keepdims=True)
    recip = lax.rsqrt(variance + EPS_NORM)
    return (centered * recip, recip)


def norm_back(unit, recip, upstream):
    mean_up = jnp.mean(upstream, -1, keepdims=True)
    mean_cross = jnp.mean(upstream * unit, -1, keepdims=True)
    return recip * (upstream - mean_up - unit * mean_cross)


def gelu_tanh(values):
    return jax.nn.gelu(values, approximate=True)


def dot(left, right, left_dim, right_dim):
    return lax.dot_general(
        left, right, (((left_dim,), (right_dim,)), ((), ())), preferred_element_type=F32
    )


def head_pad(part, head, heads):
    pieces = [part if other == head else jnp.zeros_like(part) for other in range(heads)]
    return pieces[0] if heads == 1 else jnp.concatenate(pieces, 0)


def unit_rows(raw):
    recip = lax.rsqrt(jnp.sum(raw * raw, 0, keepdims=True) + EPS_NORM)
    return raw * recip, recip


def interval(places, lengths_ref, slots):
    first, second, third = lengths_ref[0], lengths_ref[1], lengths_ref[2]
    end_one, end_two = first + second, first + second + third
    low = jnp.where(places >= end_one, end_one, jnp.where(places >= first, first, 0))
    size = jnp.where(places >= end_one, third, jnp.where(places >= first, second, first))
    big, offset = size == BIG_LEN, places - low
    reach = jnp.where(big, BIG_CUMS[0], SMALL_CUMS[0])
    for level in range(1, len(BIG_CUMS)):
        passed = offset >= jnp.where(big, BIG_CUMS[level - 1], SMALL_CUMS[level - 1])
        reach = jnp.where(passed, jnp.where(big, BIG_CUMS[level], SMALL_CUMS[level]), reach)
    padding = places >= end_two
    return jnp.where(padding, end_two, low), jnp.where(padding, slots, low + reach)


def key_spans(step, lengths_ref, slots, rows_q, rows_k):
    first_low, first_high = interval(step * rows_q, lengths_ref, slots)
    last_low, last_high = interval(step * rows_q + rows_q - 1, lengths_ref, slots)
    first = lax.div(first_low, rows_k)
    last = lax.div(last_high + rows_k - 1, rows_k)
    full_first = jnp.minimum(lax.div(last_low + rows_k - 1, rows_k), last)
    full_last = jnp.maximum(lax.div(first_high, rows_k), full_first)
    rows = interval(
        step * rows_q + lax.broadcasted_iota(jnp.int32, (1, rows_q), 1), lengths_ref, slots
    )
    return (first, full_first, full_last, last), rows


def key_loops(spans, body, carry):
    first, full_first, full_last, last = spans
    carry = lax.fori_loop(first, full_first, functools.partial(body, True), carry)
    carry = lax.fori_loop(full_first, full_last, functools.partial(body, False), carry)
    return lax.fori_loop(full_last, last, functools.partial(body, True), carry)


def allowed_block(block, rows_k, low_row, high_row):
    places = block * rows_k + lax.broadcasted_iota(jnp.int32, (rows_k, low_row.shape[1]), 0)
    return (places >= low_row) & (places < high_row)


def project_kernel(
    heads, place_ref, scale_ref, piece_ref, weight_ref, mod_ref, bias_ref, *refs
):
    width = heads * HD
    raw_ref, query_ref, key_ref, keyt_ref, value_ref, valuet_ref, unit_ref = refs[-7:]
    piece = piece_ref[...]
    unit_ref[...] = piece
    normed = (piece.astype(F32) * (1.0 + mod_ref[1:2, :]) + mod_ref[0:1, :]).astype(BF16)
    raw = dot(weight_ref[...], normed, 1, 1) + bias_ref[...]
    raw_ref[...] = raw
    for head in range(heads):
        part = slice(head * HD, (head + 1) * HD)
        unit, _ = unit_rows(raw[part])
        query_ref[part, :] = (unit * scale_ref[head]).astype(BF16)
    keys = [unit_rows(raw[width + head * HD : width + (head + 1) * HD])[0] for head in range(heads)]
    keys = keys[0] if heads == 1 else jnp.concatenate(keys, 0)
    values = raw[2 * width :]
    keyt_ref[...] = keys.astype(BF16)
    key_ref[...] = jnp.transpose(keys).astype(BF16)
    valuet_ref[...] = values.astype(BF16)
    value_ref[...] = jnp.transpose(values).astype(BF16)


def project(place, piece, weight, mod, bias, scales, held, heads, slots):
    width, local, depth = heads * HD, piece.shape[0], piece.shape[1]

    def fixed(shape):
        return pl.BlockSpec(shape, lambda step, *_: (0, 0))

    def columns(rows):
        return pl.BlockSpec((rows, local), lambda step, place, scales: (0, place[0]))

    def lines(cols):
        return pl.BlockSpec((local, cols), lambda step, place, scales: (place[0], 0))

    shapes = [
        jax.ShapeDtypeStruct((3 * width, slots), F32),
        jax.ShapeDtypeStruct((width, slots), BF16),
        jax.ShapeDtypeStruct((slots, width), BF16),
        jax.ShapeDtypeStruct((width, slots), BF16),
        jax.ShapeDtypeStruct((slots, width), BF16),
        jax.ShapeDtypeStruct((width, slots), BF16),
        jax.ShapeDtypeStruct((slots, depth), BF16),
    ]
    held = list(held)
    return pl.pallas_call(
        functools.partial(project_kernel, heads),
        grid_spec=pltpu.PrefetchScalarGridSpec(
            num_scalar_prefetch=2,
            grid=(1,),
            in_specs=[
                fixed((local, depth)),
                fixed((3 * width, depth)),
                fixed((2, depth)),
                fixed((3 * width, 1)),
            ]
            + [pl.BlockSpec(memory_space=pl.ANY)] * len(held),
            out_specs=[
                columns(3 * width),
                columns(width),
                lines(width),
                columns(width),
                lines(width),
                columns(width),
                lines(depth),
            ],
        ),
        out_shape=shapes,
        input_output_aliases={6 + i: i for i in range(len(held))},
        compiler_params=pltpu.CompilerParams(vmem_limit_bytes=40 * 2**20),
        cost_estimate=pl.CostEstimate(
            flops=2 * 3 * width * local * depth, bytes_accessed=8 * 2**20, transcendentals=0
        ),
        name="project",
    )(place, scales, piece, weight, mod, bias, *held)


def forward_kernel(heads, rows_k, lengths_ref, query_ref, key_ref, valuet_ref, out_ref, lse_ref):
    step = pl.program_id(0)
    slots, rows_q = key_ref.shape[0], query_ref.shape[1]
    queries = [
        head_pad(query_ref[head * HD : (head + 1) * HD, :], head, heads) for head in range(heads)
    ]
    spans, (low_row, high_row) = key_spans(step, lengths_ref, slots, rows_q, rows_k)

    def body(masked, block, carry):
        rows = pl.ds(pl.multiple_of(block * rows_k, rows_k), rows_k)
        keys = key_ref[rows, :]
        if masked:
            allowed = allowed_block(block, rows_k, low_row, high_row)
        result = []
        for head in range(heads):
            total, acc = carry[head]
            probs = jnp.exp(dot(keys, queries[head], 1, 0))
            if masked:
                probs = jnp.where(allowed, probs, 0.0)
            total = total + jnp.sum(probs.reshape(rows_k // 8, 8, rows_q), 0)
            acc = acc + dot(
                valuet_ref[head * HD : (head + 1) * HD, rows], probs.astype(BF16), 1, 0
            )
            result.append((total, acc))
        return tuple(result)

    start = tuple(
        (jnp.zeros((8, rows_q), F32), jnp.zeros((HD, rows_q), F32)) for _ in range(heads)
    )
    final = key_loops(spans, body, start)
    for head in range(heads):
        total, acc = final[head]
        denom = jnp.sum(total, 0, keepdims=True)
        out_ref[head * HD : (head + 1) * HD, :] = (acc / denom).astype(BF16)
        lse_ref[head : head + 1, :] = jnp.log(denom)


def backward_kernel(
    heads,
    rows_k,
    lengths_ref,
    scale_ref,
    raw_ref,
    query_ref,
    key_ref,
    keyt_ref,
    value_ref,
    lse_ref,
    up_ref,
    grad_ref,
    qsum_ref,
    gkey_s,
    gvalue_s,
    probs_s,
    gprobs_s,
):
    step = pl.program_id(0)
    width = heads * HD
    slots, rows_q = raw_ref.shape[1], query_ref.shape[1]

    @pl.when(step == 0)
    def _():
        gkey_s[...] = jnp.zeros_like(gkey_s)
        gvalue_s[...] = jnp.zeros_like(gvalue_s)

    queries, query_rows, ups, up_rows, lses = [], [], [], [], []
    for head in range(heads):
        part = slice(head * HD, (head + 1) * HD)
        padded = head_pad(query_ref[part, :], head, heads)
        queries.append(padded)
        query_rows.append(jnp.transpose(padded.astype(F32)).astype(BF16))
        padded = head_pad(up_ref[part, :], head, heads)
        ups.append(padded)
        up_rows.append(jnp.transpose(padded.astype(F32)).astype(BF16))
        lses.append(lse_ref[head : head + 1, :])
    spans, (low_row, high_row) = key_spans(step, lengths_ref, slots, rows_q, rows_k)

    def first(masked, block, carry):
        rows = pl.ds(pl.multiple_of(block * rows_k, rows_k), rows_k)
        keys, values = key_ref[rows, :], value_ref[rows, :]
        if masked:
            allowed = allowed_block(block, rows_k, low_row, high_row)
        result = []
        for head in range(heads):
            probs = jnp.exp(dot(keys, queries[head], 1, 0) - lses[head])
            if masked:
                probs = jnp.where(allowed, probs, 0.0)
            grad_probs = dot(values, ups[head], 1, 0)
            probs_s[head, rows, :] = probs
            gprobs_s[head, rows, :] = grad_probs
            terms = (probs * grad_probs).reshape(rows_k // 8, 8, rows_q)
            result.append(carry[head] + jnp.sum(terms, 0))
        return tuple(result)

    deltas = key_loops(spans, first, tuple(jnp.zeros((8, rows_q), F32) for _ in range(heads)))
    deltas = [jnp.sum(delta, 0, keepdims=True) for delta in deltas]

    def second(block, carry):
        rows = pl.ds(pl.multiple_of(block * rows_k, rows_k), rows_k)
        result = []
        gkey, gvalue = gkey_s[rows, :], gvalue_s[rows, :]
        for head in range(heads):
            probs = probs_s[head, rows, :]
            grad_scores = (probs * (gprobs_s[head, rows, :] - deltas[head])).astype(BF16)
            gvalue = gvalue + dot(probs.astype(BF16), up_rows[head], 1, 0)
            gkey = gkey + dot(grad_scores, query_rows[head], 1, 0)
            keyt = keyt_ref[head * HD : (head + 1) * HD, rows]
            result.append(carry[head] + dot(keyt, grad_scores, 1, 0))
        gkey_s[rows, :] = gkey
        gvalue_s[rows, :] = gvalue
        return tuple(result)

    start = tuple(jnp.zeros((HD, rows_q), F32) for _ in range(heads))
    final = lax.fori_loop(spans[0], spans[3], second, start)
    cols = pl.ds(pl.multiple_of(step * rows_q, rows_q), rows_q)
    for head in range(heads):
        part = slice(head * HD, (head + 1) * HD)
        grad = final[head]
        unit, recip = unit_rows(raw_ref[part, cols])
        qsum_ref[head : head + 1, :] = jnp.sum(grad * unit, 0, keepdims=True)
        scaled = scale_ref[head] * grad
        back = recip * (scaled - unit * jnp.sum(scaled * unit, 0, keepdims=True))
        grad_ref[part, cols] = back.astype(BF16)

    @pl.when(step == pl.num_programs(0) - 1)
    def _():
        def finish(block, carry):
            cols = pl.ds(pl.multiple_of(block * BLK, BLK), BLK)
            gkey = jnp.transpose(gkey_s[cols, :])
            for head in range(heads):
                part = slice(width + head * HD, width + (head + 1) * HD)
                unit, recip = unit_rows(raw_ref[part, cols])
                grad = gkey[head * HD : (head + 1) * HD, :]
                back = recip * (grad - unit * jnp.sum(grad * unit, 0, keepdims=True))
                grad_ref[part, cols] = back.astype(BF16)
            grad_ref[2 * width :, cols] = jnp.transpose(gvalue_s[cols, :]).astype(BF16)
            return carry

        lax.fori_loop(0, slots // BLK, finish, 0)


def whole_spec(shape):
    return pl.BlockSpec(shape, lambda step, *_: (0,) * len(shape))


def column_spec(rows, cols):
    return pl.BlockSpec((rows, cols), lambda step, *_: (0, step))


def attention_forward(query, key, valuet, lengths, heads):
    width, slots = query.shape
    rows_q, rows_k = FORWARD_BLOCK
    return pl.pallas_call(
        functools.partial(forward_kernel, heads, rows_k),
        grid_spec=pltpu.PrefetchScalarGridSpec(
            num_scalar_prefetch=1,
            grid=(slots // rows_q,),
            in_specs=[column_spec(width, rows_q), whole_spec(key.shape), whole_spec(valuet.shape)],
            out_specs=[column_spec(width, rows_q), column_spec(heads, rows_q)],
        ),
        out_shape=[
            jax.ShapeDtypeStruct((width, slots), BF16),
            jax.ShapeDtypeStruct((heads, slots), F32),
        ],
        compiler_params=pltpu.CompilerParams(
            dimension_semantics=("arbitrary",), vmem_limit_bytes=32 * 2**20
        ),
        cost_estimate=pl.CostEstimate(
            flops=heads * slots * slots * 1000, bytes_accessed=4 * 2**20, transcendentals=0
        ),
        name="attend",
    )(lengths, query, key, valuet)


def attention_backward(raw, query, key, keyt, value, lse, up, lengths, scales, heads):
    width, slots = query.shape
    rows_q, rows_k = BACKWARD_BLOCK
    return pl.pallas_call(
        functools.partial(backward_kernel, heads, rows_k),
        grid_spec=pltpu.PrefetchScalarGridSpec(
            num_scalar_prefetch=2,
            grid=(slots // rows_q,),
            in_specs=[
                whole_spec(raw.shape),
                column_spec(width, rows_q),
                whole_spec(key.shape),
                whole_spec(keyt.shape),
                whole_spec(value.shape),
                column_spec(heads, rows_q),
                column_spec(width, rows_q),
            ],
            out_specs=[whole_spec(raw.shape), column_spec(heads, rows_q)],
            scratch_shapes=[
                pltpu.VMEM((slots, width), F32),
                pltpu.VMEM((slots, width), F32),
                pltpu.VMEM((heads, slots, rows_q), F32),
                pltpu.VMEM((heads, slots, rows_q), F32),
            ],
        ),
        out_shape=[
            jax.ShapeDtypeStruct(raw.shape, BF16),
            jax.ShapeDtypeStruct((heads, slots), F32),
        ],
        compiler_params=pltpu.CompilerParams(
            dimension_semantics=("arbitrary",), vmem_limit_bytes=56 * 2**20
        ),
        cost_estimate=pl.CostEstimate(
            flops=heads * slots * slots * 2000, bytes_accessed=14 * 2**20, transcendentals=0
        ),
        name="attend_back",
    )(lengths, scales, raw, query, key, keyt, value, lse, up)


def after(value, *others):
    return lax.optimization_barrier((value, *others))[0]


def shards(
    block_input,
    lengths,
    scale_ids,
    class_ids,
    code_ids,
    cotangent,
    class_table,
    ada_weight,
    ada_bias,
    qkv_weight,
    qv_bias,
    qk_scale,
    proj_weight,
    proj_bias,
    fc1_weight,
    fc1_bias,
    fc2_weight,
    fc2_bias,
):
    count, data_count = lax.axis_size("head"), lax.axis_size("dp")
    me, data_me = lax.axis_index("head"), lax.axis_index("dp")
    _, local, width = block_input.shape
    slots = local * count
    heads = qk_scale.shape[0]
    feats = heads * HD
    hidden_here = fc1_weight.shape[1]
    data_masks = [1 << bit for bit in range(data_count.bit_length() - 1)]
    both_axes = ("dp", "head")

    ring = list(range(0, count, 2)) + list(range(count - 1, 0, -2))
    half_count = count // 2
    offsets = [0]
    for away in range(1, half_count):
        offsets += [away, -away]
    offsets.append(half_count)
    my_pos = jnp.where(me % 2 == 0, me // 2, count - 1 - me // 2)

    def at(away):
        pos = (my_pos + away + count) % count
        return jnp.where(pos < half_count, 2 * pos, 2 * (count - 1 - pos) + 1)

    def rot(value, away):
        pairs = [(ring[(i + away) % count], ring[i]) for i in range(count)]
        return lax.ppermute(value, "head", pairs)

    def swap(value, mask):
        return lax.ppermute(value, "dp", [(i, i ^ mask) for i in range(data_count)])

    def xor_head(value, mask):
        return lax.ppermute(value, "head", [(i, i ^ mask) for i in range(count)])

    def head_sum_far(value):
        total = value
        for mask in range(2, count, 2):
            total = total + xor_head(value, mask)
        return total

    def head_sum_near(value):
        return value + xor_head(value, 1)

    inputs_full = block_input[0].astype(F32)
    unit_one, recip_one = normalize(inputs_full)
    unit_low = unit_one.astype(BF16)

    hidden_part, feat_part = hidden_here // data_count, feats // data_count
    fc1_part = lax.dynamic_slice(fc1_weight, (0, data_me * hidden_part), (width, hidden_part)).T
    proj_part = lax.dynamic_slice(proj_weight, (data_me * feat_part, 0), (feat_part, width))
    fc2_part = lax.dynamic_slice(fc2_weight, (data_me * hidden_part, 0), (hidden_part, width))
    first_full = lax.all_gather(
        jnp.concatenate([fc1_part, proj_part], 0), both_axes, axis=0, tiled=False
    ).reshape(data_count, count, hidden_part + feat_part, width)
    fc2_full = lax.all_gather(fc2_part, both_axes, axis=0, tiled=True)
    fc1_full = first_full[:, :, :hidden_part].reshape(-1, width)
    proj_full = jnp.transpose(first_full[:, :, hidden_part:], (1, 0, 2, 3)).reshape(-1, width)

    cond = jnp.take(class_table, class_ids, axis=0).astype(F32)
    act = jax.nn.silu(cond).astype(BF16)
    mod_local = jnp.dot(act, ada_weight, preferred_element_type=F32)[0] + ada_bias.astype(F32)
    small = jnp.concatenate([mod_local, fc1_bias.astype(F32)])[None, :]
    pieces = [small] + [xor_head(small, mask) for mask in range(2, count, 2)]
    units = {0: unit_low, 1: rot(unit_low, 1), -1: rot(unit_low, -1)}
    units[1], units[-1], pieces = lax.optimization_barrier((units[1], units[-1], pieces))
    pieces = jnp.concatenate(pieces, 0)
    if half_count > 2:
        units[2], units[-2] = rot(units[1], 1), rot(units[-1], -1)
    small_all = jnp.stack([pieces, xor_head(pieces, 1)], 1).reshape(count, -1)
    if half_count > 2:
        units[2], units[-2], small_all = lax.optimization_barrier(
            (units[2], units[-2], small_all)
        )
    small_all = jnp.take(
        small_all, jnp.bitwise_xor(me, jnp.arange(count, dtype=jnp.int32)), axis=0
    )
    mod_here = mod_local.shape[0]
    modulation = small_all[:, :mod_here].reshape(6, width)
    shift_one, scale_one, gate_one, shift_two, scale_two, gate_two = [
        modulation[i : i + 1] for i in range(6)
    ]
    bias_full = small_all[:, mod_here:].reshape(count, data_count, hidden_part)
    bias_full = jnp.transpose(bias_full, (1, 0, 2)).reshape(1, -1)

    qkv_rows = jnp.transpose(
        after(qkv_weight, small_all).T.reshape(heads, 3, HD, width), (1, 0, 2, 3)
    ).reshape(3 * feats, width)
    bias_pair = qv_bias.astype(F32).reshape(heads, 2, HD)
    qkv_bias = jnp.stack([bias_pair[:, 0], jnp.zeros_like(bias_pair[:, 0]), bias_pair[:, 1]], 0)
    qkv_bias = qkv_bias.reshape(3 * feats, 1)
    scale_exp = jnp.exp(qk_scale)

    def put(held, away):
        place = at(away).astype(jnp.int32)[None]
        return project(
            place, units[away], qkv_rows, modulation[:2], qkv_bias, scale_exp, held, heads, slots
        )

    for away in range(3, half_count):
        units[away], units[-away] = rot(units[away - 1], 1), rot(units[1 - away], -1)
    held = put([], 0)
    for away in range(1, half_count - 1):
        held = put(put(held, away), -away)
        if away == 1:
            last, units[half_count - 1], units[1 - half_count] = lax.optimization_barrier(
                (held[1], units[half_count - 1], units[1 - half_count])
            )
            held = [held[0], last] + list(held[2:])
    half = local // 2
    ends = [
        rot(units[half_count - 1][:half], 1),
        rot(units[1 - half_count][half:], -1),
    ]
    held = put(put(held, half_count - 1), 1 - half_count)
    units[half_count] = jnp.concatenate(ends, 0)
    held = put(held, half_count)
    raw, query, key, keyt, value, valuet, unit_all = held
    query, fc1_full, proj_full = lax.optimization_barrier((query, fc1_full, proj_full))
    out_low, lse = attention_forward(query, key, valuet, lengths[0], heads)

    attended = jnp.zeros((feats * count, local), BF16)
    for away in offsets:
        piece = lax.dynamic_slice(out_low, (0, at(-away) * local), (feats, local))
        piece = piece if away == 0 else rot(piece, away)
        attended = lax.dynamic_update_slice(attended, piece, (at(away) * feats, 0))
    cot_full = cotangent[0].astype(F32)
    grad_mlp = (cot_full * gate_two).astype(BF16)
    grad_hidden = dot(grad_mlp, fc2_full, 1, 1)
    attended, grad_hidden = lax.optimization_barrier((attended, grad_hidden))
    attn_branch = dot(attended, proj_full, 0, 0) + proj_bias.astype(F32)
    resid = inputs_full + gate_one * attn_branch
    unit_two, recip_two = normalize(resid)
    normed_two = (unit_two * (1.0 + scale_two) + shift_two).astype(BF16)
    pre_act = dot(normed_two, fc1_full, 1, 1) + bias_full
    hidden_full, gelu_pull = jax.vjp(gelu_tanh, pre_act)
    hidden = hidden_full.astype(BF16)

    grad_pre = gelu_pull(grad_hidden)[0].astype(BF16)
    grad_normed_two = dot(grad_pre, fc1_full, 1, 0)
    grad_shift_two = jnp.sum(grad_normed_two, 0)
    grad_scale_two = jnp.sum(grad_normed_two * unit_two, 0)
    grad_resid = cot_full + norm_back(unit_two, recip_two, grad_normed_two * (1.0 + scale_two))
    grad_attn = (grad_resid * gate_one).astype(BF16)
    grad_gate_one = jnp.sum(grad_resid * attn_branch, 0)
    grad_attended = dot(proj_full, grad_attn, 1, 1).astype(BF16)
    up_pieces = {}
    for away in offsets:
        piece = lax.dynamic_slice(grad_attended, (at(away) * feats, 0), (feats, local))
        up_pieces[away] = piece if away == 0 else rot(piece, -away)

    near = [away for away in offsets if away in (1, -1, 2)]
    hidden_late, grad_pre_late, attended_late, arrived = lax.optimization_barrier(
        (hidden, grad_pre, attended, [up_pieces[away] for away in near])
    )
    for away, piece in zip(near, arrived):
        up_pieces[away] = piece
    block_cols = count * hidden_part

    def core_step(blocks):
        return {
            t: blocks(t).astype(F32) + swap(blocks(t ^ 1).astype(BF16), 1)
            for t in range(0, data_count, 2)
        }

    def fc2_block(t):
        part = jnp.bitwise_xor(data_me, t) * block_cols
        cols = lax.dynamic_slice(hidden_late, (0, part), (local, block_cols))
        return dot(cols, grad_mlp, 0, 0).reshape(count, hidden_part, width)

    def fc1_block(t):
        part = jnp.bitwise_xor(data_me, t) * block_cols
        cols = lax.dynamic_slice(grad_pre_late, (0, part), (local, block_cols))
        return dot(cols, normed_two, 0, 0).reshape(count, hidden_part, width)

    fc2_kept = core_step(fc2_block)
    fc2_stack = jnp.stack([fc2_kept[t].astype(BF16) for t in fc2_kept], 1)
    fc2_stack = fc2_stack.reshape(count, len(fc2_kept) * hidden_part, width)

    proj_grad = dot(attended_late, grad_attn, 1, 0).astype(BF16)
    proj_grad = proj_grad.reshape(count, data_count, feat_part, width)

    def first_block(t):
        part = lax.dynamic_index_in_dim(
            proj_grad, jnp.bitwise_xor(data_me, t), 1, keepdims=False
        )
        return jnp.concatenate([fc1_block(t), part.astype(F32)], 1)

    first_kept = core_step(first_block)

    def fold(kept):
        for mask in data_masks[1:]:
            kept = {
                t: kept[t] + swap(kept[t ^ mask].astype(BF16), mask)
                for t in kept
                if not t & mask
            }
        return kept[0]

    up = jnp.zeros((feats, slots), BF16)
    for away in offsets:
        up = lax.dynamic_update_slice(up, up_pieces[away], (0, at(-away) * local))
    up, first_kept, fc2_stack = lax.optimization_barrier((up, first_kept, fc2_stack))
    fc2_mine = lax.psum_scatter(fc2_stack, "head", scatter_dimension=0, tiled=True)
    fc2_mine = fc2_mine.reshape(len(fc2_kept), hidden_part, width)
    first_blocks = fold(first_kept).astype(BF16)

    def share(value):
        for mask in reversed(data_masks):
            value = jnp.stack([value, swap(value, mask)], 0)
        bits = len(data_masks)
        value = value.reshape((data_count,) + value.shape[bits:])
        table = [int(format(t, "b").zfill(bits)[::-1], 2) for t in range(data_count)]
        places = jnp.take(
            jnp.array(table, jnp.int32),
            jnp.bitwise_xor(data_me, jnp.arange(data_count, dtype=jnp.int32)),
        )
        return jnp.take(value, places, axis=0).astype(F32)

    fc2_bias_sum = jnp.sum(grad_mlp.astype(F32), 0)
    fc1_bias_sum = jnp.sum(grad_pre.astype(F32), 0)
    proj_bias_sum = jnp.sum(grad_attn.astype(F32), 0)
    valid = me * local + jnp.arange(local, dtype=jnp.int32) < jnp.sum(lengths[0])
    code_range = jnp.arange(CODES, dtype=jnp.int32)
    code_hits = (after(code_ids, units[1])[0][:, None] == code_range[None, :]) & valid[:, None]
    local_counts = jnp.sum(code_hits.astype(F32), 0)
    fc1_bias_sum = fc1_bias_sum.reshape(data_count, count, hidden_part)
    fc1_bias_sum = jnp.transpose(fc1_bias_sum, (1, 0, 2)).reshape(-1)
    early = jnp.concatenate(
        [
            local_counts,
            fc2_bias_sum,
            proj_bias_sum,
            fc1_bias_sum,
            grad_gate_one,
            grad_shift_two,
            grad_scale_two,
        ]
    )
    early, up = lax.optimization_barrier((early, up))
    early = head_sum_far(early[None, :])

    grad_raw, query_sums = attention_backward(
        raw, query, key, keyt, value, lse, up, lengths[0], scale_exp, heads
    )
    grad_raw, query_sums, first_blocks, early = lax.optimization_barrier(
        (grad_raw, query_sums, first_blocks, early)
    )

    held_rows = local + first_blocks.shape[1]
    half = held_rows // 2

    def block(away, source):
        piece = lax.dynamic_slice(source, (0, at(away) * local), (3 * feats, local))
        terms = dot(piece, qkv_rows, 0, 0).astype(BF16)
        weights = lax.dynamic_index_in_dim(first_blocks, at(away), 0, keepdims=False)
        return jnp.concatenate([terms, weights], 0).astype(F32)

    def send(ups, downs):
        return rot(ups.astype(BF16), -1), rot(downs.astype(BF16), 1)

    far = block(half_count, grad_raw)
    near_up, near_down = block(half_count - 1, grad_raw), block(1 - half_count, grad_raw)
    got_up, got_down = send(far[:half], far[half:])

    far_late, source = lax.optimization_barrier((far, grad_raw))
    bias_sums = jnp.sum(source.astype(F32), 1)
    unit_grad = dot(source, unit_all, 1, 0)
    qkv_grad = unit_grad * (1.0 + scale_one) + bias_sums[:, None] * shift_one
    qkv_grad = qkv_grad.astype(BF16)
    scale_sums = scale_exp * jnp.sum(query_sums, 1)
    rows_float = qkv_rows.astype(F32)
    grad_shift_one = jnp.sum(rows_float * bias_sums[:, None], 0)
    grad_scale_one = jnp.sum(rows_float * unit_grad, 0)
    mlp_branch = dot(after(hidden, far), fc2_full, 1, 0) + fc2_bias.astype(F32)
    block_output = (resid + gate_two * mlp_branch).astype(BF16)
    grad_gate_two = jnp.sum(cot_full * mlp_branch, 0)
    late = jnp.concatenate([grad_shift_one, grad_scale_one, grad_gate_two])[None, :]

    got_up, got_down, early, late, near_up, near_down = lax.optimization_barrier(
        (got_up, got_down, early, late, near_up, near_down)
    )
    ups = jnp.concatenate([near_up[:half] + got_up, near_up[half:]], 0)
    downs = jnp.concatenate([near_down[:half], near_down[half:] + got_down], 0)
    got_up, got_down = send(ups, downs)
    late = head_sum_far(late)
    early = head_sum_near(early)
    next_up, next_down = block(half_count - 2, source), block(2 - half_count, source)

    for away in range(half_count - 2, 0, -1):
        last = away == 1
        got_up, got_down, late, early, next_up, next_down = lax.optimization_barrier(
            (got_up, got_down, late, early, next_up, next_down)
        )
        if away == half_count - 2:
            got_up, got_down, fc2_mine = lax.optimization_barrier((got_up, got_down, fc2_mine))
        got_up, got_down = send(next_up + got_up, next_down + got_down)
        if away == half_count - 2:
            late = head_sum_near(late)[0]
            early = early[0]
            over_rows = CODES + 2 * width + count * hidden_here
            tail = jnp.concatenate([bias_sums, scale_sums, early[:over_rows]])[None, :]
            mod_all = jnp.concatenate([late[: 2 * width], early[over_rows:], late[2 * width :]])
            mod_rows = lax.dynamic_slice_in_dim(mod_all, me * mod_here, mod_here, 0)
            mod_rows = jnp.concatenate([mod_rows, class_ids.astype(F32)])[None, :]
            for mask in data_masks:
                mod_rows = jnp.concatenate([mod_rows, swap(mod_rows, mask)], 0)
                qkv_grad = (qkv_grad.astype(F32) + swap(qkv_grad, mask)).astype(BF16)
                tail = tail + swap(tail, mask)
        next_up = block(away - 1, source)
        next_down = None if last else block(1 - away, source)
        if last:
            next_down = jnp.zeros_like(next_up)

    tail = tail[0]
    mod_rows = jnp.take(
        mod_rows, jnp.bitwise_xor(data_me, jnp.arange(data_count, dtype=jnp.int32)), axis=0
    )
    class_rows = mod_rows[:, mod_here].astype(jnp.int32)
    mod_rows = mod_rows[:, :mod_here]
    cond_terms = lax.dot_general(
        mod_rows, ada_weight.astype(F32), (((1,), (1,)), ((), ())), precision=HIGH
    )
    cond_sums = head_sum_far(cond_terms)
    got_up, got_down, cond_sums, next_up = lax.optimization_barrier(
        (got_up, got_down, cond_sums, next_up)
    )
    ring_total = next_up + got_up.astype(F32) + got_down.astype(F32)
    grad_normed_one, first_mine = ring_total[:local], ring_total[local:].astype(BF16)
    cond_sums = head_sum_near(cond_sums)
    qkv_weight_grad = (
        jnp.transpose(qkv_grad.reshape(3, heads, HD, width), (1, 0, 2, 3))
        .reshape(3 * feats, width)
        .astype(F32)
        .T
    )
    bias_sums = tail[: 3 * feats].reshape(3, heads, HD)
    qv_bias_grad = jnp.stack([bias_sums[0], bias_sums[2]], 1).reshape(-1)
    qk_scale_grad = tail[3 * feats : 3 * feats + heads]
    tail = tail[3 * feats + heads :]
    code_hist = tail[:CODES].astype(jnp.int32)
    fc2_bias_grad = tail[CODES : CODES + width]
    proj_bias_grad = tail[CODES + width : CODES + 2 * width]
    fc1_bias_grad = lax.dynamic_slice_in_dim(
        tail[CODES + 2 * width :], me * hidden_here, hidden_here, 0
    )

    input_grad = (
        grad_resid + norm_back(unit_one, recip_one, grad_normed_one * (1.0 + scale_one))
    ).astype(BF16)
    fc2_mine = {t: fc2_mine[t // 2].astype(F32) for t in fc2_kept}
    fc2_weight_grad = share(fold(fc2_mine).astype(BF16)).reshape(-1, width)
    first_grad = share(first_mine)
    fc1_weight_grad = first_grad[:, :hidden_part].reshape(-1, width).T
    proj_weight_grad = first_grad[:, hidden_part:].reshape(-1, width)

    cond_rows = jnp.take(class_table, class_rows, axis=0).astype(F32)
    act_rows = jax.nn.silu(cond_rows).astype(BF16).astype(F32)
    ada_weight_grad = lax.dot_general(
        act_rows, mod_rows, (((0,), (0,)), ((), ())), precision=HIGH
    )
    ada_bias_grad = jnp.sum(mod_rows, 0)
    _, silu_pull = jax.vjp(jax.nn.silu, cond_rows)
    grad_rows = silu_pull(cond_sums)[0]
    class_range = jnp.arange(class_table.shape[0], dtype=jnp.int32)
    class_table_grad = jnp.zeros(class_table.shape, F32)
    for row in range(data_count):
        hit = class_range[:, None] == class_rows[row]
        class_table_grad = class_table_grad + jnp.where(hit, grad_rows[row][None, :], 0.0)
    return (
        block_output[None],
        input_grad[None],
        class_table_grad,
        ada_weight_grad,
        ada_bias_grad,
        qkv_weight_grad,
        qv_bias_grad,
        qk_scale_grad,
        proj_weight_grad,
        proj_bias_grad,
        fc1_weight_grad,
        fc1_bias_grad,
        fc2_weight_grad,
        fc2_bias_grad,
        code_hist,
    )


def solution(mesh):
    placed = (
        P("dp", "head", None),
        P("dp", None),
        P("dp", None),
        P("dp"),
        P("dp", "head"),
        P("dp", "head", None),
        P(),
        P(None, "head"),
        P("head"),
        P(None, "head"),
        P("head"),
        P("head"),
        P("head", None),
        P(),
        P(None, "head"),
        P("head"),
        P("head", None),
        P(),
    )
    return jax.shard_map(
        shards,
        mesh=mesh,
        in_specs=placed,
        out_specs=(
            P("dp", "head", None),
            P("dp", "head", None),
            P(),
            P(None, "head"),
            P("head"),
            P(None, "head"),
            P("head"),
            P("head"),
            P("head", None),
            P(),
            P(None, "head"),
            P("head"),
            P("head", None),
            P(),
            P(),
        ),
        check_vma=False,
    )
```

```python
import functools

import jax
import jax.numpy as jnp
from jax import lax
from jax.experimental import pallas as pl
from jax.experimental.pallas import tpu as pltpu
from jax.sharding import PartitionSpec as P

HD = 64
CODES = 4096
BLK = 256
FORWARD_BLOCK = (512, 512)
BACKWARD_BLOCK = (256, 512)
EPS_NORM = 1e-06
HIGH = lax.Precision.HIGHEST
GELU_ROOT = (2.0 / 3.141592653589793) ** 0.5
GELU_CUBE = 0.044715
F32 = jnp.float32
BF16 = jnp.bfloat16
BIG_LEN = 2240
BIG_CUMS = (1, 5, 14, 30, 66, 147, 316, 640, 1216, 2240)
SMALL_CUMS = (1, 5, 14, 30, 55, 91, 155, 255, 424, 680)


def normalize(values):
    mean_val = jnp.mean(values, -1, keepdims=True)
    centered = values - mean_val
    variance = jnp.mean(centered * centered, -1, keepdims=True)
    recip = lax.rsqrt(variance + EPS_NORM)
    return (centered * recip, recip)


def norm_back(unit, recip, upstream):
    mean_up = jnp.mean(upstream, -1, keepdims=True)
    mean_cross = jnp.mean(upstream * unit, -1, keepdims=True)
    return recip * (upstream - mean_up - unit * mean_cross)


def dot(left, right, left_dim, right_dim):
    return lax.dot_general(
        left, right, (((left_dim,), (right_dim,)), ((), ())), preferred_element_type=F32
    )


def head_pad(part, head, heads):
    pieces = [part if other == head else jnp.zeros_like(part) for other in range(heads)]
    return pieces[0] if heads == 1 else jnp.concatenate(pieces, 0)


def unit_rows(raw):
    recip = lax.rsqrt(jnp.sum(raw * raw, 0, keepdims=True) + EPS_NORM)
    return raw * recip, recip


def interval(places, lengths_ref, slots):
    first, second, third = lengths_ref[0], lengths_ref[1], lengths_ref[2]
    end_one, end_two = first + second, first + second + third
    low = jnp.where(places >= end_one, end_one, jnp.where(places >= first, first, 0))
    size = jnp.where(places >= end_one, third, jnp.where(places >= first, second, first))
    big, offset = size == BIG_LEN, places - low
    reach = jnp.where(big, BIG_CUMS[0], SMALL_CUMS[0])
    for level in range(1, len(BIG_CUMS)):
        passed = offset >= jnp.where(big, BIG_CUMS[level - 1], SMALL_CUMS[level - 1])
        reach = jnp.where(passed, jnp.where(big, BIG_CUMS[level], SMALL_CUMS[level]), reach)
    padding = places >= end_two
    return jnp.where(padding, end_two, low), jnp.where(padding, slots, low + reach)


def key_spans(step, lengths_ref, slots, rows_q, rows_k):
    first_low, first_high = interval(step * rows_q, lengths_ref, slots)
    last_low, last_high = interval(step * rows_q + rows_q - 1, lengths_ref, slots)
    first = lax.div(first_low, rows_k)
    last = lax.div(last_high + rows_k - 1, rows_k)
    full_first = jnp.minimum(lax.div(last_low + rows_k - 1, rows_k), last)
    full_last = jnp.maximum(lax.div(first_high, rows_k), full_first)
    rows = interval(
        step * rows_q + lax.broadcasted_iota(jnp.int32, (1, rows_q), 1), lengths_ref, slots
    )
    return (first, full_first, full_last, last), rows


def key_loops(spans, body, carry):
    first, full_first, full_last, last = spans
    carry = lax.fori_loop(first, full_first, functools.partial(body, True), carry)
    carry = lax.fori_loop(full_first, full_last, functools.partial(body, False), carry)
    return lax.fori_loop(full_last, last, functools.partial(body, True), carry)


def allowed_block(block, rows_k, low_row, high_row):
    places = block * rows_k + lax.broadcasted_iota(jnp.int32, (rows_k, low_row.shape[1]), 0)
    return (places >= low_row) & (places < high_row)


def project_kernel(
    heads, place_ref, scale_ref, piece_ref, weight_ref, mod_ref, bias_ref, *refs
):
    width = heads * HD
    raw_ref, query_ref, key_ref, keyt_ref, value_ref, valuet_ref, unit_ref = refs[-7:]
    piece = piece_ref[...]
    unit_ref[...] = piece
    normed = (piece.astype(F32) * (1.0 + mod_ref[1:2, :]) + mod_ref[0:1, :]).astype(BF16)
    raw = dot(weight_ref[...], normed, 1, 1) + bias_ref[...]
    raw_ref[...] = raw
    for head in range(heads):
        part = slice(head * HD, (head + 1) * HD)
        unit, _ = unit_rows(raw[part])
        query_ref[part, :] = (unit * scale_ref[head]).astype(BF16)
    keys = [unit_rows(raw[width + head * HD : width + (head + 1) * HD])[0] for head in range(heads)]
    keys = keys[0] if heads == 1 else jnp.concatenate(keys, 0)
    values = raw[2 * width :]
    keyt_ref[...] = keys.astype(BF16)
    key_ref[...] = jnp.transpose(keys).astype(BF16)
    valuet_ref[...] = values.astype(BF16)
    value_ref[...] = jnp.transpose(values).astype(BF16)


def project(place, piece, weight, mod, bias, scales, held, heads, slots):
    width, local, depth = heads * HD, piece.shape[0], piece.shape[1]

    def fixed(shape):
        return pl.BlockSpec(shape, lambda step, *_: (0, 0))

    def columns(rows):
        return pl.BlockSpec((rows, local), lambda step, place, scales: (0, place[0]))

    def lines(cols):
        return pl.BlockSpec((local, cols), lambda step, place, scales: (place[0], 0))

    shapes = [
        jax.ShapeDtypeStruct((3 * width, slots), F32),
        jax.ShapeDtypeStruct((width, slots), BF16),
        jax.ShapeDtypeStruct((slots, width), BF16),
        jax.ShapeDtypeStruct((width, slots), BF16),
        jax.ShapeDtypeStruct((slots, width), BF16),
        jax.ShapeDtypeStruct((width, slots), BF16),
        jax.ShapeDtypeStruct((slots, depth), BF16),
    ]
    held = list(held)
    return pl.pallas_call(
        functools.partial(project_kernel, heads),
        grid_spec=pltpu.PrefetchScalarGridSpec(
            num_scalar_prefetch=2,
            grid=(1,),
            in_specs=[
                fixed((local, depth)),
                fixed((3 * width, depth)),
                fixed((2, depth)),
                fixed((3 * width, 1)),
            ]
            + [pl.BlockSpec(memory_space=pl.ANY)] * len(held),
            out_specs=[
                columns(3 * width),
                columns(width),
                lines(width),
                columns(width),
                lines(width),
                columns(width),
                lines(depth),
            ],
        ),
        out_shape=shapes,
        input_output_aliases={6 + i: i for i in range(len(held))},
        compiler_params=pltpu.CompilerParams(vmem_limit_bytes=40 * 2**20),
        cost_estimate=pl.CostEstimate(
            flops=2 * 3 * width * local * depth, bytes_accessed=8 * 2**20, transcendentals=0
        ),
        name="project",
    )(place, scales, piece, weight, mod, bias, *held)


def forward_kernel(heads, rows_k, lengths_ref, query_ref, key_ref, valuet_ref, out_ref, lse_ref):
    step = pl.program_id(0)
    slots, rows_q = key_ref.shape[0], query_ref.shape[1]
    queries = [
        head_pad(query_ref[head * HD : (head + 1) * HD, :], head, heads) for head in range(heads)
    ]
    spans, (low_row, high_row) = key_spans(step, lengths_ref, slots, rows_q, rows_k)

    def body(masked, block, carry):
        rows = pl.ds(pl.multiple_of(block * rows_k, rows_k), rows_k)
        keys = key_ref[rows, :]
        if masked:
            allowed = allowed_block(block, rows_k, low_row, high_row)
        result = []
        for head in range(heads):
            total, acc = carry[head]
            probs = jnp.exp(dot(keys, queries[head], 1, 0))
            if masked:
                probs = jnp.where(allowed, probs, 0.0)
            total = total + jnp.sum(probs.reshape(rows_k // 8, 8, rows_q), 0)
            acc = acc + dot(
                valuet_ref[head * HD : (head + 1) * HD, rows], probs.astype(BF16), 1, 0
            )
            result.append((total, acc))
        return tuple(result)

    start = tuple(
        (jnp.zeros((8, rows_q), F32), jnp.zeros((HD, rows_q), F32)) for _ in range(heads)
    )
    final = key_loops(spans, body, start)
    for head in range(heads):
        total, acc = final[head]
        denom = jnp.sum(total, 0, keepdims=True)
        out_ref[head * HD : (head + 1) * HD, :] = (acc / denom).astype(BF16)
        lse_ref[head : head + 1, :] = jnp.log(denom)


def backward_kernel(
    heads,
    rows_k,
    lengths_ref,
    scale_ref,
    raw_ref,
    query_ref,
    key_ref,
    keyt_ref,
    value_ref,
    lse_ref,
    up_ref,
    grad_ref,
    qsum_ref,
    gkey_s,
    gvalue_s,
    probs_s,
    gprobs_s,
):
    step = pl.program_id(0)
    width = heads * HD
    slots, rows_q = raw_ref.shape[1], query_ref.shape[1]

    @pl.when(step == 0)
    def _():
        gkey_s[...] = jnp.zeros_like(gkey_s)
        gvalue_s[...] = jnp.zeros_like(gvalue_s)

    queries, query_rows, ups, up_rows, lses = [], [], [], [], []
    for head in range(heads):
        part = slice(head * HD, (head + 1) * HD)
        padded = head_pad(query_ref[part, :], head, heads)
        queries.append(padded)
        query_rows.append(jnp.transpose(padded.astype(F32)).astype(BF16))
        padded = head_pad(up_ref[part, :], head, heads)
        ups.append(padded)
        up_rows.append(jnp.transpose(padded.astype(F32)).astype(BF16))
        lses.append(lse_ref[head : head + 1, :])
    spans, (low_row, high_row) = key_spans(step, lengths_ref, slots, rows_q, rows_k)

    def first(masked, block, carry):
        rows = pl.ds(pl.multiple_of(block * rows_k, rows_k), rows_k)
        keys, values = key_ref[rows, :], value_ref[rows, :]
        if masked:
            allowed = allowed_block(block, rows_k, low_row, high_row)
        result = []
        for head in range(heads):
            probs = jnp.exp(dot(keys, queries[head], 1, 0) - lses[head])
            if masked:
                probs = jnp.where(allowed, probs, 0.0)
            grad_probs = dot(values, ups[head], 1, 0)
            probs_s[head, rows, :] = probs
            gprobs_s[head, rows, :] = grad_probs
            terms = (probs * grad_probs).reshape(rows_k // 8, 8, rows_q)
            result.append(carry[head] + jnp.sum(terms, 0))
        return tuple(result)

    deltas = key_loops(spans, first, tuple(jnp.zeros((8, rows_q), F32) for _ in range(heads)))
    deltas = [jnp.sum(delta, 0, keepdims=True) for delta in deltas]

    def second(block, carry):
        rows = pl.ds(pl.multiple_of(block * rows_k, rows_k), rows_k)
        result = []
        gkey, gvalue = gkey_s[rows, :], gvalue_s[rows, :]
        for head in range(heads):
            probs = probs_s[head, rows, :]
            grad_scores = (probs * (gprobs_s[head, rows, :] - deltas[head])).astype(BF16)
            gvalue = gvalue + dot(probs.astype(BF16), up_rows[head], 1, 0)
            gkey = gkey + dot(grad_scores, query_rows[head], 1, 0)
            keyt = keyt_ref[head * HD : (head + 1) * HD, rows]
            result.append(carry[head] + dot(keyt, grad_scores, 1, 0))
        gkey_s[rows, :] = gkey
        gvalue_s[rows, :] = gvalue
        return tuple(result)

    start = tuple(jnp.zeros((HD, rows_q), F32) for _ in range(heads))
    final = lax.fori_loop(spans[0], spans[3], second, start)
    cols = pl.ds(pl.multiple_of(step * rows_q, rows_q), rows_q)
    for head in range(heads):
        part = slice(head * HD, (head + 1) * HD)
        grad = final[head]
        unit, recip = unit_rows(raw_ref[part, cols])
        qsum_ref[head : head + 1, :] = jnp.sum(grad * unit, 0, keepdims=True)
        scaled = scale_ref[head] * grad
        back = recip * (scaled - unit * jnp.sum(scaled * unit, 0, keepdims=True))
        grad_ref[part, cols] = back.astype(BF16)

    @pl.when(step == pl.num_programs(0) - 1)
    def _():
        def finish(block, carry):
            cols = pl.ds(pl.multiple_of(block * BLK, BLK), BLK)
            gkey = jnp.transpose(gkey_s[cols, :])
            for head in range(heads):
                part = slice(width + head * HD, width + (head + 1) * HD)
                unit, recip = unit_rows(raw_ref[part, cols])
                grad = gkey[head * HD : (head + 1) * HD, :]
                back = recip * (grad - unit * jnp.sum(grad * unit, 0, keepdims=True))
                grad_ref[part, cols] = back.astype(BF16)
            grad_ref[2 * width :, cols] = jnp.transpose(gvalue_s[cols, :]).astype(BF16)
            return carry

        lax.fori_loop(0, slots // BLK, finish, 0)


def whole_spec(shape):
    return pl.BlockSpec(shape, lambda step, *_: (0,) * len(shape))


def column_spec(rows, cols):
    return pl.BlockSpec((rows, cols), lambda step, *_: (0, step))


def attention_forward(query, key, valuet, lengths, heads):
    width, slots = query.shape
    rows_q, rows_k = FORWARD_BLOCK
    return pl.pallas_call(
        functools.partial(forward_kernel, heads, rows_k),
        grid_spec=pltpu.PrefetchScalarGridSpec(
            num_scalar_prefetch=1,
            grid=(slots // rows_q,),
            in_specs=[column_spec(width, rows_q), whole_spec(key.shape), whole_spec(valuet.shape)],
            out_specs=[column_spec(width, rows_q), column_spec(heads, rows_q)],
        ),
        out_shape=[
            jax.ShapeDtypeStruct((width, slots), BF16),
            jax.ShapeDtypeStruct((heads, slots), F32),
        ],
        compiler_params=pltpu.CompilerParams(
            dimension_semantics=("arbitrary",), vmem_limit_bytes=32 * 2**20
        ),
        cost_estimate=pl.CostEstimate(
            flops=heads * slots * slots * 1000, bytes_accessed=4 * 2**20, transcendentals=0
        ),
        name="attend",
    )(lengths, query, key, valuet)


def attention_backward(raw, query, key, keyt, value, lse, up, lengths, scales, heads):
    width, slots = query.shape
    rows_q, rows_k = BACKWARD_BLOCK
    return pl.pallas_call(
        functools.partial(backward_kernel, heads, rows_k),
        grid_spec=pltpu.PrefetchScalarGridSpec(
            num_scalar_prefetch=2,
            grid=(slots // rows_q,),
            in_specs=[
                whole_spec(raw.shape),
                column_spec(width, rows_q),
                whole_spec(key.shape),
                whole_spec(keyt.shape),
                whole_spec(value.shape),
                column_spec(heads, rows_q),
                column_spec(width, rows_q),
            ],
            out_specs=[whole_spec(raw.shape), column_spec(heads, rows_q)],
            scratch_shapes=[
                pltpu.VMEM((slots, width), F32),
                pltpu.VMEM((slots, width), F32),
                pltpu.VMEM((heads, slots, rows_q), F32),
                pltpu.VMEM((heads, slots, rows_q), F32),
            ],
        ),
        out_shape=[
            jax.ShapeDtypeStruct(raw.shape, BF16),
            jax.ShapeDtypeStruct((heads, slots), F32),
        ],
        compiler_params=pltpu.CompilerParams(
            dimension_semantics=("arbitrary",), vmem_limit_bytes=56 * 2**20
        ),
        cost_estimate=pl.CostEstimate(
            flops=heads * slots * slots * 2000, bytes_accessed=14 * 2**20, transcendentals=0
        ),
        name="attend_back",
    )(lengths, scales, raw, query, key, keyt, value, lse, up)


def mlp_kernel(
    rows,
    part_ref,
    normed_ref,
    up_ref,
    first_ref,
    second_ref,
    bias_ref,
    sent_one_ref,
    kept_one_ref,
    sent_two_ref,
    kept_two_ref,
    bias_grad_ref,
    branch_ref,
    grad_ref,
):
    part, step = pl.program_id(0), pl.program_id(1)
    start = (part == 0) & (step == 0)
    group = first_ref.shape[0]
    normed, up = normed_ref[...], up_ref[...]
    first = first_ref[:, :rows, :].reshape(group * rows, first_ref.shape[2])
    second = second_ref[...]
    pre = dot(normed, first, 1, 1) + bias_ref[...]
    grad_hidden = dot(up, second, 1, 1)
    square = pre * pre
    angle = jnp.tanh(GELU_ROOT * pre * (1.0 + GELU_CUBE * square))
    half = 0.5 * (1.0 + angle)
    slope = half + 0.5 * pre * (1.0 - angle * angle) * GELU_ROOT * (1.0 + 3.0 * GELU_CUBE * square)
    hidden = (pre * half).astype(BF16)
    grad_pre = (slope * grad_hidden).astype(BF16)
    bias_grad_ref[...] = jnp.sum(grad_pre.astype(F32), 0, keepdims=True)
    branch = dot(hidden, second, 1, 0)
    grad = dot(grad_pre, first, 1, 0)

    @pl.when(start)
    def _():
        branch_ref[...] = branch
        grad_ref[...] = grad

    @pl.when(jnp.logical_not(start))
    def _():
        branch_ref[...] += branch
        grad_ref[...] += grad

    one = dot(grad_pre, normed, 0, 0).astype(BF16).reshape(kept_one_ref.shape)
    two = dot(hidden, up, 0, 0).astype(BF16).reshape(kept_two_ref.shape)
    sending = part < pl.num_programs(0) // 2

    @pl.when(sending)
    def _():
        sent_one_ref[...] = one
        sent_two_ref[...] = two

    @pl.when(jnp.logical_not(sending))
    def _():
        kept_one_ref[...] = one
        kept_two_ref[...] = two


def mlp(parts, normed, up, first, second, bias, heads_all, rows):
    local, width = normed.shape
    total = parts.shape[0]
    group = max(4, 128 // rows)
    steps = heads_all // group
    cols = group * rows
    full_rows = first.shape[1]
    half = total // 2

    def fixed(p, j, part):
        return (0, 0)

    def sent(p, j, part):
        flat = jnp.minimum(p * steps + j, half * steps - 1)
        return (flat // steps, flat % steps, 0, 0)

    def kept(p, j, part):
        flat = jnp.maximum(p * steps + j - half * steps, 0)
        return (flat // steps, flat % steps, 0, 0)

    grads = jax.ShapeDtypeStruct((half, heads_all, rows, width), BF16)
    return pl.pallas_call(
        functools.partial(mlp_kernel, rows),
        grid_spec=pltpu.PrefetchScalarGridSpec(
            num_scalar_prefetch=1,
            grid=(total, steps),
            in_specs=[
                pl.BlockSpec((local, width), fixed),
                pl.BlockSpec((local, width), fixed),
                pl.BlockSpec((group, full_rows, width), lambda p, j, part: (part[p] * steps + j, 0, 0)),
                pl.BlockSpec((cols, width), lambda p, j, part: (part[p] * steps + j, 0)),
                pl.BlockSpec((1, cols), lambda p, j, part: (0, part[p] * steps + j)),
            ],
            out_specs=[
                pl.BlockSpec((1, group, rows, width), sent),
                pl.BlockSpec((1, group, rows, width), kept),
                pl.BlockSpec((1, group, rows, width), sent),
                pl.BlockSpec((1, group, rows, width), kept),
                pl.BlockSpec((1, cols), lambda p, j, part: (0, part[p] * steps + j)),
                pl.BlockSpec((local, width), fixed),
                pl.BlockSpec((local, width), fixed),
            ],
        ),
        out_shape=[
            grads,
            grads,
            grads,
            grads,
            jax.ShapeDtypeStruct((1, total * heads_all * rows), F32),
            jax.ShapeDtypeStruct((local, width), F32),
            jax.ShapeDtypeStruct((local, width), F32),
        ],
        compiler_params=pltpu.CompilerParams(
            dimension_semantics=("arbitrary", "arbitrary"), vmem_limit_bytes=52 * 2**20
        ),
        cost_estimate=pl.CostEstimate(
            flops=12 * local * width * total * heads_all * rows,
            bytes_accessed=40 * 2**20,
            transcendentals=0,
        ),
        name="mlp",
    )(parts, normed, up, first, second, bias)


def ring_blocks_kernel(
    halves, place_ref, grad_ref, weight_ref, one_ref, two_ref, three_ref, four_ref, *out_refs
):
    terms = dot(grad_ref[...], weight_ref[...], 0, 0).astype(BF16)
    rest = (one_ref[0].astype(F32) + two_ref[0].astype(F32)).astype(BF16)
    last = (three_ref[0].astype(F32) + four_ref[0].astype(F32)).astype(BF16)
    rest = jnp.concatenate([rest, last], 0)
    local = terms.shape[0]
    if halves:
        half = out_refs[0].shape[0]
        out_refs[0][...] = terms[:half]
        out_refs[1][: local - half, :] = terms[half:]
        out_refs[1][local - half :, :] = rest
    else:
        out_refs[0][0, :local, :] = terms
        out_refs[0][0, local:, :] = rest


def ring_blocks(places, grad, weight, pairs, local, halves):
    depth, width = weight.shape
    total = local + pairs[0].shape[1] + pairs[2].shape[1]
    if halves:
        sizes = [total // 2, total - total // 2]
        out_specs = [pl.BlockSpec((size, width), lambda step, place: (0, 0)) for size in sizes]
        out_shape = [jax.ShapeDtypeStruct((size, width), BF16) for size in sizes]
    else:
        out_specs = pl.BlockSpec((1, total, width), lambda step, place: (step, 0, 0))
        out_shape = jax.ShapeDtypeStruct((places.shape[0], total, width), BF16)
    return pl.pallas_call(
        functools.partial(ring_blocks_kernel, halves),
        grid_spec=pltpu.PrefetchScalarGridSpec(
            num_scalar_prefetch=1,
            grid=(places.shape[0],),
            in_specs=[
                pl.BlockSpec((depth, local), lambda step, place: (0, place[step])),
                pl.BlockSpec((depth, width), lambda step, place: (0, 0)),
            ]
            + [
                pl.BlockSpec((1, pair.shape[1], width), lambda step, place: (place[step], 0, 0))
                for pair in pairs
            ],
            out_specs=out_specs,
        ),
        out_shape=out_shape,
        compiler_params=pltpu.CompilerParams(vmem_limit_bytes=40 * 2**20),
        cost_estimate=pl.CostEstimate(flops=1, bytes_accessed=1, transcendentals=0),
        name="ring_blocks",
    )(places, grad, weight, *pairs)


def finish_kernel(rows, order_ref, value_ref, first_ref, second_ref):
    value = value_ref[0].astype(F32)
    first_ref[...] = jnp.transpose(value[:rows])
    second_ref[...] = value[rows:]


def finish_weights(order, value, rows):
    total, full_rows, width = value.shape
    return pl.pallas_call(
        functools.partial(finish_kernel, rows),
        grid_spec=pltpu.PrefetchScalarGridSpec(
            num_scalar_prefetch=1,
            grid=(total,),
            in_specs=[pl.BlockSpec((1, full_rows, width), lambda step, order: (order[step], 0, 0))],
            out_specs=[
                pl.BlockSpec((width, rows), lambda step, order: (0, step)),
                pl.BlockSpec((full_rows - rows, width), lambda step, order: (step, 0)),
            ],
        ),
        out_shape=[
            jax.ShapeDtypeStruct((width, total * rows), F32),
            jax.ShapeDtypeStruct((total * (full_rows - rows), width), F32),
        ],
        name="finish_weights",
    )(order, value)


def after(value, *others):
    return lax.optimization_barrier((value, *others))[0]


def shards(
    block_input,
    lengths,
    scale_ids,
    class_ids,
    code_ids,
    cotangent,
    class_table,
    ada_weight,
    ada_bias,
    qkv_weight,
    qv_bias,
    qk_scale,
    proj_weight,
    proj_bias,
    fc1_weight,
    fc1_bias,
    fc2_weight,
    fc2_bias,
):
    count, data_count = lax.axis_size("head"), lax.axis_size("dp")
    me, data_me = lax.axis_index("head"), lax.axis_index("dp")
    _, local, width = block_input.shape
    slots = local * count
    heads = qk_scale.shape[0]
    feats = heads * HD
    hidden_here = fc1_weight.shape[1]
    data_masks = [1 << bit for bit in range(data_count.bit_length() - 1)]
    both_axes = ("dp", "head")

    ring = list(range(0, count, 2)) + list(range(count - 1, 0, -2))
    half_count = count // 2
    offsets = [0]
    for away in range(1, half_count):
        offsets += [away, -away]
    offsets.append(half_count)
    my_pos = jnp.where(me % 2 == 0, me // 2, count - 1 - me // 2)

    def at(away):
        pos = (my_pos + away + count) % count
        return jnp.where(pos < half_count, 2 * pos, 2 * (count - 1 - pos) + 1)

    def rot(value, away):
        pairs = [(ring[(i + away) % count], ring[i]) for i in range(count)]
        return lax.ppermute(value, "head", pairs)

    def swap(value, mask):
        return lax.ppermute(value, "dp", [(i, i ^ mask) for i in range(data_count)])

    def xor_head(value, mask):
        return lax.ppermute(value, "head", [(i, i ^ mask) for i in range(count)])

    def head_sum_far(value):
        total = value
        for mask in range(2, count, 2):
            total = total + xor_head(value, mask)
        return total

    def head_sum_near(value):
        return value + xor_head(value, 1)

    inputs_full = block_input[0].astype(F32)
    unit_one, recip_one = normalize(inputs_full)
    unit_low = unit_one.astype(BF16)

    hidden_part, feat_part = hidden_here // data_count, feats // data_count
    fc1_part = lax.dynamic_slice(fc1_weight, (0, data_me * hidden_part), (width, hidden_part)).T
    proj_part = lax.dynamic_slice(proj_weight, (data_me * feat_part, 0), (feat_part, width))
    fc2_part = lax.dynamic_slice(fc2_weight, (data_me * hidden_part, 0), (hidden_part, width))
    first_full = lax.all_gather(
        jnp.concatenate([fc1_part, proj_part], 0), both_axes, axis=0, tiled=False
    )
    fc2_full = lax.all_gather(fc2_part, both_axes, axis=0, tiled=True)
    proj_full = first_full[:, hidden_part:].reshape(data_count, count, feat_part, width)
    proj_full = jnp.transpose(proj_full, (1, 0, 2, 3)).reshape(-1, width)

    cond = jnp.take(class_table, class_ids, axis=0).astype(F32)
    act = jax.nn.silu(cond).astype(BF16)
    mod_local = jnp.dot(act, ada_weight, preferred_element_type=F32)[0] + ada_bias.astype(F32)
    small = jnp.concatenate([mod_local, fc1_bias.astype(F32)])[None, :]
    pieces = [small] + [xor_head(small, mask) for mask in range(2, count, 2)]
    units = {0: unit_low, 1: rot(unit_low, 1), -1: rot(unit_low, -1)}
    units[1], units[-1], pieces = lax.optimization_barrier((units[1], units[-1], pieces))
    pieces = jnp.concatenate(pieces, 0)
    if half_count > 2:
        units[2], units[-2] = rot(units[1], 1), rot(units[-1], -1)
    small_all = jnp.stack([pieces, xor_head(pieces, 1)], 1).reshape(count, -1)
    if half_count > 2:
        units[2], units[-2], small_all = lax.optimization_barrier(
            (units[2], units[-2], small_all)
        )
    small_all = jnp.take(
        small_all, jnp.bitwise_xor(me, jnp.arange(count, dtype=jnp.int32)), axis=0
    )
    mod_here = mod_local.shape[0]
    modulation = small_all[:, :mod_here].reshape(6, width)
    shift_one, scale_one, gate_one, shift_two, scale_two, gate_two = [
        modulation[i : i + 1] for i in range(6)
    ]
    bias_full = small_all[:, mod_here:].reshape(count, data_count, hidden_part)
    bias_full = jnp.transpose(bias_full, (1, 0, 2)).reshape(1, -1)

    qkv_rows = jnp.transpose(
        after(qkv_weight, small_all).T.reshape(heads, 3, HD, width), (1, 0, 2, 3)
    ).reshape(3 * feats, width)
    bias_pair = qv_bias.astype(F32).reshape(heads, 2, HD)
    qkv_bias = jnp.stack([bias_pair[:, 0], jnp.zeros_like(bias_pair[:, 0]), bias_pair[:, 1]], 0)
    qkv_bias = qkv_bias.reshape(3 * feats, 1)
    scale_exp = jnp.exp(qk_scale)

    def put(held, away):
        place = at(away).astype(jnp.int32)[None]
        return project(
            place, units[away], qkv_rows, modulation[:2], qkv_bias, scale_exp, held, heads, slots
        )

    for away in range(3, half_count):
        units[away], units[-away] = rot(units[away - 1], 1), rot(units[1 - away], -1)
    held = put([], 0)
    for away in range(1, half_count - 1):
        held = put(put(held, away), -away)
        if away == 1:
            last, units[half_count - 1], units[1 - half_count] = lax.optimization_barrier(
                (held[1], units[half_count - 1], units[1 - half_count])
            )
            held = [held[0], last] + list(held[2:])
            proj_full, units[half_count - 1] = lax.optimization_barrier(
                (proj_full, units[half_count - 1])
            )
    half = local // 2
    ends = [
        rot(units[half_count - 1][:half], 1),
        rot(units[1 - half_count][half:], -1),
    ]
    held = put(put(held, half_count - 1), 1 - half_count)
    units[half_count] = jnp.concatenate(ends, 0)
    held = put(held, half_count)
    raw, query, key, keyt, value, valuet, unit_all = held
    out_low, lse = attention_forward(query, key, valuet, lengths[0], heads)

    attended = jnp.zeros((feats * count, local), BF16)
    for away in offsets:
        piece = lax.dynamic_slice(out_low, (0, at(-away) * local), (feats, local))
        piece = piece if away == 0 else rot(piece, away)
        attended = lax.dynamic_update_slice(attended, piece, (at(away) * feats, 0))
    cot_full = cotangent[0].astype(F32)
    grad_mlp = (cot_full * gate_two).astype(BF16)
    attn_branch = dot(attended, proj_full, 0, 0) + proj_bias.astype(F32)
    resid = inputs_full + gate_one * attn_branch
    unit_two, recip_two = normalize(resid)
    normed_two = (unit_two * (1.0 + scale_two) + shift_two).astype(BF16)

    kept_t = list(range(0, data_count, 2))
    all_t = [t + 1 for t in kept_t] + kept_t
    parts = jnp.bitwise_xor(data_me, jnp.array(all_t, jnp.int32))
    sent_one, kept_one, sent_two, kept_two, fc1_bias_sum, mlp_branch, grad_normed_two = mlp(
        parts, normed_two, grad_mlp, first_full, fc2_full, bias_full, count, hidden_part
    )
    grad_shift_two = jnp.sum(grad_normed_two, 0)
    grad_scale_two = jnp.sum(grad_normed_two * unit_two, 0)
    grad_resid = cot_full + norm_back(unit_two, recip_two, grad_normed_two * (1.0 + scale_two))
    grad_attn = (grad_resid * gate_one).astype(BF16)
    grad_gate_one = jnp.sum(grad_resid * attn_branch, 0)
    grad_attended = dot(proj_full, grad_attn, 1, 1).astype(BF16)
    up_pieces = {}
    for away in offsets:
        piece = lax.dynamic_slice(grad_attended, (at(away) * feats, 0), (feats, local))
        up_pieces[away] = piece if away == 0 else rot(piece, -away)

    sent_one, sent_two = lax.optimization_barrier((sent_one, sent_two))
    got_one, got_two = swap(sent_one, 1), swap(sent_two, 1)

    def add(left, right):
        return (left.astype(F32) + right.astype(F32)).astype(BF16)

    def split_pair(kept):
        kept = {t: kept[i] for i, t in enumerate(kept_t)}
        for mask in data_masks[1:-1]:
            kept = {
                t: add(kept[t], swap(kept[t ^ mask], mask)) for t in kept if not t & mask
            }
        return kept[0], swap(kept[data_masks[-1]], data_masks[-1])

    kept_one = [add(kept_one[i], got_one[i]) for i in range(len(kept_t))]
    fc2_stack = jnp.stack([add(kept_two[i], got_two[i]) for i in range(len(kept_t))], 1)
    fc2_stack = fc2_stack.reshape(count, len(kept_t) * hidden_part, width)
    proj_grad = dot(attended, grad_attn, 1, 0).astype(BF16)
    proj_grad = proj_grad.reshape(count, data_count, feat_part, width)
    proj_parts = [
        lax.dynamic_index_in_dim(proj_grad, parts[i], 1, keepdims=False) for i in range(data_count)
    ]
    got_three = swap(jnp.stack(proj_parts[: len(kept_t)], 0), 1)
    kept_three = [add(proj_parts[len(kept_t) + i], got_three[i]) for i in range(len(kept_t))]
    mlp_branch = mlp_branch + fc2_bias.astype(F32)
    block_output = (resid + gate_two * mlp_branch).astype(BF16)
    grad_gate_two = jnp.sum(cot_full * mlp_branch, 0)

    up = jnp.zeros((feats, slots), BF16)
    for away in offsets:
        up = lax.dynamic_update_slice(up, up_pieces[away], (0, at(-away) * local))
    up, kept_one, kept_three, fc2_stack = lax.optimization_barrier(
        (up, kept_one, kept_three, fc2_stack)
    )
    fc2_mine = lax.psum_scatter(fc2_stack, "head", scatter_dimension=0, tiled=True)
    fc2_mine = fc2_mine.reshape(len(kept_t), hidden_part, width)

    one_here, one_got = split_pair(kept_one)
    three_here, three_got = split_pair(kept_three)

    def share(value):
        for mask in reversed(data_masks):
            value = jnp.stack([value, swap(value, mask)], 0)
        bits = len(data_masks)
        value = value.reshape((data_count,) + value.shape[bits:])
        table = [int(format(t, "b").zfill(bits)[::-1], 2) for t in range(data_count)]
        places = jnp.take(
            jnp.array(table, jnp.int32),
            jnp.bitwise_xor(data_me, jnp.arange(data_count, dtype=jnp.int32)),
        )
        return value, places

    fc2_bias_sum = jnp.sum(grad_mlp.astype(F32), 0)
    proj_bias_sum = jnp.sum(grad_attn.astype(F32), 0)
    valid = me * local + jnp.arange(local, dtype=jnp.int32) < jnp.sum(lengths[0])
    code_range = jnp.arange(CODES, dtype=jnp.int32)
    code_hits = (after(code_ids, units[1])[0][:, None] == code_range[None, :]) & valid[:, None]
    local_counts = jnp.sum(code_hits.astype(F32), 0)
    fc1_bias_sum = fc1_bias_sum.reshape(data_count, count, hidden_part)
    fc1_bias_sum = jnp.transpose(fc1_bias_sum, (1, 0, 2)).reshape(-1)
    early = jnp.concatenate(
        [
            local_counts,
            fc2_bias_sum,
            proj_bias_sum,
            fc1_bias_sum,
            grad_gate_one,
            grad_shift_two,
            grad_scale_two,
            grad_gate_two,
        ]
    )
    early, up = lax.optimization_barrier((early, up))
    early = head_sum_far(early[None, :])

    grad_raw, query_sums = attention_backward(
        raw, query, key, keyt, value, lse, up, lengths[0], scale_exp, heads
    )
    grad_raw, query_sums, one_got, three_got, early = lax.optimization_barrier(
        (grad_raw, query_sums, one_got, three_got, early)
    )
    pairs = [one_here, one_got, three_here, three_got]

    def send(ups, downs):
        return rot(ups, -1), rot(downs, 1)

    places = jnp.stack([at(away) for away in offsets]).astype(jnp.int32)
    far_up, far_down = ring_blocks(places[-1:], grad_raw, qkv_rows, pairs, local, True)
    got_up, got_down = send(far_up, far_down)
    half = far_up.shape[0]

    source, _ = lax.optimization_barrier((grad_raw, far_up))
    blocks = ring_blocks(places[:-1], source, qkv_rows, pairs, local, False)

    got_up, got_down, blocks, source = lax.optimization_barrier(
        (got_up, got_down, blocks, source)
    )
    blocks = {away: blocks[i] for i, away in enumerate(offsets[:-1])}
    near_up, near_down = blocks[half_count - 1], blocks[1 - half_count]
    ups = jnp.concatenate([add(near_up[:half], got_up), near_up[half:]], 0)
    downs = jnp.concatenate([near_down[:half], add(near_down[half:], got_down)], 0)
    ups, downs, source = lax.optimization_barrier((ups, downs, source))
    got_up, got_down = send(ups, downs)
    bias_sums = jnp.sum(source.astype(F32), 1)
    unit_grad = dot(source, unit_all, 1, 0)
    qkv_grad = unit_grad * (1.0 + scale_one) + bias_sums[:, None] * shift_one
    qkv_grad = qkv_grad.astype(BF16)
    scale_sums = scale_exp * jnp.sum(query_sums, 1)
    rows_float = qkv_rows.astype(F32)
    grad_shift_one = jnp.sum(rows_float * bias_sums[:, None], 0)
    grad_scale_one = jnp.sum(rows_float * unit_grad, 0)
    late = head_sum_far(jnp.concatenate([grad_shift_one, grad_scale_one])[None, :])
    over_rows = CODES + 2 * width + count * hidden_here

    for away in range(half_count - 2, 0, -1):
        got_up, got_down, late, qkv_grad = lax.optimization_barrier(
            (got_up, got_down, late, qkv_grad)
        )
        ups, downs = add(blocks[away], got_up), add(blocks[-away], got_down)
        ups, downs, late, early, qkv_grad, fc2_mine = lax.optimization_barrier(
            (ups, downs, late, early, qkv_grad, fc2_mine)
        )
        got_up, got_down = send(ups, downs)
        if away == half_count - 2:
            late = head_sum_near(jnp.concatenate([late, early], 1))
            for mask in data_masks:
                qkv_grad = add(qkv_grad, swap(qkv_grad, mask))
            fc2_pair = {t: fc2_mine[i].astype(F32) for i, t in enumerate(kept_t)}
            for mask in data_masks[1:]:
                fc2_pair = {
                    t: fc2_pair[t] + swap(fc2_pair[t ^ mask].astype(BF16), mask).astype(F32)
                    for t in fc2_pair
                    if not t & mask
                }
            fc2_mine = fc2_pair[0].astype(BF16)
        if away == 1:
            sums = late[0]
            mod_all = jnp.concatenate([sums[: 2 * width], sums[2 * width + over_rows :]])
            rows = jnp.concatenate(
                [
                    lax.dynamic_slice_in_dim(mod_all, me * mod_here, mod_here, 0),
                    class_ids.astype(F32),
                    bias_sums,
                    scale_sums,
                    sums[2 * width : 2 * width + over_rows],
                ]
            )[None, :]
            rows = jnp.concatenate(
                [rows] + [swap(rows, mask) for mask in range(1, data_count)], 0
            )
            rows = jnp.take(
                rows, jnp.bitwise_xor(data_me, jnp.arange(data_count, dtype=jnp.int32)), axis=0
            )
            class_rows = rows[:, mod_here].astype(jnp.int32)
            mod_rows = rows[:, :mod_here]
            tail = jnp.sum(rows[:, mod_here + 1 :], 0)
            cond_terms = lax.dot_general(
                mod_rows, ada_weight.astype(F32), (((1,), (1,)), ((), ())), precision=HIGH
            )
            cond_sums = head_sum_far(cond_terms)
            fc2_all, order = share(fc2_mine)
            fc2_weight_grad = jnp.take(fc2_all, order, axis=0).astype(F32).reshape(-1, width)

    qkv_weight_grad = (
        jnp.transpose(qkv_grad.reshape(3, heads, HD, width), (1, 0, 2, 3))
        .reshape(3 * feats, width)
        .astype(F32)
        .T
    )
    cond_rows = jnp.take(class_table, class_rows, axis=0).astype(F32)
    act_rows = jax.nn.silu(cond_rows).astype(BF16).astype(F32)
    ada_weight_grad = lax.dot_general(
        act_rows, mod_rows, (((0,), (0,)), ((), ())), precision=HIGH
    )
    ada_bias_grad = jnp.sum(mod_rows, 0)
    got_up, got_down, tail, cond_sums, qkv_weight_grad, ada_weight_grad, fc2_weight_grad = (
        lax.optimization_barrier(
            (got_up, got_down, tail, cond_sums, qkv_weight_grad, ada_weight_grad, fc2_weight_grad)
        )
    )
    ring_total = blocks[0].astype(F32) + got_up.astype(F32) + got_down.astype(F32)
    grad_normed_one, first_mine = ring_total[:local], ring_total[local:].astype(BF16)
    bias_sums = tail[: 3 * feats].reshape(3, heads, HD)
    qv_bias_grad = jnp.stack([bias_sums[0], bias_sums[2]], 1).reshape(-1)
    qk_scale_grad = tail[3 * feats : 3 * feats + heads]
    tail = tail[3 * feats + heads :]
    code_hist = tail[:CODES].astype(jnp.int32)
    fc2_bias_grad = tail[CODES : CODES + width]
    proj_bias_grad = tail[CODES + width : CODES + 2 * width]
    fc1_bias_grad = lax.dynamic_slice_in_dim(
        tail[CODES + 2 * width :], me * hidden_here, hidden_here, 0
    )

    input_grad = (
        grad_resid + norm_back(unit_one, recip_one, grad_normed_one * (1.0 + scale_one))
    ).astype(BF16)
    first_grad, order = share(first_mine)
    cond_sums = head_sum_near(cond_sums)
    _, silu_pull = jax.vjp(jax.nn.silu, cond_rows)
    grad_rows = silu_pull(cond_sums)[0]
    class_range = jnp.arange(class_table.shape[0], dtype=jnp.int32)
    class_table_grad = jnp.zeros(class_table.shape, F32)
    for row in range(data_count):
        hit = class_range[:, None] == class_rows[row]
        class_table_grad = class_table_grad + jnp.where(hit, grad_rows[row][None, :], 0.0)
    if hidden_part % 128 == 0:
        fc1_weight_grad, proj_weight_grad = finish_weights(order, first_grad, hidden_part)
    else:
        first_grad = jnp.take(first_grad, order, axis=0).astype(F32)
        fc1_weight_grad = first_grad[:, :hidden_part].reshape(-1, width).T
        proj_weight_grad = first_grad[:, hidden_part:].reshape(-1, width)

    return (
        block_output[None],
        input_grad[None],
        class_table_grad,
        ada_weight_grad,
        ada_bias_grad,
        qkv_weight_grad,
        qv_bias_grad,
        qk_scale_grad,
        proj_weight_grad,
        proj_bias_grad,
        fc1_weight_grad,
        fc1_bias_grad,
        fc2_weight_grad,
        fc2_bias_grad,
        code_hist,
    )


def solution(mesh):
    placed = (
        P("dp", "head", None),
        P("dp", None),
        P("dp", None),
        P("dp"),
        P("dp", "head"),
        P("dp", "head", None),
        P(),
        P(None, "head"),
        P("head"),
        P(None, "head"),
        P("head"),
        P("head"),
        P("head", None),
        P(),
        P(None, "head"),
        P("head"),
        P("head", None),
        P(),
    )
    return jax.shard_map(
        shards,
        mesh=mesh,
        in_specs=placed,
        out_specs=(
            P("dp", "head", None),
            P("dp", "head", None),
            P(),
            P(None, "head"),
            P("head"),
            P(None, "head"),
            P("head"),
            P("head"),
            P("head", None),
            P(),
            P(None, "head"),
            P("head"),
            P("head", None),
            P(),
            P(),
        ),
        check_vma=False,
    )
```

```python
import functools

import jax
import jax.numpy as jnp
from jax import lax
from jax.experimental import pallas as pl
from jax.experimental.pallas import tpu as pltpu
from jax.sharding import PartitionSpec as P

HD = 64
CODES = 4096
BLK = 256
FORWARD_BLOCK = (512, 512)
BACKWARD_BLOCK = (256, 512)
EPS_NORM = 1e-06
HIGH = lax.Precision.HIGHEST
GELU_ROOT = (2.0 / 3.141592653589793) ** 0.5
GELU_CUBE = 0.044715
GAIN_LEAST = 0.25
F32 = jnp.float32
BF16 = jnp.bfloat16
BIG_LEN = 2240
BIG_CUMS = (1, 5, 14, 30, 66, 147, 316, 640, 1216, 2240)
SMALL_CUMS = (1, 5, 14, 30, 55, 91, 155, 255, 424, 680)


def normalize(values):
    mean_val = jnp.mean(values, -1, keepdims=True)
    centered = values - mean_val
    variance = jnp.mean(centered * centered, -1, keepdims=True)
    recip = lax.rsqrt(variance + EPS_NORM)
    return (centered * recip, recip)


def norm_back(unit, recip, upstream):
    mean_up = jnp.mean(upstream, -1, keepdims=True)
    mean_cross = jnp.mean(upstream * unit, -1, keepdims=True)
    return recip * (upstream - mean_up - unit * mean_cross)


def dot(left, right, left_dim, right_dim):
    return lax.dot_general(
        left, right, (((left_dim,), (right_dim,)), ((), ())), preferred_element_type=F32
    )


def head_pad(part, head, heads):
    pieces = [part if other == head else jnp.zeros_like(part) for other in range(heads)]
    return pieces[0] if heads == 1 else jnp.concatenate(pieces, 0)


def unit_rows(raw):
    recip = lax.rsqrt(jnp.sum(raw * raw, 0, keepdims=True) + EPS_NORM)
    return raw * recip, recip


def interval(places, lengths_ref, slots):
    first, second, third = lengths_ref[0], lengths_ref[1], lengths_ref[2]
    end_one, end_two = first + second, first + second + third
    low = jnp.where(places >= end_one, end_one, jnp.where(places >= first, first, 0))
    size = jnp.where(places >= end_one, third, jnp.where(places >= first, second, first))
    big, offset = size == BIG_LEN, places - low
    reach = jnp.where(big, BIG_CUMS[0], SMALL_CUMS[0])
    for level in range(1, len(BIG_CUMS)):
        passed = offset >= jnp.where(big, BIG_CUMS[level - 1], SMALL_CUMS[level - 1])
        reach = jnp.where(passed, jnp.where(big, BIG_CUMS[level], SMALL_CUMS[level]), reach)
    padding = places >= end_two
    return jnp.where(padding, end_two, low), jnp.where(padding, slots, low + reach)


def key_spans(step, lengths_ref, slots, rows_q, rows_k):
    first_low, first_high = interval(step * rows_q, lengths_ref, slots)
    last_low, last_high = interval(step * rows_q + rows_q - 1, lengths_ref, slots)
    first = lax.div(first_low, rows_k)
    last = lax.div(last_high + rows_k - 1, rows_k)
    full_first = jnp.minimum(lax.div(last_low + rows_k - 1, rows_k), last)
    full_last = jnp.maximum(lax.div(first_high, rows_k), full_first)
    rows = interval(
        step * rows_q + lax.broadcasted_iota(jnp.int32, (1, rows_q), 1), lengths_ref, slots
    )
    return (first, full_first, full_last, last), rows


def key_loops(spans, body, carry):
    first, full_first, full_last, last = spans
    carry = lax.fori_loop(first, full_first, functools.partial(body, True), carry)
    carry = lax.fori_loop(full_first, full_last, functools.partial(body, False), carry)
    return lax.fori_loop(full_last, last, functools.partial(body, True), carry)


def allowed_block(block, rows_k, low_row, high_row):
    places = block * rows_k + lax.broadcasted_iota(jnp.int32, (rows_k, low_row.shape[1]), 0)
    return (places >= low_row) & (places < high_row)


def project_kernel(
    heads, place_ref, scale_ref, piece_ref, weight_ref, mod_ref, bias_ref, *refs
):
    width = heads * HD
    raw_ref, query_ref, key_ref, keyt_ref, value_ref, valuet_ref, unit_ref = refs[-7:]
    piece = piece_ref[...].astype(F32)
    shift, gain = mod_ref[0:1, :], 1.0 + mod_ref[1:2, :]
    sent_normed = jnp.abs(gain) >= GAIN_LEAST
    inverse = 1.0 / jnp.where(sent_normed, gain, 1.0)
    unit_ref[...] = jnp.where(sent_normed, (piece - shift) * inverse, piece).astype(BF16)
    normed = jnp.where(sent_normed, piece, piece * gain + shift).astype(BF16)
    raw = dot(weight_ref[...], normed, 1, 1) + bias_ref[...]
    raw_ref[...] = raw
    for head in range(heads):
        part = slice(head * HD, (head + 1) * HD)
        unit, _ = unit_rows(raw[part])
        query_ref[part, :] = (unit * scale_ref[head]).astype(BF16)
    keys = [unit_rows(raw[width + head * HD : width + (head + 1) * HD])[0] for head in range(heads)]
    keys = keys[0] if heads == 1 else jnp.concatenate(keys, 0)
    values = raw[2 * width :]
    keyt_ref[...] = keys.astype(BF16)
    key_ref[...] = jnp.transpose(keys).astype(BF16)
    valuet_ref[...] = values.astype(BF16)
    value_ref[...] = jnp.transpose(values).astype(BF16)


def project(place, piece, weight, mod, bias, scales, held, heads, slots):
    width, local, depth = heads * HD, piece.shape[0], piece.shape[1]

    def fixed(shape):
        return pl.BlockSpec(shape, lambda step, *_: (0, 0))

    def columns(rows):
        return pl.BlockSpec((rows, local), lambda step, place, scales: (0, place[0]))

    def lines(cols):
        return pl.BlockSpec((local, cols), lambda step, place, scales: (place[0], 0))

    shapes = [
        jax.ShapeDtypeStruct((3 * width, slots), F32),
        jax.ShapeDtypeStruct((width, slots), BF16),
        jax.ShapeDtypeStruct((slots, width), BF16),
        jax.ShapeDtypeStruct((width, slots), BF16),
        jax.ShapeDtypeStruct((slots, width), BF16),
        jax.ShapeDtypeStruct((width, slots), BF16),
        jax.ShapeDtypeStruct((slots, depth), BF16),
    ]
    held = list(held)
    return pl.pallas_call(
        functools.partial(project_kernel, heads),
        grid_spec=pltpu.PrefetchScalarGridSpec(
            num_scalar_prefetch=2,
            grid=(1,),
            in_specs=[
                fixed((local, depth)),
                fixed((3 * width, depth)),
                fixed((2, depth)),
                fixed((3 * width, 1)),
            ]
            + [pl.BlockSpec(memory_space=pl.ANY)] * len(held),
            out_specs=[
                columns(3 * width),
                columns(width),
                lines(width),
                columns(width),
                lines(width),
                columns(width),
                lines(depth),
            ],
        ),
        out_shape=shapes,
        input_output_aliases={6 + i: i for i in range(len(held))},
        compiler_params=pltpu.CompilerParams(vmem_limit_bytes=40 * 2**20),
        cost_estimate=pl.CostEstimate(
            flops=2 * 3 * width * local * depth, bytes_accessed=8 * 2**20, transcendentals=0
        ),
        name="project",
    )(place, scales, piece, weight, mod, bias, *held)


def forward_kernel(heads, rows_k, lengths_ref, query_ref, key_ref, valuet_ref, out_ref, lse_ref):
    step = pl.program_id(0)
    slots, rows_q = key_ref.shape[0], query_ref.shape[1]
    queries = [
        head_pad(query_ref[head * HD : (head + 1) * HD, :], head, heads) for head in range(heads)
    ]
    spans, (low_row, high_row) = key_spans(step, lengths_ref, slots, rows_q, rows_k)

    def body(masked, block, carry):
        rows = pl.ds(pl.multiple_of(block * rows_k, rows_k), rows_k)
        keys = key_ref[rows, :]
        if masked:
            allowed = allowed_block(block, rows_k, low_row, high_row)
        result = []
        for head in range(heads):
            total, acc = carry[head]
            probs = jnp.exp(dot(keys, queries[head], 1, 0))
            if masked:
                probs = jnp.where(allowed, probs, 0.0)
            total = total + jnp.sum(probs.reshape(rows_k // 8, 8, rows_q), 0)
            acc = acc + dot(
                valuet_ref[head * HD : (head + 1) * HD, rows], probs.astype(BF16), 1, 0
            )
            result.append((total, acc))
        return tuple(result)

    start = tuple(
        (jnp.zeros((8, rows_q), F32), jnp.zeros((HD, rows_q), F32)) for _ in range(heads)
    )
    final = key_loops(spans, body, start)
    for head in range(heads):
        total, acc = final[head]
        denom = jnp.sum(total, 0, keepdims=True)
        out_ref[head * HD : (head + 1) * HD, :] = (acc / denom).astype(BF16)
        lse_ref[head : head + 1, :] = jnp.log(denom)


def backward_kernel(
    heads,
    rows_k,
    lengths_ref,
    scale_ref,
    raw_ref,
    query_ref,
    key_ref,
    keyt_ref,
    value_ref,
    lse_ref,
    up_ref,
    grad_ref,
    qsum_ref,
    gkey_s,
    gvalue_s,
    probs_s,
    gprobs_s,
):
    step = pl.program_id(0)
    width = heads * HD
    slots, rows_q = raw_ref.shape[1], query_ref.shape[1]

    @pl.when(step == 0)
    def _():
        gkey_s[...] = jnp.zeros_like(gkey_s)
        gvalue_s[...] = jnp.zeros_like(gvalue_s)

    queries, query_rows, ups, up_rows, lses = [], [], [], [], []
    for head in range(heads):
        part = slice(head * HD, (head + 1) * HD)
        padded = head_pad(query_ref[part, :], head, heads)
        queries.append(padded)
        query_rows.append(jnp.transpose(padded.astype(F32)).astype(BF16))
        padded = head_pad(up_ref[part, :], head, heads)
        ups.append(padded)
        up_rows.append(jnp.transpose(padded.astype(F32)).astype(BF16))
        lses.append(lse_ref[head : head + 1, :])
    spans, (low_row, high_row) = key_spans(step, lengths_ref, slots, rows_q, rows_k)

    def first(masked, block, carry):
        rows = pl.ds(pl.multiple_of(block * rows_k, rows_k), rows_k)
        keys, values = key_ref[rows, :], value_ref[rows, :]
        if masked:
            allowed = allowed_block(block, rows_k, low_row, high_row)
        result = []
        for head in range(heads):
            probs = jnp.exp(dot(keys, queries[head], 1, 0) - lses[head])
            if masked:
                probs = jnp.where(allowed, probs, 0.0)
            grad_probs = dot(values, ups[head], 1, 0)
            probs_s[head, rows, :] = probs
            gprobs_s[head, rows, :] = grad_probs
            terms = (probs * grad_probs).reshape(rows_k // 8, 8, rows_q)
            result.append(carry[head] + jnp.sum(terms, 0))
        return tuple(result)

    deltas = key_loops(spans, first, tuple(jnp.zeros((8, rows_q), F32) for _ in range(heads)))
    deltas = [jnp.sum(delta, 0, keepdims=True) for delta in deltas]

    def second(block, carry):
        rows = pl.ds(pl.multiple_of(block * rows_k, rows_k), rows_k)
        result = []
        gkey, gvalue = gkey_s[rows, :], gvalue_s[rows, :]
        for head in range(heads):
            probs = probs_s[head, rows, :]
            grad_scores = (probs * (gprobs_s[head, rows, :] - deltas[head])).astype(BF16)
            gvalue = gvalue + dot(probs.astype(BF16), up_rows[head], 1, 0)
            gkey = gkey + dot(grad_scores, query_rows[head], 1, 0)
            keyt = keyt_ref[head * HD : (head + 1) * HD, rows]
            result.append(carry[head] + dot(keyt, grad_scores, 1, 0))
        gkey_s[rows, :] = gkey
        gvalue_s[rows, :] = gvalue
        return tuple(result)

    start = tuple(jnp.zeros((HD, rows_q), F32) for _ in range(heads))
    final = lax.fori_loop(spans[0], spans[3], second, start)
    cols = pl.ds(pl.multiple_of(step * rows_q, rows_q), rows_q)
    for head in range(heads):
        part = slice(head * HD, (head + 1) * HD)
        grad = final[head]
        unit, recip = unit_rows(raw_ref[part, cols])
        qsum_ref[head : head + 1, :] = jnp.sum(grad * unit, 0, keepdims=True)
        scaled = scale_ref[head] * grad
        back = recip * (scaled - unit * jnp.sum(scaled * unit, 0, keepdims=True))
        grad_ref[part, cols] = back.astype(BF16)

    @pl.when(step == pl.num_programs(0) - 1)
    def _():
        def finish(block, carry):
            cols = pl.ds(pl.multiple_of(block * BLK, BLK), BLK)
            gkey = jnp.transpose(gkey_s[cols, :])
            for head in range(heads):
                part = slice(width + head * HD, width + (head + 1) * HD)
                unit, recip = unit_rows(raw_ref[part, cols])
                grad = gkey[head * HD : (head + 1) * HD, :]
                back = recip * (grad - unit * jnp.sum(grad * unit, 0, keepdims=True))
                grad_ref[part, cols] = back.astype(BF16)
            grad_ref[2 * width :, cols] = jnp.transpose(gvalue_s[cols, :]).astype(BF16)
            return carry

        lax.fori_loop(0, slots // BLK, finish, 0)


def whole_spec(shape):
    return pl.BlockSpec(shape, lambda step, *_: (0,) * len(shape))


def column_spec(rows, cols):
    return pl.BlockSpec((rows, cols), lambda step, *_: (0, step))


def attention_forward(query, key, valuet, lengths, heads):
    width, slots = query.shape
    rows_q, rows_k = FORWARD_BLOCK
    return pl.pallas_call(
        functools.partial(forward_kernel, heads, rows_k),
        grid_spec=pltpu.PrefetchScalarGridSpec(
            num_scalar_prefetch=1,
            grid=(slots // rows_q,),
            in_specs=[column_spec(width, rows_q), whole_spec(key.shape), whole_spec(valuet.shape)],
            out_specs=[column_spec(width, rows_q), column_spec(heads, rows_q)],
        ),
        out_shape=[
            jax.ShapeDtypeStruct((width, slots), BF16),
            jax.ShapeDtypeStruct((heads, slots), F32),
        ],
        compiler_params=pltpu.CompilerParams(
            dimension_semantics=("arbitrary",), vmem_limit_bytes=32 * 2**20
        ),
        cost_estimate=pl.CostEstimate(
            flops=heads * slots * slots * 1000, bytes_accessed=4 * 2**20, transcendentals=0
        ),
        name="attend",
    )(lengths, query, key, valuet)


def attention_backward(raw, query, key, keyt, value, lse, up, lengths, scales, heads):
    width, slots = query.shape
    rows_q, rows_k = BACKWARD_BLOCK
    return pl.pallas_call(
        functools.partial(backward_kernel, heads, rows_k),
        grid_spec=pltpu.PrefetchScalarGridSpec(
            num_scalar_prefetch=2,
            grid=(slots // rows_q,),
            in_specs=[
                whole_spec(raw.shape),
                column_spec(width, rows_q),
                whole_spec(key.shape),
                whole_spec(keyt.shape),
                whole_spec(value.shape),
                column_spec(heads, rows_q),
                column_spec(width, rows_q),
            ],
            out_specs=[whole_spec(raw.shape), column_spec(heads, rows_q)],
            scratch_shapes=[
                pltpu.VMEM((slots, width), F32),
                pltpu.VMEM((slots, width), F32),
                pltpu.VMEM((heads, slots, rows_q), F32),
                pltpu.VMEM((heads, slots, rows_q), F32),
            ],
        ),
        out_shape=[
            jax.ShapeDtypeStruct(raw.shape, BF16),
            jax.ShapeDtypeStruct((heads, slots), F32),
        ],
        compiler_params=pltpu.CompilerParams(
            dimension_semantics=("arbitrary",), vmem_limit_bytes=56 * 2**20
        ),
        cost_estimate=pl.CostEstimate(
            flops=heads * slots * slots * 2000, bytes_accessed=14 * 2**20, transcendentals=0
        ),
        name="attend_back",
    )(lengths, scales, raw, query, key, keyt, value, lse, up)


def mlp_kernel(
    rows,
    part_ref,
    normed_ref,
    up_ref,
    first_ref,
    second_ref,
    bias_ref,
    sent_one_ref,
    kept_one_ref,
    sent_two_ref,
    kept_two_ref,
    bias_grad_ref,
    branch_ref,
    grad_ref,
):
    part, step = pl.program_id(0), pl.program_id(1)
    start = (part == 0) & (step == 0)
    group = first_ref.shape[0]
    normed, up = normed_ref[...], up_ref[...]
    first = first_ref[:, :rows, :].reshape(group * rows, first_ref.shape[2])
    second = second_ref[...]
    pre = dot(normed, first, 1, 1) + bias_ref[...]
    grad_hidden = dot(up, second, 1, 1)
    square = pre * pre
    angle = jnp.tanh(GELU_ROOT * pre * (1.0 + GELU_CUBE * square))
    half = 0.5 * (1.0 + angle)
    slope = half + 0.5 * pre * (1.0 - angle * angle) * GELU_ROOT * (1.0 + 3.0 * GELU_CUBE * square)
    hidden = (pre * half).astype(BF16)
    grad_pre = (slope * grad_hidden).astype(BF16)
    bias_grad_ref[...] = jnp.sum(grad_pre.astype(F32), 0, keepdims=True)
    branch = dot(hidden, second, 1, 0)
    grad = dot(grad_pre, first, 1, 0)

    @pl.when(start)
    def _():
        branch_ref[...] = branch
        grad_ref[...] = grad

    @pl.when(jnp.logical_not(start))
    def _():
        branch_ref[...] += branch
        grad_ref[...] += grad

    one = dot(grad_pre, normed, 0, 0).astype(BF16).reshape(kept_one_ref.shape)
    two = dot(hidden, up, 0, 0).astype(BF16).reshape(kept_two_ref.shape)
    sending = part < pl.num_programs(0) // 2

    @pl.when(sending)
    def _():
        sent_one_ref[...] = one
        sent_two_ref[...] = two

    @pl.when(jnp.logical_not(sending))
    def _():
        kept_one_ref[...] = one
        kept_two_ref[...] = two


def mlp(parts, normed, up, first, second, bias, heads_all, rows):
    local, width = normed.shape
    total = parts.shape[0]
    group = max(8, 128 // rows)
    steps = heads_all // group
    cols = group * rows
    full_rows = first.shape[1]
    half = total // 2

    def fixed(p, j, part):
        return (0, 0)

    def sent(p, j, part):
        flat = jnp.minimum(p * steps + j, half * steps - 1)
        return (flat // steps, flat % steps, 0, 0)

    def kept(p, j, part):
        flat = jnp.maximum(p * steps + j - half * steps, 0)
        return (flat // steps, flat % steps, 0, 0)

    grads = jax.ShapeDtypeStruct((half, heads_all, rows, width), BF16)
    return pl.pallas_call(
        functools.partial(mlp_kernel, rows),
        grid_spec=pltpu.PrefetchScalarGridSpec(
            num_scalar_prefetch=1,
            grid=(total, steps),
            in_specs=[
                pl.BlockSpec((local, width), fixed),
                pl.BlockSpec((local, width), fixed),
                pl.BlockSpec((group, full_rows, width), lambda p, j, part: (part[p] * steps + j, 0, 0)),
                pl.BlockSpec((cols, width), lambda p, j, part: (part[p] * steps + j, 0)),
                pl.BlockSpec((1, cols), lambda p, j, part: (0, part[p] * steps + j)),
            ],
            out_specs=[
                pl.BlockSpec((1, group, rows, width), sent),
                pl.BlockSpec((1, group, rows, width), kept),
                pl.BlockSpec((1, group, rows, width), sent),
                pl.BlockSpec((1, group, rows, width), kept),
                pl.BlockSpec((1, cols), lambda p, j, part: (0, part[p] * steps + j)),
                pl.BlockSpec((local, width), fixed),
                pl.BlockSpec((local, width), fixed),
            ],
        ),
        out_shape=[
            grads,
            grads,
            grads,
            grads,
            jax.ShapeDtypeStruct((1, total * heads_all * rows), F32),
            jax.ShapeDtypeStruct((local, width), F32),
            jax.ShapeDtypeStruct((local, width), F32),
        ],
        compiler_params=pltpu.CompilerParams(
            dimension_semantics=("arbitrary", "arbitrary"), vmem_limit_bytes=52 * 2**20
        ),
        cost_estimate=pl.CostEstimate(
            flops=12 * local * width * total * heads_all * rows,
            bytes_accessed=40 * 2**20,
            transcendentals=0,
        ),
        name="mlp",
    )(parts, normed, up, first, second, bias)


def ring_blocks_kernel(
    halves, place_ref, grad_ref, weight_ref, one_ref, two_ref, three_ref, four_ref, *out_refs
):
    terms = dot(grad_ref[...], weight_ref[...], 0, 0).astype(BF16)
    rest = (one_ref[0].astype(F32) + two_ref[0].astype(F32)).astype(BF16)
    last = (three_ref[0].astype(F32) + four_ref[0].astype(F32)).astype(BF16)
    rest = jnp.concatenate([rest, last], 0)
    local = terms.shape[0]
    if halves:
        half = out_refs[0].shape[0]
        out_refs[0][...] = terms[:half]
        out_refs[1][: local - half, :] = terms[half:]
        out_refs[1][local - half :, :] = rest
    else:
        out_refs[0][0, :local, :] = terms
        out_refs[0][0, local:, :] = rest


def ring_blocks(places, grad, weight, pairs, local, halves):
    depth, width = weight.shape
    total = local + pairs[0].shape[1] + pairs[2].shape[1]
    if halves:
        sizes = [total // 2, total - total // 2]
        out_specs = [pl.BlockSpec((size, width), lambda step, place: (0, 0)) for size in sizes]
        out_shape = [jax.ShapeDtypeStruct((size, width), BF16) for size in sizes]
    else:
        out_specs = pl.BlockSpec((1, total, width), lambda step, place: (step, 0, 0))
        out_shape = jax.ShapeDtypeStruct((places.shape[0], total, width), BF16)
    return pl.pallas_call(
        functools.partial(ring_blocks_kernel, halves),
        grid_spec=pltpu.PrefetchScalarGridSpec(
            num_scalar_prefetch=1,
            grid=(places.shape[0],),
            in_specs=[
                pl.BlockSpec((depth, local), lambda step, place: (0, place[step])),
                pl.BlockSpec((depth, width), lambda step, place: (0, 0)),
            ]
            + [
                pl.BlockSpec((1, pair.shape[1], width), lambda step, place: (place[step], 0, 0))
                for pair in pairs
            ],
            out_specs=out_specs,
        ),
        out_shape=out_shape,
        compiler_params=pltpu.CompilerParams(vmem_limit_bytes=60 * 2**20),
        cost_estimate=pl.CostEstimate(flops=1, bytes_accessed=1, transcendentals=0),
        name="ring_blocks",
    )(places, grad, weight, *pairs)


def add_half_kernel(index, lower, blocks_ref, got_ref, out_ref):
    half = got_ref.shape[0]
    block = blocks_ref[0]
    part = slice(0, half) if lower else slice(block.shape[0] - half, block.shape[0])
    rest = slice(half, block.shape[0]) if lower else slice(0, block.shape[0] - half)
    out_ref[rest, :] = block[rest]
    out_ref[part, :] = (block[part].astype(F32) + got_ref[...].astype(F32)).astype(BF16)


def add_half(blocks, index, got, lower):
    _, rows, width = blocks.shape
    return pl.pallas_call(
        functools.partial(add_half_kernel, index, lower),
        grid=(1,),
        in_specs=[
            pl.BlockSpec((1, rows, width), lambda step: (index, 0, 0)),
            pl.BlockSpec(got.shape, lambda step: (0, 0)),
        ],
        out_specs=pl.BlockSpec((rows, width), lambda step: (0, 0)),
        out_shape=jax.ShapeDtypeStruct((rows, width), BF16),
        compiler_params=pltpu.CompilerParams(vmem_limit_bytes=60 * 2**20),
        cost_estimate=pl.CostEstimate(flops=1, bytes_accessed=1, transcendentals=0),
        name="add_half",
    )(blocks, got)


def finish_kernel(rows, order_ref, value_ref, first_ref, second_ref):
    value = value_ref[0].astype(F32)
    first_ref[...] = jnp.transpose(value[:rows])
    second_ref[...] = value[rows:]


def finish_weights(order, value, rows):
    total, full_rows, width = value.shape
    return pl.pallas_call(
        functools.partial(finish_kernel, rows),
        grid_spec=pltpu.PrefetchScalarGridSpec(
            num_scalar_prefetch=1,
            grid=(total,),
            in_specs=[pl.BlockSpec((1, full_rows, width), lambda step, order: (order[step], 0, 0))],
            out_specs=[
                pl.BlockSpec((width, rows), lambda step, order: (0, step)),
                pl.BlockSpec((full_rows - rows, width), lambda step, order: (step, 0)),
            ],
        ),
        out_shape=[
            jax.ShapeDtypeStruct((width, total * rows), F32),
            jax.ShapeDtypeStruct((total * (full_rows - rows), width), F32),
        ],
        name="finish_weights",
    )(order, value)


def after(value, *others):
    return lax.optimization_barrier((value, *others))[0]


def shards(
    block_input,
    lengths,
    scale_ids,
    class_ids,
    code_ids,
    cotangent,
    class_table,
    ada_weight,
    ada_bias,
    qkv_weight,
    qv_bias,
    qk_scale,
    proj_weight,
    proj_bias,
    fc1_weight,
    fc1_bias,
    fc2_weight,
    fc2_bias,
):
    count, data_count = lax.axis_size("head"), lax.axis_size("dp")
    me, data_me = lax.axis_index("head"), lax.axis_index("dp")
    _, local, width = block_input.shape
    slots = local * count
    heads = qk_scale.shape[0]
    feats = heads * HD
    hidden_here = fc1_weight.shape[1]
    data_masks = [1 << bit for bit in range(data_count.bit_length() - 1)]
    both_axes = ("dp", "head")

    ring = list(range(0, count, 2)) + list(range(count - 1, 0, -2))
    half_count = count // 2
    offsets = [0]
    for away in range(1, half_count):
        offsets += [away, -away]
    offsets.append(half_count)
    my_pos = jnp.where(me % 2 == 0, me // 2, count - 1 - me // 2)

    def at(away):
        pos = (my_pos + away + count) % count
        return jnp.where(pos < half_count, 2 * pos, 2 * (count - 1 - pos) + 1)

    def rot(value, away):
        pairs = [(ring[(i + away) % count], ring[i]) for i in range(count)]
        return lax.ppermute(value, "head", pairs)

    def swap(value, mask):
        return lax.ppermute(value, "dp", [(i, i ^ mask) for i in range(data_count)])

    def xor_head(value, mask):
        return lax.ppermute(value, "head", [(i, i ^ mask) for i in range(count)])

    def head_sum_far(value):
        total = value
        for mask in range(2, count, 2):
            total = total + xor_head(value, mask)
        return total

    def head_sum_near(value):
        return value + xor_head(value, 1)

    inputs_full = block_input[0].astype(F32)
    unit_one, recip_one = normalize(inputs_full)

    hidden_part, feat_part = hidden_here // data_count, feats // data_count
    fc1_part = lax.dynamic_slice(fc1_weight, (0, data_me * hidden_part), (width, hidden_part)).T
    proj_part = lax.dynamic_slice(proj_weight, (data_me * feat_part, 0), (feat_part, width))
    fc2_part = lax.dynamic_slice(fc2_weight, (data_me * hidden_part, 0), (hidden_part, width))
    first_full = lax.all_gather(
        jnp.concatenate([fc1_part, proj_part], 0), both_axes, axis=0, tiled=False
    )
    fc2_full = lax.all_gather(fc2_part, both_axes, axis=0, tiled=True)
    proj_full = first_full[:, hidden_part:].reshape(data_count, count, feat_part, width)
    proj_full = jnp.transpose(proj_full, (1, 0, 2, 3)).reshape(-1, width)

    cond = jnp.take(class_table, class_ids, axis=0).astype(F32)
    act = jax.nn.silu(cond).astype(BF16)
    mod_local = jnp.dot(act, ada_weight, preferred_element_type=F32)[0] + ada_bias.astype(F32)
    small = jnp.concatenate([mod_local, fc1_bias.astype(F32)])[None, :]
    pieces = [small] + [xor_head(small, mask) for mask in range(2, count, 2)]
    pieces = jnp.concatenate(pieces, 0)
    small_all = jnp.stack([pieces, xor_head(pieces, 1)], 1).reshape(count, -1)
    small_all = jnp.take(
        small_all, jnp.bitwise_xor(me, jnp.arange(count, dtype=jnp.int32)), axis=0
    )
    mod_here = mod_local.shape[0]
    modulation = small_all[:, :mod_here].reshape(6, width)
    shift_one, scale_one, gate_one, shift_two, scale_two, gate_two = [
        modulation[i : i + 1] for i in range(6)
    ]
    gain_one = 1.0 + scale_one
    ring_low = jnp.where(
        jnp.abs(gain_one) >= GAIN_LEAST, unit_one * gain_one + shift_one, unit_one
    ).astype(BF16)
    units = {0: ring_low, 1: rot(ring_low, 1), -1: rot(ring_low, -1)}
    bias_full = small_all[:, mod_here:].reshape(count, data_count, hidden_part)
    bias_full = jnp.transpose(bias_full, (1, 0, 2)).reshape(1, -1)

    qkv_rows = jnp.transpose(
        after(qkv_weight, small_all).T.reshape(heads, 3, HD, width), (1, 0, 2, 3)
    ).reshape(3 * feats, width)
    bias_pair = qv_bias.astype(F32).reshape(heads, 2, HD)
    qkv_bias = jnp.stack([bias_pair[:, 0], jnp.zeros_like(bias_pair[:, 0]), bias_pair[:, 1]], 0)
    qkv_bias = qkv_bias.reshape(3 * feats, 1)
    scale_exp = jnp.exp(qk_scale)

    def put(held, away):
        place = at(away).astype(jnp.int32)[None]
        return project(
            place, units[away], qkv_rows, modulation[:2], qkv_bias, scale_exp, held, heads, slots
        )

    for away in range(2, half_count):
        units[away], units[-away] = rot(units[away - 1], 1), rot(units[1 - away], -1)
    held = put([], 0)
    for away in range(1, half_count - 1):
        held = put(put(held, away), -away)
        if away == 1:
            last, units[half_count - 1], units[1 - half_count] = lax.optimization_barrier(
                (held[1], units[half_count - 1], units[1 - half_count])
            )
            held = [held[0], last] + list(held[2:])
            proj_full, units[half_count - 1] = lax.optimization_barrier(
                (proj_full, units[half_count - 1])
            )
    half = local // 2
    ends = [
        rot(units[half_count - 1][:half], 1),
        rot(units[1 - half_count][half:], -1),
    ]
    held = put(put(held, half_count - 1), 1 - half_count)
    units[half_count] = jnp.concatenate(ends, 0)
    held = put(held, half_count)
    raw, query, key, keyt, value, valuet, unit_all = held
    out_low, lse = attention_forward(query, key, valuet, lengths[0], heads)

    attended = jnp.zeros((feats * count, local), BF16)
    for away in offsets:
        piece = lax.dynamic_slice(out_low, (0, at(-away) * local), (feats, local))
        piece = piece if away == 0 else rot(piece, away)
        attended = lax.dynamic_update_slice(attended, piece, (at(away) * feats, 0))
    cot_full = cotangent[0].astype(F32)
    grad_mlp = (cot_full * gate_two).astype(BF16)
    attn_branch = dot(attended, proj_full, 0, 0) + proj_bias.astype(F32)
    resid = inputs_full + gate_one * attn_branch
    unit_two, recip_two = normalize(resid)
    normed_two = (unit_two * (1.0 + scale_two) + shift_two).astype(BF16)

    kept_t = list(range(0, data_count, 2))
    all_t = [t + 1 for t in kept_t] + kept_t
    parts = jnp.bitwise_xor(data_me, jnp.array(all_t, jnp.int32))
    sent_one, kept_one, sent_two, kept_two, fc1_bias_sum, mlp_branch, grad_normed_two = mlp(
        parts, normed_two, grad_mlp, first_full, fc2_full, bias_full, count, hidden_part
    )
    grad_shift_two = jnp.sum(grad_normed_two, 0)
    grad_scale_two = jnp.sum(grad_normed_two * unit_two, 0)
    grad_resid = cot_full + norm_back(unit_two, recip_two, grad_normed_two * (1.0 + scale_two))
    grad_attn = (grad_resid * gate_one).astype(BF16)
    grad_gate_one = jnp.sum(grad_resid * attn_branch, 0)
    grad_attended = dot(proj_full, grad_attn, 1, 1).astype(BF16)
    up_pieces = {}
    for away in offsets:
        piece = lax.dynamic_slice(grad_attended, (at(away) * feats, 0), (feats, local))
        up_pieces[away] = piece if away == 0 else rot(piece, -away)

    sent_one, sent_two = lax.optimization_barrier((sent_one, sent_two))
    got_one, got_two = swap(sent_one, 1), swap(sent_two, 1)

    def add(left, right):
        return (left.astype(F32) + right.astype(F32)).astype(BF16)

    def split_pair(kept):
        kept = {t: kept[i] for i, t in enumerate(kept_t)}
        for mask in data_masks[1:-1]:
            kept = {
                t: add(kept[t], swap(kept[t ^ mask], mask)) for t in kept if not t & mask
            }
        return kept[0], swap(kept[data_masks[-1]], data_masks[-1])

    kept_one = [add(kept_one[i], got_one[i]) for i in range(len(kept_t))]
    fc2_stack = jnp.stack([add(kept_two[i], got_two[i]) for i in range(len(kept_t))], 1)
    fc2_stack = fc2_stack.reshape(count, len(kept_t) * hidden_part, width)
    proj_grad = dot(attended, grad_attn, 1, 0).astype(BF16)
    proj_grad = proj_grad.reshape(count, data_count, feat_part, width)
    proj_parts = [
        lax.dynamic_index_in_dim(proj_grad, parts[i], 1, keepdims=False) for i in range(data_count)
    ]
    got_three = swap(jnp.stack(proj_parts[: len(kept_t)], 0), 1)
    kept_three = [add(proj_parts[len(kept_t) + i], got_three[i]) for i in range(len(kept_t))]
    mlp_branch = mlp_branch + fc2_bias.astype(F32)
    block_output = (resid + gate_two * mlp_branch).astype(BF16)
    grad_gate_two = jnp.sum(cot_full * mlp_branch, 0)

    up = jnp.zeros((feats, slots), BF16)
    for away in offsets[:5]:
        up = lax.dynamic_update_slice(up, up_pieces[away], (0, at(-away) * local))
    up, kept_one, kept_three, fc2_stack = lax.optimization_barrier(
        (up, kept_one, kept_three, fc2_stack)
    )
    for away in offsets[5:]:
        up = lax.dynamic_update_slice(up, up_pieces[away], (0, at(-away) * local))
    fc2_mine = lax.psum_scatter(fc2_stack, "head", scatter_dimension=0, tiled=True)
    fc2_mine = fc2_mine.reshape(len(kept_t), hidden_part, width)

    one_here, one_got = split_pair(kept_one)
    three_here, three_got = split_pair(kept_three)

    def share(value, hop):
        value = jnp.stack([value, hop], 0)
        for mask in reversed(data_masks[:-1]):
            value = jnp.stack([value, swap(value, mask)], 0)
        bits = len(data_masks)
        value = value.reshape((data_count,) + value.shape[bits:])
        table = [int(format(t, "b").zfill(bits)[::-1], 2) for t in range(data_count)]
        places = jnp.take(
            jnp.array(table, jnp.int32),
            jnp.bitwise_xor(data_me, jnp.arange(data_count, dtype=jnp.int32)),
        )
        return value, places

    fc2_bias_sum = jnp.sum(grad_mlp.astype(F32), 0)
    proj_bias_sum = jnp.sum(grad_attn.astype(F32), 0)
    valid = me * local + jnp.arange(local, dtype=jnp.int32) < jnp.sum(lengths[0])
    code_range = jnp.arange(CODES, dtype=jnp.int32)
    code_hits = (after(code_ids, units[1])[0][:, None] == code_range[None, :]) & valid[:, None]
    local_counts = jnp.sum(code_hits.astype(F32), 0)
    fc1_bias_sum = fc1_bias_sum.reshape(data_count, count, hidden_part)
    fc1_bias_sum = jnp.transpose(fc1_bias_sum, (1, 0, 2)).reshape(-1)
    early = jnp.concatenate(
        [
            local_counts,
            fc2_bias_sum,
            proj_bias_sum,
            fc1_bias_sum,
            grad_gate_one,
            grad_shift_two,
            grad_scale_two,
            grad_gate_two,
        ]
    )
    early, up = lax.optimization_barrier((early, up))
    early = head_sum_far(early[None, :])

    grad_raw, query_sums = attention_backward(
        raw, query, key, keyt, value, lse, up, lengths[0], scale_exp, heads
    )
    grad_raw, query_sums, one_got, three_got, early = lax.optimization_barrier(
        (grad_raw, query_sums, one_got, three_got, early)
    )
    pairs = [one_here, one_got, three_here, three_got]

    def send(ups, downs):
        return rot(ups, -1), rot(downs, 1)

    places = jnp.stack([at(away) for away in offsets]).astype(jnp.int32)
    far_up, far_down = ring_blocks(places[-1:], grad_raw, qkv_rows, pairs, local, True)
    got_up, got_down = send(far_up, far_down)
    half = far_up.shape[0]

    source, _ = lax.optimization_barrier((grad_raw, far_up))
    blocks = ring_blocks(places[:-1], source, qkv_rows, pairs, local, False)

    got_up, got_down, blocks, source = lax.optimization_barrier(
        (got_up, got_down, blocks, source)
    )
    ups = add_half(blocks, offsets.index(half_count - 1), got_up, True)
    downs = add_half(blocks, offsets.index(1 - half_count), got_down, False)
    blocks = {away: blocks[i] for i, away in enumerate(offsets[:-1])}
    ups, downs, source = lax.optimization_barrier((ups, downs, source))
    got_up, got_down = send(ups, downs)
    bias_sums = jnp.sum(source.astype(F32), 1)
    unit_grad = dot(source, unit_all, 1, 0)
    qkv_grad = unit_grad * (1.0 + scale_one) + bias_sums[:, None] * shift_one
    qkv_grad = qkv_grad.astype(BF16)
    scale_sums = scale_exp * jnp.sum(query_sums, 1)
    rows_float = qkv_rows.astype(F32)
    grad_shift_one = jnp.sum(rows_float * bias_sums[:, None], 0)
    grad_scale_one = jnp.sum(rows_float * unit_grad, 0)
    late = head_sum_far(jnp.concatenate([grad_shift_one, grad_scale_one])[None, :])
    over_rows = CODES + 2 * width + count * hidden_here

    for away in range(half_count - 2, 0, -1):
        got_up, got_down, late, qkv_grad = lax.optimization_barrier(
            (got_up, got_down, late, qkv_grad)
        )
        ups, downs = add(blocks[away], got_up), add(blocks[-away], got_down)
        ups, downs, late, early, qkv_grad, fc2_mine = lax.optimization_barrier(
            (ups, downs, late, early, qkv_grad, fc2_mine)
        )
        got_up, got_down = send(ups, downs)
        if away == half_count - 2:
            late = head_sum_near(jnp.concatenate([late, early], 1))
            for mask in data_masks:
                qkv_grad = add(qkv_grad, swap(qkv_grad, mask))
            for mask in data_masks[1:]:
                got = swap(fc2_mine, mask)
                fc2_mine = jnp.stack(
                    [add(fc2_mine[i], got[kept_t.index(t ^ mask)]) for i, t in enumerate(kept_t)], 0
                )
            fc2_all = jnp.concatenate([fc2_mine, swap(fc2_mine, 1)], 0)
            fc2_order = jnp.bitwise_xor(data_me, jnp.arange(data_count, dtype=jnp.int32))
            fc2_order = fc2_order // 2 + (fc2_order % 2) * len(kept_t)
            fc2_mine = jnp.take(fc2_all, fc2_order, axis=0).astype(F32).reshape(-1, width)
        if away == 1:
            sums = late[0]
            mod_all = jnp.concatenate([sums[: 2 * width], sums[2 * width + over_rows :]])
            rows = jnp.concatenate(
                [
                    lax.dynamic_slice_in_dim(mod_all, me * mod_here, mod_here, 0),
                    class_ids.astype(F32),
                    bias_sums,
                    scale_sums,
                    sums[2 * width : 2 * width + over_rows],
                ]
            )[None, :]
            rows = jnp.concatenate(
                [rows] + [swap(rows, mask) for mask in range(1, data_count)], 0
            )
            rows = jnp.take(
                rows, jnp.bitwise_xor(data_me, jnp.arange(data_count, dtype=jnp.int32)), axis=0
            )
            class_rows = rows[:, mod_here].astype(jnp.int32)
            mod_rows = rows[:, :mod_here]
            tail = jnp.sum(rows[:, mod_here + 1 :], 0)
            cond_terms = lax.dot_general(
                mod_rows, ada_weight.astype(F32), (((1,), (1,)), ((), ())), precision=HIGH
            )
            cond_sums = head_sum_far(cond_terms)

    qkv_weight_grad = (
        jnp.transpose(qkv_grad.reshape(3, heads, HD, width), (1, 0, 2, 3))
        .reshape(3 * feats, width)
        .astype(F32)
        .T
    )
    cond_rows = jnp.take(class_table, class_rows, axis=0).astype(F32)
    act_rows = jax.nn.silu(cond_rows).astype(BF16).astype(F32)
    ada_weight_grad = lax.dot_general(
        act_rows, mod_rows, (((0,), (0,)), ((), ())), precision=HIGH
    )
    ada_bias_grad = jnp.sum(mod_rows, 0)
    got_up, got_down, tail, cond_sums, qkv_weight_grad, ada_weight_grad, fc2_weight_grad = (
        lax.optimization_barrier(
            (got_up, got_down, tail, cond_sums, qkv_weight_grad, ada_weight_grad, fc2_mine)
        )
    )
    ring_total = blocks[0].astype(F32) + got_up.astype(F32) + got_down.astype(F32)
    grad_normed_one = ring_total[:local]
    first_mine = [value[local:].astype(F32) for value in (blocks[0], got_up, got_down)]
    first_mine = (first_mine[0] + first_mine[1] + first_mine[2]).astype(BF16)
    bias_sums = tail[: 3 * feats].reshape(3, heads, HD)
    qv_bias_grad = jnp.stack([bias_sums[0], bias_sums[2]], 1).reshape(-1)
    qk_scale_grad = tail[3 * feats : 3 * feats + heads]
    tail = tail[3 * feats + heads :]
    code_hist = tail[:CODES].astype(jnp.int32)
    fc2_bias_grad = tail[CODES : CODES + width]
    proj_bias_grad = tail[CODES + width : CODES + 2 * width]
    fc1_bias_grad = lax.dynamic_slice_in_dim(
        tail[CODES + 2 * width :], me * hidden_here, hidden_here, 0
    )

    input_grad = (
        grad_resid + norm_back(unit_one, recip_one, grad_normed_one * (1.0 + scale_one))
    ).astype(BF16)
    first_hop = swap(first_mine, data_masks[-1])
    cond_sums, first_hop = lax.optimization_barrier((cond_sums, first_hop))
    first_grad, order = share(first_mine, first_hop)
    cond_sums = head_sum_near(cond_sums)
    _, silu_pull = jax.vjp(jax.nn.silu, cond_rows)
    grad_rows = silu_pull(cond_sums)[0]
    class_range = jnp.arange(class_table.shape[0], dtype=jnp.int32)
    class_table_grad = jnp.zeros(class_table.shape, F32)
    for row in range(data_count):
        hit = class_range[:, None] == class_rows[row]
        class_table_grad = class_table_grad + jnp.where(hit, grad_rows[row][None, :], 0.0)
    if hidden_part % 128 == 0:
        fc1_weight_grad, proj_weight_grad = finish_weights(order, first_grad, hidden_part)
    else:
        first_grad = jnp.take(first_grad, order, axis=0).astype(F32)
        fc1_weight_grad = first_grad[:, :hidden_part].reshape(-1, width).T
        proj_weight_grad = first_grad[:, hidden_part:].reshape(-1, width)

    return (
        block_output[None],
        input_grad[None],
        class_table_grad,
        ada_weight_grad,
        ada_bias_grad,
        qkv_weight_grad,
        qv_bias_grad,
        qk_scale_grad,
        proj_weight_grad,
        proj_bias_grad,
        fc1_weight_grad,
        fc1_bias_grad,
        fc2_weight_grad,
        fc2_bias_grad,
        code_hist,
    )


def solution(mesh):
    placed = (
        P("dp", "head", None),
        P("dp", None),
        P("dp", None),
        P("dp"),
        P("dp", "head"),
        P("dp", "head", None),
        P(),
        P(None, "head"),
        P("head"),
        P(None, "head"),
        P("head"),
        P("head"),
        P("head", None),
        P(),
        P(None, "head"),
        P("head"),
        P("head", None),
        P(),
    )
    return jax.shard_map(
        shards,
        mesh=mesh,
        in_specs=placed,
        out_specs=(
            P("dp", "head", None),
            P("dp", "head", None),
            P(),
            P(None, "head"),
            P("head"),
            P(None, "head"),
            P("head"),
            P("head"),
            P("head", None),
            P(),
            P(None, "head"),
            P("head"),
            P("head", None),
            P(),
            P(),
        ),
        check_vma=False,
    )
```

```python
import functools

import jax
import jax.numpy as jnp
from jax import lax
from jax.experimental import pallas as pl
from jax.experimental.pallas import tpu as pltpu
from jax.sharding import PartitionSpec as P

HD = 64
CODES = 4096
BLK = 256
FORWARD_BLOCK = (1024, 512)
BACKWARD_BLOCK = (256, 512)
EPS_NORM = 1e-06
HIGH = lax.Precision.HIGHEST
GELU_ROOT = (2.0 / 3.141592653589793) ** 0.5
GELU_CUBE = 0.044715
GAIN_LEAST = 0.25
F32 = jnp.float32
BF16 = jnp.bfloat16
BIG_LEN = 2240
BIG_CUMS = (1, 5, 14, 30, 66, 147, 316, 640, 1216, 2240)
SMALL_CUMS = (1, 5, 14, 30, 55, 91, 155, 255, 424, 680)


def normalize(values):
    mean_val = jnp.mean(values, -1, keepdims=True)
    centered = values - mean_val
    variance = jnp.mean(centered * centered, -1, keepdims=True)
    recip = lax.rsqrt(variance + EPS_NORM)
    return (centered * recip, recip)


def norm_back(unit, recip, upstream):
    mean_up = jnp.mean(upstream, -1, keepdims=True)
    mean_cross = jnp.mean(upstream * unit, -1, keepdims=True)
    return recip * (upstream - mean_up - unit * mean_cross)


def dot(left, right, left_dim, right_dim):
    return lax.dot_general(
        left, right, (((left_dim,), (right_dim,)), ((), ())), preferred_element_type=F32
    )


def head_pad(part, head, heads):
    pieces = [part if other == head else jnp.zeros_like(part) for other in range(heads)]
    return pieces[0] if heads == 1 else jnp.concatenate(pieces, 0)


def unit_rows(raw):
    recip = lax.rsqrt(jnp.sum(raw * raw, 0, keepdims=True) + EPS_NORM)
    return raw * recip, recip


def interval(places, lengths_ref, slots):
    first, second, third = lengths_ref[0], lengths_ref[1], lengths_ref[2]
    end_one, end_two = first + second, first + second + third
    low = jnp.where(places >= end_one, end_one, jnp.where(places >= first, first, 0))
    size = jnp.where(places >= end_one, third, jnp.where(places >= first, second, first))
    big, offset = size == BIG_LEN, places - low
    reach = jnp.where(big, BIG_CUMS[0], SMALL_CUMS[0])
    for level in range(1, len(BIG_CUMS)):
        passed = offset >= jnp.where(big, BIG_CUMS[level - 1], SMALL_CUMS[level - 1])
        reach = jnp.where(passed, jnp.where(big, BIG_CUMS[level], SMALL_CUMS[level]), reach)
    padding = places >= end_two
    return jnp.where(padding, end_two, low), jnp.where(padding, slots, low + reach)


def key_spans(step, lengths_ref, slots, rows_q, rows_k):
    first_low, first_high = interval(step * rows_q, lengths_ref, slots)
    last_low, last_high = interval(step * rows_q + rows_q - 1, lengths_ref, slots)
    first = lax.div(first_low, rows_k)
    last = lax.div(last_high + rows_k - 1, rows_k)
    full_first = jnp.minimum(lax.div(last_low + rows_k - 1, rows_k), last)
    full_last = jnp.maximum(lax.div(first_high, rows_k), full_first)
    rows = interval(
        step * rows_q + lax.broadcasted_iota(jnp.int32, (1, rows_q), 1), lengths_ref, slots
    )
    return (first, full_first, full_last, last), rows


def key_loops(spans, body, carry):
    first, full_first, full_last, last = spans
    carry = lax.fori_loop(first, full_first, functools.partial(body, True), carry)
    carry = lax.fori_loop(full_first, full_last, functools.partial(body, False), carry)
    return lax.fori_loop(full_last, last, functools.partial(body, True), carry)


def allowed_block(block, rows_k, low_row, high_row):
    places = block * rows_k + lax.broadcasted_iota(jnp.int32, (rows_k, low_row.shape[1]), 0)
    return (places >= low_row) & (places < high_row)


def project_kernel(
    heads, place_ref, scale_ref, piece_ref, weight_ref, mod_ref, bias_ref, *refs
):
    width = heads * HD
    raw_ref, query_ref, key_ref, keyt_ref, value_ref, valuet_ref, unit_ref = refs[-7:]
    piece = piece_ref[...].astype(F32)
    shift, gain = mod_ref[0:1, :], 1.0 + mod_ref[1:2, :]
    sent_normed = jnp.abs(gain) >= GAIN_LEAST
    inverse = 1.0 / jnp.where(sent_normed, gain, 1.0)
    unit_ref[...] = jnp.where(sent_normed, (piece - shift) * inverse, piece).astype(BF16)
    normed = jnp.where(sent_normed, piece, piece * gain + shift).astype(BF16)
    raw = dot(weight_ref[...], normed, 1, 1) + bias_ref[...]
    raw_ref[...] = raw
    for head in range(heads):
        part = slice(head * HD, (head + 1) * HD)
        unit, _ = unit_rows(raw[part])
        query_ref[part, :] = (unit * scale_ref[head]).astype(BF16)
    keys = [unit_rows(raw[width + head * HD : width + (head + 1) * HD])[0] for head in range(heads)]
    keys = keys[0] if heads == 1 else jnp.concatenate(keys, 0)
    values = raw[2 * width :]
    keyt_ref[...] = keys.astype(BF16)
    key_ref[...] = jnp.transpose(keys).astype(BF16)
    valuet_ref[...] = values.astype(BF16)
    value_ref[...] = jnp.transpose(values).astype(BF16)


def project(place, piece, weight, mod, bias, scales, held, heads, slots):
    width, local, depth = heads * HD, piece.shape[0], piece.shape[1]

    def fixed(shape):
        return pl.BlockSpec(shape, lambda step, *_: (0, 0))

    def columns(rows):
        return pl.BlockSpec((rows, local), lambda step, place, scales: (0, place[0]))

    def lines(cols):
        return pl.BlockSpec((local, cols), lambda step, place, scales: (place[0], 0))

    shapes = [
        jax.ShapeDtypeStruct((3 * width, slots), F32),
        jax.ShapeDtypeStruct((width, slots), BF16),
        jax.ShapeDtypeStruct((slots, width), BF16),
        jax.ShapeDtypeStruct((width, slots), BF16),
        jax.ShapeDtypeStruct((slots, width), BF16),
        jax.ShapeDtypeStruct((width, slots), BF16),
        jax.ShapeDtypeStruct((slots, depth), BF16),
    ]
    held = list(held)
    return pl.pallas_call(
        functools.partial(project_kernel, heads),
        grid_spec=pltpu.PrefetchScalarGridSpec(
            num_scalar_prefetch=2,
            grid=(1,),
            in_specs=[
                fixed((local, depth)),
                fixed((3 * width, depth)),
                fixed((2, depth)),
                fixed((3 * width, 1)),
            ]
            + [pl.BlockSpec(memory_space=pl.ANY)] * len(held),
            out_specs=[
                columns(3 * width),
                columns(width),
                lines(width),
                columns(width),
                lines(width),
                columns(width),
                lines(depth),
            ],
        ),
        out_shape=shapes,
        input_output_aliases={6 + i: i for i in range(len(held))},
        compiler_params=pltpu.CompilerParams(vmem_limit_bytes=40 * 2**20),
        cost_estimate=pl.CostEstimate(
            flops=2 * 3 * width * local * depth, bytes_accessed=8 * 2**20, transcendentals=0
        ),
        name="project",
    )(place, scales, piece, weight, mod, bias, *held)


def forward_kernel(heads, rows_k, lengths_ref, query_ref, key_ref, valuet_ref, out_ref, lse_ref):
    step = pl.program_id(0)
    slots, rows_q = key_ref.shape[0], query_ref.shape[1]
    queries = [
        head_pad(query_ref[head * HD : (head + 1) * HD, :], head, heads) for head in range(heads)
    ]
    spans, (low_row, high_row) = key_spans(step, lengths_ref, slots, rows_q, rows_k)

    def body(masked, block, carry):
        rows = pl.ds(pl.multiple_of(block * rows_k, rows_k), rows_k)
        keys = key_ref[rows, :]
        if masked:
            allowed = allowed_block(block, rows_k, low_row, high_row)
        result = []
        for head in range(heads):
            total, acc = carry[head]
            probs = jnp.exp(dot(keys, queries[head], 1, 0))
            if masked:
                probs = jnp.where(allowed, probs, 0.0)
            total = total + jnp.sum(probs.reshape(rows_k // 8, 8, rows_q), 0)
            acc = acc + dot(
                valuet_ref[head * HD : (head + 1) * HD, rows], probs.astype(BF16), 1, 0
            )
            result.append((total, acc))
        return tuple(result)

    start = tuple(
        (jnp.zeros((8, rows_q), F32), jnp.zeros((HD, rows_q), F32)) for _ in range(heads)
    )
    final = key_loops(spans, body, start)
    for head in range(heads):
        total, acc = final[head]
        denom = jnp.sum(total, 0, keepdims=True)
        out_ref[head * HD : (head + 1) * HD, :] = (acc / denom).astype(BF16)
        lse_ref[head : head + 1, :] = jnp.log(denom)


def backward_kernel(
    heads,
    rows_k,
    lengths_ref,
    scale_ref,
    raw_ref,
    query_ref,
    key_ref,
    keyt_ref,
    value_ref,
    lse_ref,
    up_ref,
    grad_ref,
    qsum_ref,
    gkey_s,
    gvalue_s,
    probs_s,
    gprobs_s,
):
    step = pl.program_id(0)
    width = heads * HD
    slots, rows_q = raw_ref.shape[1], query_ref.shape[1]

    @pl.when(step == 0)
    def _():
        gkey_s[...] = jnp.zeros_like(gkey_s)
        gvalue_s[...] = jnp.zeros_like(gvalue_s)

    queries, query_rows, ups, up_rows, lses = [], [], [], [], []
    for head in range(heads):
        part = slice(head * HD, (head + 1) * HD)
        padded = head_pad(query_ref[part, :], head, heads)
        queries.append(padded)
        query_rows.append(jnp.transpose(padded.astype(F32)).astype(BF16))
        padded = head_pad(up_ref[part, :], head, heads)
        ups.append(padded)
        up_rows.append(jnp.transpose(padded.astype(F32)).astype(BF16))
        lses.append(lse_ref[head : head + 1, :])
    spans, (low_row, high_row) = key_spans(step, lengths_ref, slots, rows_q, rows_k)

    def first(masked, block, carry):
        rows = pl.ds(pl.multiple_of(block * rows_k, rows_k), rows_k)
        keys, values = key_ref[rows, :], value_ref[rows, :]
        if masked:
            allowed = allowed_block(block, rows_k, low_row, high_row)
        result = []
        for head in range(heads):
            probs = jnp.exp(dot(keys, queries[head], 1, 0) - lses[head])
            if masked:
                probs = jnp.where(allowed, probs, 0.0)
            grad_probs = dot(values, ups[head], 1, 0)
            probs_s[head, rows, :] = probs
            gprobs_s[head, rows, :] = grad_probs
            terms = (probs * grad_probs).reshape(rows_k // 8, 8, rows_q)
            result.append(carry[head] + jnp.sum(terms, 0))
        return tuple(result)

    deltas = key_loops(spans, first, tuple(jnp.zeros((8, rows_q), F32) for _ in range(heads)))
    deltas = [jnp.sum(delta, 0, keepdims=True) for delta in deltas]

    def second(block, carry):
        rows = pl.ds(pl.multiple_of(block * rows_k, rows_k), rows_k)
        result = []
        gkey, gvalue = gkey_s[rows, :], gvalue_s[rows, :]
        for head in range(heads):
            probs = probs_s[head, rows, :]
            grad_scores = (probs * (gprobs_s[head, rows, :] - deltas[head])).astype(BF16)
            gvalue = gvalue + dot(probs.astype(BF16), up_rows[head], 1, 0)
            gkey = gkey + dot(grad_scores, query_rows[head], 1, 0)
            keyt = keyt_ref[head * HD : (head + 1) * HD, rows]
            result.append(carry[head] + dot(keyt, grad_scores, 1, 0))
        gkey_s[rows, :] = gkey
        gvalue_s[rows, :] = gvalue
        return tuple(result)

    start = tuple(jnp.zeros((HD, rows_q), F32) for _ in range(heads))
    final = lax.fori_loop(spans[0], spans[3], second, start)
    cols = pl.ds(pl.multiple_of(step * rows_q, rows_q), rows_q)
    for head in range(heads):
        part = slice(head * HD, (head + 1) * HD)
        grad = final[head]
        unit, recip = unit_rows(raw_ref[part, cols])
        qsum_ref[head : head + 1, :] = jnp.sum(grad * unit, 0, keepdims=True)
        scaled = scale_ref[head] * grad
        back = recip * (scaled - unit * jnp.sum(scaled * unit, 0, keepdims=True))
        grad_ref[part, cols] = back.astype(BF16)

    @pl.when(step == pl.num_programs(0) - 1)
    def _():
        def finish(block, carry):
            cols = pl.ds(pl.multiple_of(block * BLK, BLK), BLK)
            gkey = jnp.transpose(gkey_s[cols, :])
            for head in range(heads):
                part = slice(width + head * HD, width + (head + 1) * HD)
                unit, recip = unit_rows(raw_ref[part, cols])
                grad = gkey[head * HD : (head + 1) * HD, :]
                back = recip * (grad - unit * jnp.sum(grad * unit, 0, keepdims=True))
                grad_ref[part, cols] = back.astype(BF16)
            grad_ref[2 * width :, cols] = jnp.transpose(gvalue_s[cols, :]).astype(BF16)
            return carry

        lax.fori_loop(0, slots // BLK, finish, 0)


def whole_spec(shape):
    return pl.BlockSpec(shape, lambda step, *_: (0,) * len(shape))


def column_spec(rows, cols):
    return pl.BlockSpec((rows, cols), lambda step, *_: (0, step))


def attention_forward(query, key, valuet, lengths, heads):
    width, slots = query.shape
    rows_q, rows_k = FORWARD_BLOCK
    return pl.pallas_call(
        functools.partial(forward_kernel, heads, rows_k),
        grid_spec=pltpu.PrefetchScalarGridSpec(
            num_scalar_prefetch=1,
            grid=(slots // rows_q,),
            in_specs=[column_spec(width, rows_q), whole_spec(key.shape), whole_spec(valuet.shape)],
            out_specs=[column_spec(width, rows_q), column_spec(heads, rows_q)],
        ),
        out_shape=[
            jax.ShapeDtypeStruct((width, slots), BF16),
            jax.ShapeDtypeStruct((heads, slots), F32),
        ],
        compiler_params=pltpu.CompilerParams(
            dimension_semantics=("arbitrary",), vmem_limit_bytes=32 * 2**20
        ),
        cost_estimate=pl.CostEstimate(
            flops=heads * slots * slots * 1000, bytes_accessed=4 * 2**20, transcendentals=0
        ),
        name="attend",
    )(lengths, query, key, valuet)


def attention_backward(raw, query, key, keyt, value, lse, up, lengths, scales, heads):
    width, slots = query.shape
    rows_q, rows_k = BACKWARD_BLOCK
    return pl.pallas_call(
        functools.partial(backward_kernel, heads, rows_k),
        grid_spec=pltpu.PrefetchScalarGridSpec(
            num_scalar_prefetch=2,
            grid=(slots // rows_q,),
            in_specs=[
                whole_spec(raw.shape),
                column_spec(width, rows_q),
                whole_spec(key.shape),
                whole_spec(keyt.shape),
                whole_spec(value.shape),
                column_spec(heads, rows_q),
                column_spec(width, rows_q),
            ],
            out_specs=[whole_spec(raw.shape), column_spec(heads, rows_q)],
            scratch_shapes=[
                pltpu.VMEM((slots, width), F32),
                pltpu.VMEM((slots, width), F32),
                pltpu.VMEM((heads, slots, rows_q), F32),
                pltpu.VMEM((heads, slots, rows_q), F32),
            ],
        ),
        out_shape=[
            jax.ShapeDtypeStruct(raw.shape, BF16),
            jax.ShapeDtypeStruct((heads, slots), F32),
        ],
        compiler_params=pltpu.CompilerParams(
            dimension_semantics=("arbitrary",), vmem_limit_bytes=56 * 2**20
        ),
        cost_estimate=pl.CostEstimate(
            flops=heads * slots * slots * 2000, bytes_accessed=14 * 2**20, transcendentals=0
        ),
        name="attend_back",
    )(lengths, scales, raw, query, key, keyt, value, lse, up)


def mlp_kernel(
    rows,
    part_ref,
    normed_ref,
    up_ref,
    first_ref,
    second_ref,
    bias_ref,
    sent_one_ref,
    kept_one_ref,
    sent_two_ref,
    kept_two_ref,
    bias_grad_ref,
    branch_ref,
    grad_ref,
):
    part, step = pl.program_id(0), pl.program_id(1)
    start = (part == 0) & (step == 0)
    group = first_ref.shape[0]
    normed, up = normed_ref[...], up_ref[...]
    first = first_ref[:, :rows, :].reshape(group * rows, first_ref.shape[2])
    second = second_ref[...]
    pre = dot(normed, first, 1, 1) + bias_ref[...]
    grad_hidden = dot(up, second, 1, 1)
    square = pre * pre
    angle = jnp.tanh(GELU_ROOT * pre * (1.0 + GELU_CUBE * square))
    half = 0.5 * (1.0 + angle)
    slope = half + 0.5 * pre * (1.0 - angle * angle) * GELU_ROOT * (1.0 + 3.0 * GELU_CUBE * square)
    hidden = (pre * half).astype(BF16)
    grad_pre = (slope * grad_hidden).astype(BF16)
    bias_grad_ref[...] = jnp.sum(grad_pre.astype(F32), 0, keepdims=True)
    branch = dot(hidden, second, 1, 0)
    grad = dot(grad_pre, first, 1, 0)

    @pl.when(start)
    def _():
        branch_ref[...] = branch
        grad_ref[...] = grad

    @pl.when(jnp.logical_not(start))
    def _():
        branch_ref[...] += branch
        grad_ref[...] += grad

    one = dot(grad_pre, normed, 0, 0).astype(BF16).reshape(kept_one_ref.shape)
    two = dot(hidden, up, 0, 0).astype(BF16).reshape(kept_two_ref.shape)
    sending = part < pl.num_programs(0) // 2

    @pl.when(sending)
    def _():
        sent_one_ref[...] = one
        sent_two_ref[...] = two

    @pl.when(jnp.logical_not(sending))
    def _():
        kept_one_ref[...] = one
        kept_two_ref[...] = two


def mlp(parts, normed, up, first, second, bias, heads_all, rows):
    local, width = normed.shape
    total = parts.shape[0]
    group = max(8, 128 // rows)
    steps = heads_all // group
    cols = group * rows
    full_rows = first.shape[1]
    half = total // 2

    def fixed(p, j, part):
        return (0, 0)

    def sent(p, j, part):
        flat = jnp.minimum(p * steps + j, half * steps - 1)
        return (flat // steps, flat % steps, 0, 0)

    def kept(p, j, part):
        flat = jnp.maximum(p * steps + j - half * steps, 0)
        return (flat // steps, flat % steps, 0, 0)

    grads = jax.ShapeDtypeStruct((half, heads_all, rows, width), BF16)
    return pl.pallas_call(
        functools.partial(mlp_kernel, rows),
        grid_spec=pltpu.PrefetchScalarGridSpec(
            num_scalar_prefetch=1,
            grid=(total, steps),
            in_specs=[
                pl.BlockSpec((local, width), fixed),
                pl.BlockSpec((local, width), fixed),
                pl.BlockSpec((group, full_rows, width), lambda p, j, part: (part[p] * steps + j, 0, 0)),
                pl.BlockSpec((cols, width), lambda p, j, part: (part[p] * steps + j, 0)),
                pl.BlockSpec((1, cols), lambda p, j, part: (0, part[p] * steps + j)),
            ],
            out_specs=[
                pl.BlockSpec((1, group, rows, width), sent),
                pl.BlockSpec((1, group, rows, width), kept),
                pl.BlockSpec((1, group, rows, width), sent),
                pl.BlockSpec((1, group, rows, width), kept),
                pl.BlockSpec((1, cols), lambda p, j, part: (0, part[p] * steps + j)),
                pl.BlockSpec((local, width), fixed),
                pl.BlockSpec((local, width), fixed),
            ],
        ),
        out_shape=[
            grads,
            grads,
            grads,
            grads,
            jax.ShapeDtypeStruct((1, total * heads_all * rows), F32),
            jax.ShapeDtypeStruct((local, width), F32),
            jax.ShapeDtypeStruct((local, width), F32),
        ],
        compiler_params=pltpu.CompilerParams(
            dimension_semantics=("arbitrary", "arbitrary"), vmem_limit_bytes=52 * 2**20
        ),
        cost_estimate=pl.CostEstimate(
            flops=12 * local * width * total * heads_all * rows,
            bytes_accessed=40 * 2**20,
            transcendentals=0,
        ),
        name="mlp",
    )(parts, normed, up, first, second, bias)


def ring_blocks_kernel(
    halves, place_ref, grad_ref, weight_ref, one_ref, two_ref, three_ref, four_ref, *out_refs
):
    terms = dot(grad_ref[...], weight_ref[...], 0, 0).astype(BF16)
    rest = (one_ref[0].astype(F32) + two_ref[0].astype(F32)).astype(BF16)
    last = (three_ref[0].astype(F32) + four_ref[0].astype(F32)).astype(BF16)
    rest = jnp.concatenate([rest, last], 0)
    local = terms.shape[0]
    if halves:
        half = out_refs[0].shape[0]
        out_refs[0][...] = terms[:half]
        out_refs[1][: local - half, :] = terms[half:]
        out_refs[1][local - half :, :] = rest
    else:
        out_refs[0][0, :local, :] = terms
        out_refs[0][0, local:, :] = rest


def ring_blocks(places, grad, weight, pairs, local, halves):
    depth, width = weight.shape
    total = local + pairs[0].shape[1] + pairs[2].shape[1]
    if halves:
        sizes = [total // 2, total - total // 2]
        out_specs = [pl.BlockSpec((size, width), lambda step, place: (0, 0)) for size in sizes]
        out_shape = [jax.ShapeDtypeStruct((size, width), BF16) for size in sizes]
    else:
        out_specs = pl.BlockSpec((1, total, width), lambda step, place: (step, 0, 0))
        out_shape = jax.ShapeDtypeStruct((places.shape[0], total, width), BF16)
    return pl.pallas_call(
        functools.partial(ring_blocks_kernel, halves),
        grid_spec=pltpu.PrefetchScalarGridSpec(
            num_scalar_prefetch=1,
            grid=(places.shape[0],),
            in_specs=[
                pl.BlockSpec((depth, local), lambda step, place: (0, place[step])),
                pl.BlockSpec((depth, width), lambda step, place: (0, 0)),
            ]
            + [
                pl.BlockSpec((1, pair.shape[1], width), lambda step, place: (place[step], 0, 0))
                for pair in pairs
            ],
            out_specs=out_specs,
        ),
        out_shape=out_shape,
        compiler_params=pltpu.CompilerParams(vmem_limit_bytes=60 * 2**20),
        cost_estimate=pl.CostEstimate(flops=1, bytes_accessed=1, transcendentals=0),
        name="ring_blocks",
    )(places, grad, weight, *pairs)


def add_half_kernel(index, lower, blocks_ref, got_ref, out_ref):
    half = got_ref.shape[0]
    block = blocks_ref[0]
    part = slice(0, half) if lower else slice(block.shape[0] - half, block.shape[0])
    rest = slice(half, block.shape[0]) if lower else slice(0, block.shape[0] - half)
    out_ref[rest, :] = block[rest]
    out_ref[part, :] = (block[part].astype(F32) + got_ref[...].astype(F32)).astype(BF16)


def add_half(blocks, index, got, lower):
    _, rows, width = blocks.shape
    return pl.pallas_call(
        functools.partial(add_half_kernel, index, lower),
        grid=(1,),
        in_specs=[
            pl.BlockSpec((1, rows, width), lambda step: (index, 0, 0)),
            pl.BlockSpec(got.shape, lambda step: (0, 0)),
        ],
        out_specs=pl.BlockSpec((rows, width), lambda step: (0, 0)),
        out_shape=jax.ShapeDtypeStruct((rows, width), BF16),
        compiler_params=pltpu.CompilerParams(vmem_limit_bytes=60 * 2**20),
        cost_estimate=pl.CostEstimate(flops=1, bytes_accessed=1, transcendentals=0),
        name="add_half",
    )(blocks, got)


def finish_kernel(rows, order_ref, value_ref, first_ref, second_ref):
    value = value_ref[0].astype(F32)
    first_ref[...] = jnp.transpose(value[:rows])
    second_ref[...] = value[rows:]


def finish_weights(order, value, rows):
    total, full_rows, width = value.shape
    return pl.pallas_call(
        functools.partial(finish_kernel, rows),
        grid_spec=pltpu.PrefetchScalarGridSpec(
            num_scalar_prefetch=1,
            grid=(total,),
            in_specs=[pl.BlockSpec((1, full_rows, width), lambda step, order: (order[step], 0, 0))],
            out_specs=[
                pl.BlockSpec((width, rows), lambda step, order: (0, step)),
                pl.BlockSpec((full_rows - rows, width), lambda step, order: (step, 0)),
            ],
        ),
        out_shape=[
            jax.ShapeDtypeStruct((width, total * rows), F32),
            jax.ShapeDtypeStruct((total * (full_rows - rows), width), F32),
        ],
        name="finish_weights",
    )(order, value)


def after(value, *others):
    return lax.optimization_barrier((value, *others))[0]


def shards(
    block_input,
    lengths,
    scale_ids,
    class_ids,
    code_ids,
    cotangent,
    class_table,
    ada_weight,
    ada_bias,
    qkv_weight,
    qv_bias,
    qk_scale,
    proj_weight,
    proj_bias,
    fc1_weight,
    fc1_bias,
    fc2_weight,
    fc2_bias,
):
    count, data_count = lax.axis_size("head"), lax.axis_size("dp")
    me, data_me = lax.axis_index("head"), lax.axis_index("dp")
    _, local, width = block_input.shape
    slots = local * count
    heads = qk_scale.shape[0]
    feats = heads * HD
    hidden_here = fc1_weight.shape[1]
    data_masks = [1 << bit for bit in range(data_count.bit_length() - 1)]
    both_axes = ("dp", "head")

    ring = list(range(0, count, 2)) + list(range(count - 1, 0, -2))
    half_count = count // 2
    offsets = [0]
    for away in range(1, half_count):
        offsets += [away, -away]
    offsets.append(half_count)
    my_pos = jnp.where(me % 2 == 0, me // 2, count - 1 - me // 2)

    def at(away):
        pos = (my_pos + away + count) % count
        return jnp.where(pos < half_count, 2 * pos, 2 * (count - 1 - pos) + 1)

    def rot(value, away):
        pairs = [(ring[(i + away) % count], ring[i]) for i in range(count)]
        return lax.ppermute(value, "head", pairs)

    def swap(value, mask):
        return lax.ppermute(value, "dp", [(i, i ^ mask) for i in range(data_count)])

    def xor_head(value, mask):
        return lax.ppermute(value, "head", [(i, i ^ mask) for i in range(count)])

    def head_sum_far(value):
        total = value
        for mask in range(2, count, 2):
            total = total + xor_head(value, mask)
        return total

    def head_sum_near(value):
        return value + xor_head(value, 1)

    inputs_full = block_input[0].astype(F32)
    unit_one, recip_one = normalize(inputs_full)

    hidden_part, feat_part = hidden_here // data_count, feats // data_count
    fc1_part = lax.dynamic_slice(fc1_weight, (0, data_me * hidden_part), (width, hidden_part)).T
    proj_part = lax.dynamic_slice(proj_weight, (data_me * feat_part, 0), (feat_part, width))
    fc2_part = lax.dynamic_slice(fc2_weight, (data_me * hidden_part, 0), (hidden_part, width))
    first_full = lax.all_gather(
        jnp.concatenate([fc1_part, proj_part], 0), both_axes, axis=0, tiled=False
    )
    fc2_full = lax.all_gather(fc2_part, both_axes, axis=0, tiled=True)
    proj_full = first_full[:, hidden_part:].reshape(data_count, count, feat_part, width)
    proj_full = jnp.transpose(proj_full, (1, 0, 2, 3)).reshape(-1, width)

    cond = jnp.take(class_table, class_ids, axis=0).astype(F32)
    act = jax.nn.silu(cond).astype(BF16)
    mod_local = jnp.dot(act, ada_weight, preferred_element_type=F32)[0] + ada_bias.astype(F32)
    small = jnp.concatenate([mod_local, fc1_bias.astype(F32)])[None, :]
    pieces = [small] + [xor_head(small, mask) for mask in range(2, count, 2)]
    pieces = jnp.concatenate(pieces, 0)
    small_all = jnp.stack([pieces, xor_head(pieces, 1)], 1).reshape(count, -1)
    small_all = jnp.take(
        small_all, jnp.bitwise_xor(me, jnp.arange(count, dtype=jnp.int32)), axis=0
    )
    mod_here = mod_local.shape[0]
    modulation = small_all[:, :mod_here].reshape(6, width)
    shift_one, scale_one, gate_one, shift_two, scale_two, gate_two = [
        modulation[i : i + 1] for i in range(6)
    ]
    gain_one = 1.0 + scale_one
    ring_low = jnp.where(
        jnp.abs(gain_one) >= GAIN_LEAST, unit_one * gain_one + shift_one, unit_one
    ).astype(BF16)
    units = {0: ring_low, 1: rot(ring_low, 1), -1: rot(ring_low, -1)}
    bias_full = small_all[:, mod_here:].reshape(count, data_count, hidden_part)
    bias_full = jnp.transpose(bias_full, (1, 0, 2)).reshape(1, -1)

    qkv_rows = jnp.transpose(
        after(qkv_weight, small_all).T.reshape(heads, 3, HD, width), (1, 0, 2, 3)
    ).reshape(3 * feats, width)
    bias_pair = qv_bias.astype(F32).reshape(heads, 2, HD)
    qkv_bias = jnp.stack([bias_pair[:, 0], jnp.zeros_like(bias_pair[:, 0]), bias_pair[:, 1]], 0)
    qkv_bias = qkv_bias.reshape(3 * feats, 1)
    scale_exp = jnp.exp(qk_scale)

    def put(held, away):
        place = at(away).astype(jnp.int32)[None]
        return project(
            place, units[away], qkv_rows, modulation[:2], qkv_bias, scale_exp, held, heads, slots
        )

    for away in range(2, half_count):
        units[away], units[-away] = rot(units[away - 1], 1), rot(units[1 - away], -1)
    held = put([], 0)
    for away in range(1, half_count - 1):
        held = put(put(held, away), -away)
        if away == 1:
            last, units[half_count - 1], units[1 - half_count] = lax.optimization_barrier(
                (held[1], units[half_count - 1], units[1 - half_count])
            )
            held = [held[0], last] + list(held[2:])
            proj_full, units[half_count - 1] = lax.optimization_barrier(
                (proj_full, units[half_count - 1])
            )
    half = local // 2
    ends = [
        rot(units[half_count - 1][:half], 1),
        rot(units[1 - half_count][half:], -1),
    ]
    held = put(put(held, half_count - 1), 1 - half_count)
    units[half_count] = jnp.concatenate(ends, 0)
    held = put(held, half_count)
    raw, query, key, keyt, value, valuet, unit_all = held
    out_low, lse = attention_forward(query, key, valuet, lengths[0], heads)

    valid = me * local + jnp.arange(local, dtype=jnp.int32) < jnp.sum(lengths[0])
    code_range = jnp.arange(CODES, dtype=jnp.int32)
    code_hits = (after(code_ids, out_low)[0][:, None] == code_range[None, :]) & valid[:, None]
    local_counts = jnp.sum(code_hits.astype(F32), 0)
    attended = jnp.zeros((feats * count, local), BF16)
    for away in offsets:
        piece = lax.dynamic_slice(out_low, (0, at(-away) * local), (feats, local))
        piece = piece if away == 0 else rot(piece, away)
        attended = lax.dynamic_update_slice(attended, piece, (at(away) * feats, 0))
    cot_full = cotangent[0].astype(F32)
    grad_mlp = (cot_full * gate_two).astype(BF16)
    attended, local_counts = lax.optimization_barrier((attended, local_counts))
    attn_branch = dot(attended, proj_full, 0, 0) + proj_bias.astype(F32)
    resid = inputs_full + gate_one * attn_branch
    unit_two, recip_two = normalize(resid)
    normed_two = (unit_two * (1.0 + scale_two) + shift_two).astype(BF16)

    kept_t = list(range(0, data_count, 2))
    all_t = [t + 1 for t in kept_t] + kept_t
    parts = jnp.bitwise_xor(data_me, jnp.array(all_t, jnp.int32))
    sent_one, kept_one, sent_two, kept_two, fc1_bias_sum, mlp_branch, grad_normed_two = mlp(
        parts, normed_two, grad_mlp, first_full, fc2_full, bias_full, count, hidden_part
    )
    grad_shift_two = jnp.sum(grad_normed_two, 0)
    grad_scale_two = jnp.sum(grad_normed_two * unit_two, 0)
    grad_resid = cot_full + norm_back(unit_two, recip_two, grad_normed_two * (1.0 + scale_two))
    grad_attn = (grad_resid * gate_one).astype(BF16)
    grad_gate_one = jnp.sum(grad_resid * attn_branch, 0)
    grad_attended = dot(proj_full, grad_attn, 1, 1).astype(BF16)
    up_pieces = {}
    for away in offsets:
        piece = lax.dynamic_slice(grad_attended, (at(away) * feats, 0), (feats, local))
        up_pieces[away] = piece if away == 0 else rot(piece, -away)

    sent_one, sent_two = lax.optimization_barrier((sent_one, sent_two))
    got_one, got_two = swap(sent_one, 1), swap(sent_two, 1)

    def add(left, right):
        return (left.astype(F32) + right.astype(F32)).astype(BF16)

    def split_pair(kept):
        kept = {t: kept[i] for i, t in enumerate(kept_t)}
        for mask in data_masks[1:-1]:
            kept = {
                t: add(kept[t], swap(kept[t ^ mask], mask)) for t in kept if not t & mask
            }
        return kept[0], swap(kept[data_masks[-1]], data_masks[-1])

    kept_one = [add(kept_one[i], got_one[i]) for i in range(len(kept_t))]
    fc2_stack = jnp.stack([add(kept_two[i], got_two[i]) for i in range(len(kept_t))], 1)
    fc2_stack = fc2_stack.reshape(count, len(kept_t) * hidden_part, width)
    proj_grad = dot(attended, grad_attn, 1, 0).astype(BF16)
    proj_grad = proj_grad.reshape(count, data_count, feat_part, width)
    proj_parts = [
        lax.dynamic_index_in_dim(
            proj_grad, jnp.bitwise_xor(data_me, t).astype(jnp.uint32), 1, keepdims=False
        )
        for t in all_t
    ]
    got_three = swap(jnp.stack(proj_parts[: len(kept_t)], 0), 1)
    kept_three = [add(proj_parts[len(kept_t) + i], got_three[i]) for i in range(len(kept_t))]
    mlp_branch = mlp_branch + fc2_bias.astype(F32)
    block_output = (resid + gate_two * mlp_branch).astype(BF16)
    grad_gate_two = jnp.sum(cot_full * mlp_branch, 0)

    up = jnp.zeros((feats, slots), BF16)
    for away in offsets[:5]:
        up = lax.dynamic_update_slice(up, up_pieces[away], (0, at(-away) * local))
    up, kept_one, kept_three, fc2_stack = lax.optimization_barrier(
        (up, kept_one, kept_three, fc2_stack)
    )
    for away in offsets[5:]:
        up = lax.dynamic_update_slice(up, up_pieces[away], (0, at(-away) * local))
    fc2_mine = lax.psum_scatter(fc2_stack, "head", scatter_dimension=0, tiled=True)
    fc2_mine = fc2_mine.reshape(len(kept_t), hidden_part, width)

    one_here, one_got = split_pair(kept_one)
    three_here, three_got = split_pair(kept_three)

    def share(value, hop):
        value = jnp.stack([value, hop], 0)
        for mask in reversed(data_masks[:-1]):
            value = jnp.stack([value, swap(value, mask)], 0)
        bits = len(data_masks)
        value = value.reshape((data_count,) + value.shape[bits:])
        table = [int(format(t, "b").zfill(bits)[::-1], 2) for t in range(data_count)]
        places = jnp.take(
            jnp.array(table, jnp.int32),
            jnp.bitwise_xor(data_me, jnp.arange(data_count, dtype=jnp.int32)),
        )
        return value, places

    fc2_bias_sum = jnp.sum(grad_mlp.astype(F32), 0)
    proj_bias_sum = jnp.sum(grad_attn.astype(F32), 0)
    fc1_bias_sum = fc1_bias_sum.reshape(data_count, count, hidden_part)
    fc1_bias_sum = jnp.transpose(fc1_bias_sum, (1, 0, 2)).reshape(-1)
    early = jnp.concatenate(
        [
            local_counts,
            fc2_bias_sum,
            proj_bias_sum,
            fc1_bias_sum,
            grad_gate_one,
            grad_shift_two,
            grad_scale_two,
            grad_gate_two,
        ]
    )
    early, up = lax.optimization_barrier((early, up))
    early = head_sum_far(early[None, :])

    grad_raw, query_sums = attention_backward(
        raw, query, key, keyt, value, lse, up, lengths[0], scale_exp, heads
    )
    grad_raw, query_sums, one_got, three_got, early = lax.optimization_barrier(
        (grad_raw, query_sums, one_got, three_got, early)
    )
    pairs = [one_here, one_got, three_here, three_got]

    def send(ups, downs):
        return rot(ups, -1), rot(downs, 1)

    places = jnp.stack([at(away) for away in offsets]).astype(jnp.int32)
    far_up, far_down = ring_blocks(places[-1:], grad_raw, qkv_rows, pairs, local, True)
    got_up, got_down = send(far_up, far_down)
    half = far_up.shape[0]

    source, _ = lax.optimization_barrier((grad_raw, far_up))
    blocks = ring_blocks(places[:-1], source, qkv_rows, pairs, local, False)

    got_up, got_down, blocks, source = lax.optimization_barrier(
        (got_up, got_down, blocks, source)
    )
    ups = add_half(blocks, offsets.index(half_count - 1), got_up, True)
    downs = add_half(blocks, offsets.index(1 - half_count), got_down, False)
    blocks = {away: blocks[i] for i, away in enumerate(offsets[:-1])}
    ups, downs, source = lax.optimization_barrier((ups, downs, source))
    got_up, got_down = send(ups, downs)
    unit_grad = dot(source, unit_all, 1, 0)
    bias_sums = jnp.sum(after(source, unit_grad).astype(F32), 1)
    qkv_grad = unit_grad * (1.0 + scale_one) + bias_sums[:, None] * shift_one
    qkv_grad = qkv_grad.astype(BF16)
    scale_sums = scale_exp * jnp.sum(query_sums, 1)
    rows_float = qkv_rows.astype(F32)
    grad_shift_one = jnp.sum(rows_float * bias_sums[:, None], 0)
    grad_scale_one = jnp.sum(rows_float * unit_grad, 0)
    late = head_sum_far(jnp.concatenate([grad_shift_one, grad_scale_one])[None, :])
    over_rows = CODES + 2 * width + count * hidden_here

    for away in range(half_count - 2, 0, -1):
        got_up, got_down, late, qkv_grad = lax.optimization_barrier(
            (got_up, got_down, late, qkv_grad)
        )
        ups, downs = add(blocks[away], got_up), add(blocks[-away], got_down)
        ups, downs, late, early, qkv_grad, fc2_mine = lax.optimization_barrier(
            (ups, downs, late, early, qkv_grad, fc2_mine)
        )
        got_up, got_down = send(ups, downs)
        if away == half_count - 2:
            late = head_sum_near(jnp.concatenate([late, early], 1))
            for mask in data_masks:
                qkv_grad = add(qkv_grad, swap(qkv_grad, mask))
            for mask in data_masks[1:]:
                got = swap(fc2_mine, mask)
                fc2_mine = jnp.stack(
                    [add(fc2_mine[i], got[kept_t.index(t ^ mask)]) for i, t in enumerate(kept_t)], 0
                )
            fc2_all = jnp.concatenate([fc2_mine, swap(fc2_mine, 1)], 0)
            fc2_order = jnp.bitwise_xor(data_me, jnp.arange(data_count, dtype=jnp.int32))
            fc2_order = fc2_order // 2 + (fc2_order % 2) * len(kept_t)
            fc2_mine = jnp.take(fc2_all, fc2_order, axis=0).astype(F32).reshape(-1, width)
        if away == 1:
            sums = late[0]
            mod_all = jnp.concatenate([sums[: 2 * width], sums[2 * width + over_rows :]])
            rows = jnp.concatenate(
                [
                    lax.dynamic_slice_in_dim(mod_all, me * mod_here, mod_here, 0),
                    class_ids.astype(F32),
                    bias_sums,
                    scale_sums,
                    sums[2 * width : 2 * width + over_rows],
                ]
            )[None, :]
            rows = jnp.concatenate(
                [rows] + [swap(rows, mask) for mask in range(1, data_count)], 0
            )
            rows = jnp.take(
                rows, jnp.bitwise_xor(data_me, jnp.arange(data_count, dtype=jnp.int32)), axis=0
            )
            class_rows = rows[:, mod_here].astype(jnp.int32)
            mod_rows = rows[:, :mod_here]
            tail = jnp.sum(rows[:, mod_here + 1 :], 0)
            cond_terms = lax.dot_general(
                mod_rows, ada_weight.astype(F32), (((1,), (1,)), ((), ())), precision=HIGH
            )
            cond_sums = head_sum_far(cond_terms)

    qkv_weight_grad = (
        jnp.transpose(qkv_grad.reshape(3, heads, HD, width), (1, 0, 2, 3))
        .reshape(3 * feats, width)
        .astype(F32)
        .T
    )
    cond_rows = jnp.take(class_table, class_rows, axis=0).astype(F32)
    act_rows = jax.nn.silu(cond_rows).astype(BF16).astype(F32)
    ada_weight_grad = lax.dot_general(
        act_rows, mod_rows, (((0,), (0,)), ((), ())), precision=HIGH
    )
    ada_bias_grad = jnp.sum(mod_rows, 0)
    got_up, got_down, tail, cond_sums, qkv_weight_grad, ada_weight_grad, fc2_weight_grad = (
        lax.optimization_barrier(
            (got_up, got_down, tail, cond_sums, qkv_weight_grad, ada_weight_grad, fc2_mine)
        )
    )
    ring_total = blocks[0].astype(F32) + got_up.astype(F32) + got_down.astype(F32)
    grad_normed_one = ring_total[:local]
    first_mine = [value[local:].astype(F32) for value in (blocks[0], got_up, got_down)]
    first_mine = (first_mine[0] + first_mine[1] + first_mine[2]).astype(BF16)
    bias_sums = tail[: 3 * feats].reshape(3, heads, HD)
    qv_bias_grad = jnp.stack([bias_sums[0], bias_sums[2]], 1).reshape(-1)
    qk_scale_grad = tail[3 * feats : 3 * feats + heads]
    tail = tail[3 * feats + heads :]
    code_hist = tail[:CODES].astype(jnp.int32)
    fc2_bias_grad = tail[CODES : CODES + width]
    proj_bias_grad = tail[CODES + width : CODES + 2 * width]
    fc1_bias_grad = lax.dynamic_slice_in_dim(
        tail[CODES + 2 * width :], me * hidden_here, hidden_here, 0
    )

    input_grad = (
        grad_resid + norm_back(unit_one, recip_one, grad_normed_one * (1.0 + scale_one))
    ).astype(BF16)
    first_hop = swap(first_mine, data_masks[-1])
    cond_sums, first_hop = lax.optimization_barrier((cond_sums, first_hop))
    first_grad, order = share(first_mine, first_hop)
    cond_sums = head_sum_near(cond_sums)
    _, silu_pull = jax.vjp(jax.nn.silu, cond_rows)
    grad_rows = silu_pull(cond_sums)[0]
    class_range = jnp.arange(class_table.shape[0], dtype=jnp.int32)
    class_table_grad = jnp.zeros(class_table.shape, F32)
    for row in range(data_count):
        hit = class_range[:, None] == class_rows[row]
        class_table_grad = class_table_grad + jnp.where(hit, grad_rows[row][None, :], 0.0)
    if hidden_part % 128 == 0:
        fc1_weight_grad, proj_weight_grad = finish_weights(order, first_grad, hidden_part)
    else:
        first_grad = jnp.take(first_grad, order, axis=0).astype(F32)
        fc1_weight_grad = first_grad[:, :hidden_part].reshape(-1, width).T
        proj_weight_grad = first_grad[:, hidden_part:].reshape(-1, width)

    return (
        block_output[None],
        input_grad[None],
        class_table_grad,
        ada_weight_grad,
        ada_bias_grad,
        qkv_weight_grad,
        qv_bias_grad,
        qk_scale_grad,
        proj_weight_grad,
        proj_bias_grad,
        fc1_weight_grad,
        fc1_bias_grad,
        fc2_weight_grad,
        fc2_bias_grad,
        code_hist,
    )


def solution(mesh):
    placed = (
        P("dp", "head", None),
        P("dp", None),
        P("dp", None),
        P("dp"),
        P("dp", "head"),
        P("dp", "head", None),
        P(),
        P(None, "head"),
        P("head"),
        P(None, "head"),
        P("head"),
        P("head"),
        P("head", None),
        P(),
        P(None, "head"),
        P("head"),
        P("head", None),
        P(),
    )
    return jax.shard_map(
        shards,
        mesh=mesh,
        in_specs=placed,
        out_specs=(
            P("dp", "head", None),
            P("dp", "head", None),
            P(),
            P(None, "head"),
            P("head"),
            P(None, "head"),
            P("head"),
            P("head"),
            P("head", None),
            P(),
            P(None, "head"),
            P("head"),
            P("head", None),
            P(),
            P(),
        ),
        check_vma=False,
    )
```
